32 devices in a mesh: dp: 8 (over y, x, core), tensor: 4 (over z).
Axes of the slice: x: 2, y: 2, z: 4, core: 2. Of those that a mesh axis runs over, the one named last changes fastest.
Arguments:
- layer_input: bfloat16 [2, 8, 1024, 1024], P(None, 'dp', 'tensor'), may hold values from -6 to 6
- segment: int32 [2, 8, 1024], P(None, 'dp'), may hold values from 0 to 3, never falling along the last dimension, each value on 1 to 800 neighbouring positions
- d_out: bfloat16 [2, 8, 1024, 1024], P(None, 'dp', 'tensor'), may hold values from -6 to 6
- norm1_gain: bfloat16 [1024], replicated, may hold values from 0.099609375 to 1.8984375
- w_query: bfloat16 [1024, 1024], P(None, 'tensor'), may hold values from -0.1875 to 0.1875
- w_key: bfloat16 [1024, 1024], P(None, 'tensor'), may hold values from -0.1875 to 0.1875
- w_value: bfloat16 [1024, 1024], P(None, 'tensor'), may hold values from -0.1875 to 0.1875
- w_beta: bfloat16 [1024, 8], P(None, 'tensor'), may hold values from -0.1875 to 0.1875
- conv_weight: bfloat16 [3, 4, 1024], P(None, None, 'tensor'), may hold values from -2 to 2
- w_out: bfloat16 [1024, 1024], P('tensor'), may hold values from -0.25 to 0.25
- norm2_gain: bfloat16 [1024], replicated, may hold values from 0.099609375 to 1.8984375
- w_gate: bfloat16 [1024, 2816], P(None, 'tensor'), may hold values from -0.1875 to 0.1875
- w_up: bfloat16 [1024, 2816], P(None, 'tensor'), may hold values from -0.1875 to 0.1875
- w_down: bfloat16 [2816, 1024], P('tensor'), may hold values from -0.109375 to 0.109375
Outputs:
- output: bfloat16 [2, 8, 1024, 1024], P(None, 'dp', 'tensor')
- input_grad: bfloat16 [2, 8, 1024, 1024], P(None, 'dp', 'tensor')
- grad_norm1_gain: float32 [1024], P('tensor')
- grad_w_query: float32 [1024, 1024], P(None, 'tensor')
- grad_w_key: float32 [1024, 1024], P(None, 'tensor')
- grad_w_value: float32 [1024, 1024], P(None, 'tensor')
- grad_w_beta: float32 [1024, 8], P(None, 'tensor')
- grad_conv_weight: float32 [3, 4, 1024], P(None, None, 'tensor')
- grad_w_out: float32 [1024, 1024], P('tensor')
- grad_norm2_gain: float32 [1024], P('tensor')
- grad_w_gate: float32 [1024, 2816], P(None, 'tensor')
- grad_w_up: float32 [1024, 2816], P(None, 'tensor')
- grad_w_down: float32 [2816, 1024], P('tensor')
The draws below stay inside these ranges and needn't reach their ends.
Inputs may be any that keep to these rules, and one draw needn't show every extreme that they name: `segment`: segment numbers never fall along a sequence; a document holds at most 800 tokens, and some document of each sequence holds exactly that many.
All inputs are finite; a program needn't handle non-finite values.
Results may differ from the reference program's by a relative error of at most 0.02.
Values may be sent and summed in bfloat16 or wider, within the bound.
No kernel may reach another device: no remote copies, remote signals or barrier semaphores. Data moves between devices by JAX's collectives and lax.ppermute only.
A program may use at most 256 MiB of HBM per device.

```python
import math
import jax
import jax.numpy as jnp
import numpy as np
from jax import lax

D = 1024
HEADS = 8
HD = 128
FF = 2816
CONV = 4
SPAN = 64
L = 1024
MB = 2
SEQS = 8


def block_scale(stream_key, dims, cuts, least, high):
    factor_of, own = 1.0, jax.random.fold_in(stream_key, 6)
    for axis_at, shards_of in cuts:
        draws = jnp.exp(jax.random.uniform(jax.random.fold_in(own, axis_at), (shards_of,), jnp.float32, least / len(cuts), high / len(cuts)))
        factor_of = factor_of * jnp.repeat(draws, dims[axis_at] // shards_of).reshape([-1 if axis == axis_at else 1 for axis in range(len(dims))])
    return factor_of


def length_profile(amount, total, reach, lean):
    portions = [(1 << 20) // math.isqrt(standing ** lean) + 1 for standing in range(2, amount + 1)]
    rest, counts = total - reach - (amount - 1), [1] * (amount - 1)
    while rest > 0:
        movable = [i for i in range(amount - 1) if counts[i] < reach]
        mass, budget = sum([portions[i] for i in movable]), rest
        for i in movable:
            addition = min(reach - counts[i], max(1, budget * portions[i] // mass), rest)
            counts[i] = counts[i] + addition
            rest = rest - addition
    return np.array([reach] + counts)


def uneven_parts(rng, amount, total, most, lean):
    if amount == 2:
        one = jax.random.randint(rng, (), max(1, total - most), min(most, total - 1) + 1)
        return jnp.stack([one, total - one])
    sizes = jnp.asarray(length_profile(amount, total, most, lean), jnp.int32)
    couples = (amount - 1) // 2
    source_of, sink = sizes[1:1 + 2 * couples:2], sizes[2:2 + 2 * couples:2]
    slack = jnp.minimum(source_of - 1, most - sink)
    moved = jax.random.randint(jax.random.fold_in(rng, 1), (couples,), 0, 1 << 20) % (slack + 1)
    sizes = sizes.at[1:1 + 2 * couples:2].set(source_of - moved).at[2:2 + 2 * couples:2].set(sink + moved)
    return sizes[jax.random.permutation(jax.random.fold_in(rng, 2), amount)]


def normal_values(rng, extent, scale, reach, cuts=(), held_as=jnp.bfloat16):
    drawn = scale * jax.random.normal(rng, extent, jnp.float32)
    if cuts:
        drawn = drawn * block_scale(rng, extent, cuts, -0.22, 0.18)
    return jnp.clip(drawn, -reach, reach).astype(held_as)


def setup_inputs(seed: int = 0) -> dict:
    seeds = jax.random.split(jax.random.key(seed), 15)
    return {
        "layer_input": normal_values(seeds[0], (MB, SEQS, L, D), 1.0, 6.0, ((1, 8), (2, 4))),
        "segment": jax.vmap(lambda own: jnp.searchsorted(jnp.cumsum(uneven_parts(own, max(2, L // 256), L, L * 25 // 32, 2)), jnp.arange(L), side="right"))(jax.random.split(seeds[1], MB * SEQS)).reshape((MB, SEQS, L)).astype(jnp.int32),
        "d_out": normal_values(seeds[2], (MB, SEQS, L, D), 1.0, 6.0, ((1, 8), (2, 4))),
        "norm1_gain": jnp.clip(1.0 + 0.18 * jax.random.normal(seeds[3], (D,), jnp.float32), 0.099609375, 1.8984375).astype(jnp.bfloat16),
        "w_query": normal_values(seeds[4], (D, HEADS * HD), D ** -0.5, 0.1875, ((1, 4),)),
        "w_key": normal_values(seeds[5], (D, HEADS * HD), D ** -0.5, 0.1875, ((1, 4),)),
        "w_value": normal_values(seeds[6], (D, HEADS * HD), D ** -0.5, 0.1875, ((1, 4),)),
        "w_beta": normal_values(seeds[7], (D, HEADS), D ** -0.5, 0.1875, ((1, 4),)),
        "conv_weight": normal_values(seeds[8], (3, CONV, HEADS * HD), 0.5, 2.0, ((2, 4),)),
        "w_out": normal_values(seeds[9], (HEADS * HD, D), (HEADS * HD // 2) ** -0.5, 0.25, ((0, 4),)),
        "norm2_gain": jnp.clip(1.0 + 0.18 * jax.random.normal(seeds[10], (D,), jnp.float32), 0.099609375, 1.8984375).astype(jnp.bfloat16),
        "w_gate": normal_values(seeds[11], (D, FF), D ** -0.5, 0.1875, ((1, 4),)),
        "w_up": normal_values(seeds[12], (D, FF), D ** -0.5, 0.1875, ((1, 4),)),
        "w_down": normal_values(seeds[13], (FF, D), FF ** -0.5, 0.109375, ((0, 4),)),
    }


EPS = 1e-06

@jax.custom_vjp
def low(v):
    return lax.optimization_barrier(v.astype(jnp.bfloat16)).astype(jnp.float32)

@jax.custom_vjp
def low_back(v):
    return v

def low_keep(v):
    return (low(v), None)

def low_pass(kept, grad):
    return (grad,)

def back_keep(v):
    return (v, None)

def back_low(kept, grad):
    return (low(grad),)
low.defvjp(low_keep, low_pass)
low_back.defvjp(back_keep, back_low)

def matmul(left, right):
    return jnp.einsum('gtd,dc->gtc', left, right, precision=lax.Precision.HIGHEST)

def rms(values, gain):
    return values * lax.rsqrt(lax.optimization_barrier(jnp.mean(values * values, axis=-1, keepdims=True)) + EPS) * gain

def short_conv(proj, taps, seg):
    length = proj.shape[1]
    total = jnp.zeros_like(proj)
    for offset in range(taps.shape[0]):
        moved = jnp.pad(proj, ((0, 0), (offset, 0), (0, 0)))[:, :length]
        earlier = jnp.pad(seg, ((0, 0), (offset, 0)), constant_values=-1)[:, :length]
        keep = (earlier == seg).astype(proj.dtype)
        total = total + taps[offset] * moved * keep[:, :, None]
    return total

def unit_heads(values, head):
    shaped = values.reshape(values.shape[0], values.shape[1], -1, head)
    return shaped / jnp.sqrt(lax.optimization_barrier(jnp.sum(shaped * shaped, axis=-1, keepdims=True)) + EPS)

def span_step(state, block):
    query, key, value, beta, seg, before = block
    high = lax.Precision.HIGHEST
    size = query.shape[1]
    same = seg[:, :, None] == seg[:, None, :]
    row_ids = lax.broadcasted_iota(jnp.int32, (size, size), 0)
    col_ids = lax.broadcasted_iota(jnp.int32, (size, size), 1)
    strict = (same & (row_ids > col_ids)[None]).astype(query.dtype)
    within = (same & (row_ids >= col_ids)[None]).astype(query.dtype)
    live = (seg == before[:, None]).astype(query.dtype)
    beta_heads = jnp.transpose(beta, (0, 2, 1))
    keys_keys = jnp.einsum('gihe,gjhe->ghij', key, key, precision=high)
    system = jnp.eye(size, dtype=query.dtype) + beta_heads[:, :, :, None] * keys_keys * strict[:, None]
    carried = jnp.einsum('ghde,gihe->ghid', state, key, precision=high)
    live_heads = live[:, None, :, None]
    right = beta_heads[..., None] * (jnp.transpose(value, (0, 2, 1, 3)) - live_heads * carried)
    update = lax.linalg.triangular_solve(system, right, left_side=True, lower=True, unit_diagonal=True)
    scores = jnp.einsum('gihe,gjhe->ghij', query, key, precision=high) * within[:, None]
    mixed = live_heads * jnp.einsum('ghde,gihe->ghid', state, query, precision=high)
    mixed = mixed + jnp.einsum('ghij,ghjd->ghid', scores, update, precision=high)
    last = same[:, -1, :].astype(query.dtype)
    state_next = live[:, -1][:, None, None, None] * state + jnp.einsum('ghjd,ghje->ghde', update * last[:, None, :, None], jnp.transpose(key, (0, 2, 1, 3)), precision=high)
    return (state_next, jnp.transpose(mixed, (0, 2, 1, 3)))

def delta_rule(query, key, value, beta, seg):
    batch, length, heads, head = query.shape
    blocks = length // SPAN

    def split(values):
        return jnp.swapaxes(values.reshape((batch, blocks, SPAN) + values.shape[2:]), 0, 1)
    before = jnp.pad(seg, ((0, 0), (1, 0)), constant_values=-1)[:, :length]
    starts = jnp.swapaxes(before.reshape(batch, blocks, SPAN)[:, :, 0], 0, 1)
    state = jnp.zeros((batch, heads, head, head), query.dtype)
    _, outputs = lax.scan(jax.checkpoint(span_step), state, (split(query), split(key), split(value), split(beta), split(seg), starts))
    return jnp.swapaxes(outputs, 0, 1).reshape(batch, length, heads * head)

def layer(params, rows, seg):
    gain1, w_q, w_k, w_v, w_b, taps, w_o, gain2, w_g, w_u, w_d = params
    normed1 = low(rms(rows, gain1))
    q_proj = low_back(matmul(normed1, w_q))
    k_proj = low_back(matmul(normed1, w_k))
    v_proj = low_back(matmul(normed1, w_v))
    b_proj = low_back(matmul(normed1, w_b))
    query = unit_heads(jax.nn.silu(short_conv(q_proj, taps[0], seg)), HD)
    key = unit_heads(jax.nn.silu(short_conv(k_proj, taps[1], seg)), HD)
    value = jax.nn.silu(short_conv(v_proj, taps[2], seg)).reshape(query.shape)
    beta = jax.nn.sigmoid(b_proj)
    mixed = low(delta_rule(query, key, value, beta, seg))
    mid = rows + low_back(matmul(mixed, w_o))
    normed2 = low(rms(mid, gain2))
    gate = low_back(matmul(normed2, w_g))
    up_part = low_back(matmul(normed2, w_u))
    hidden = low(jax.nn.silu(gate) * up_part)
    return mid + matmul(hidden, w_d)

def reference(layer_input, segment, d_out, norm1_gain, w_query, w_key, w_value, w_beta, conv_weight, w_out, norm2_gain, w_gate, w_up, w_down):
    params = tuple((p.astype(jnp.float32) for p in (norm1_gain, w_query, w_key, w_value, w_beta, conv_weight, w_out, norm2_gain, w_gate, w_up, w_down)))
    length = layer_input.shape[2]
    width = layer_input.shape[3]
    rows = layer_input.astype(jnp.float32).reshape(-1, 2, length, width)
    cotangents = d_out.astype(jnp.float32).reshape(-1, 2, length, width)
    segs = segment.reshape(-1, 2, length).astype(jnp.int32)
    zeros = jax.tree.map(jnp.zeros_like, params)

    def group(totals, item):
        part, cotangent, seg = item

        def forward(weights, values):
            return layer(weights, values, seg)
        result, back = jax.vjp(forward, params, part)
        grads, d_rows = back(cotangent)
        totals = jax.tree.map(jnp.add, totals, grads)
        return (totals, (result.astype(jnp.bfloat16), d_rows.astype(jnp.bfloat16)))
    totals, (results, d_inputs) = lax.scan(group, zeros, (rows, cotangents, segs))
    return (results.reshape(layer_input.shape), d_inputs.reshape(layer_input.shape), totals[0], totals[1], totals[2], totals[3], totals[4], totals[5], totals[6], totals[7], totals[8], totals[9], totals[10])
```

```python
import functools

import jax
import jax.numpy as jnp
from jax import lax
from jax.experimental import pallas as pl
from jax.experimental.pallas import tpu as pltpu
from jax.sharding import PartitionSpec as P

HD = 128
HALO = 16
PIECES = 8
EPS = 1e-06
F32 = jnp.float32
BF16 = jnp.bfloat16
MIB = 1 << 20


def mm(a, b, ta=False, tb=False):
    dims = (((0 if ta else 1,), (1 if tb else 0,)), ((), ()))
    return lax.dot_general(a.astype(BF16), b.astype(BF16), dims, preferred_element_type=F32)


def invert_unit(low):
    size = low.shape[0]
    row = lax.broadcasted_iota(jnp.int32, (size, size), 0)
    col = lax.broadcasted_iota(jnp.int32, (size, size), 1)
    eye = (row == col).astype(F32)
    inv = eye - jnp.where((row >> 1) == (col >> 1), low, 0.0)
    step = 1
    while (2 << step) <= size:
        pair = ((row >> (step + 1)) == (col >> (step + 1))) & ((row >> step) != (col >> step))
        part = jnp.where(pair, low, 0.0)
        inv = inv - mm(mm(inv, part), inv)
        step += 1
    return inv


def short_conv(proj, taps, keeps):
    total = taps[0:1] * proj[HALO:]
    for i in range(1, 4):
        total = total + taps[i : i + 1] * (pltpu.roll(proj, i, 0)[HALO:] * keeps[i - 1])
    return total


def silu_unit(conv):
    sig = jax.nn.sigmoid(conv)
    act = conv * sig
    scale = lax.rsqrt(jnp.sum(act * act, axis=-1, keepdims=True) + EPS)
    return act * scale, scale, sig


def silu_unit_back(grad, conv, unit, scale, sig):
    d_act = scale * (grad - unit * jnp.sum(grad * unit, axis=-1, keepdims=True))
    return d_act * sig * (1.0 + conv * (1.0 - sig))


def masks(aux, seg_row):
    n = aux.shape[0]
    row = lax.broadcasted_iota(jnp.int32, (n, n), 0)
    col = lax.broadcasted_iota(jnp.int32, (n, n), 1)
    same = aux[:, 5:6] == seg_row
    strict = jnp.where(same & (row > col), 1.0, 0.0)
    within = jnp.where(same & (row >= col), 1.0, 0.0)
    return strict, within


def head_weights(ref):
    return ref[0]


def local_kernel(x_ref, w_ref, taps_ref, aux_ref, seg_ref, beta_ref,
                 proj_ref, qk_ref, t_ref, p_ref, ub_ref, w_out_ref, m_ref, a_ref):
    weights = w_ref[0]
    taps = taps_ref[0]
    micro = x_ref.shape[0]
    tokens = aux_ref.shape[1]
    half = tokens // 2
    for m in range(micro):
        aux = aux_ref[m]
        keeps = [aux[:, i : i + 1] for i in range(3)]
        live, last = aux[:, 3:4], aux[:, 4:5]
        strict, within = masks(aux, seg_ref[m, 0:1])
        proj = jnp.dot(x_ref[m], weights, preferred_element_type=F32)
        proj_ref[0, m] = proj
        convs = [
            short_conv(proj[:, j * HD : (j + 1) * HD], taps[4 * j : 4 * j + 4], keeps)
            for j in range(3)
        ]
        query = silu_unit(convs[0])[0]
        key = silu_unit(convs[1])[0]
        value = convs[2] * jax.nn.sigmoid(convs[2])
        beta = beta_ref[0, m]
        low = beta * mm(key, key, tb=True) * strict
        scores = mm(query, key, tb=True) * within
        top = invert_unit(low[:half, :half])
        bottom = invert_unit(low[half:, half:])
        cross = -mm(mm(bottom, low[half:, :half]), top)
        inv = jnp.concatenate(
            [
                jnp.concatenate([top, jnp.zeros_like(top)], axis=1),
                jnp.concatenate([cross, bottom], axis=1),
            ],
            axis=0,
        ).astype(BF16)
        both = mm(inv, jnp.concatenate([beta * value, (beta * live) * key], axis=1))
        late = (last * key).astype(BF16)
        sums = mm(both, late, ta=True)
        row = lax.broadcasted_iota(jnp.int32, (HD, HD), 0)
        col = lax.broadcasted_iota(jnp.int32, (HD, HD), 1)
        keep_state = jnp.where(row == col, live[tokens - 1 : tokens], 0.0)
        qk_ref[0, m] = jnp.concatenate([query, key], axis=1).astype(BF16)
        t_ref[0, m] = inv
        p_ref[0, m] = scores.astype(BF16)
        ub_ref[0, m] = both[:, :HD]
        w_out_ref[0, m] = both[:, HD:].astype(BF16)
        a_ref[0, m] = sums[:HD]
        m_ref[0, m] = keep_state - sums[HD:]


def output_kernel(qk_ref, p_ref, ub_ref, w_ref, state_ref, aux_ref, mixed_ref, u_ref):
    for m in range(aux_ref.shape[0]):
        live = aux_ref[m][:, 3:4]
        state = state_ref[0, m].astype(BF16)
        update = ub_ref[0, m] - mm(w_ref[0, m], state, tb=True)
        update = update.astype(BF16)
        mixed = live * mm(qk_ref[0, m][:, :HD], state, tb=True) + mm(p_ref[0, m], update)
        mixed_ref[m] = mixed.astype(BF16)
        u_ref[0, m] = update


def back_local_kernel(dmix_ref, qk_ref, t_ref, p_ref, beta_ref, aux_ref, y_ref, b_ref):
    for m in range(aux_ref.shape[0]):
        live = aux_ref[m][:, 3:4]
        d_out = dmix_ref[m]
        y0 = mm(t_ref[0, m], mm(p_ref[0, m], d_out, ta=True), ta=True)
        y_ref[0, m] = y0
        qk = qk_ref[0, m]
        b_ref[0, m] = mm(live * d_out, qk[:, :HD], ta=True) - mm(
            (beta_ref[0, m] * live) * y0, qk[:, HD:], ta=True
        )


def back_kernel(dmix_ref, y_ref, qk_ref, t_ref, u_ref, state_ref, dstate_ref, proj_ref,
                p_ref, taps_ref, beta_ref, aux_ref, seg_ref,
                dmain_ref, tail_ref, front_ref, dbeta_ref, dtaps_ref):
    taps = taps_ref[0]
    micro, tokens = aux_ref.shape[0], aux_ref.shape[1]
    for m in range(micro):
        aux = aux_ref[m]
        keeps = [aux[:, i : i + 1] for i in range(3)]
        live, last = aux[:, 3:4], aux[:, 4:5]
        strict, within = masks(aux, seg_ref[m, 0:1])
        proj = proj_ref[0, m]
        beta = beta_ref[0, m]
        convs = [
            short_conv(proj[:, j * HD : (j + 1) * HD], taps[4 * j : 4 * j + 4], keeps)
            for j in range(3)
        ]
        query, q_scale, q_sig = silu_unit(convs[0])
        key, k_scale, k_sig = silu_unit(convs[1])
        v_sig = jax.nn.sigmoid(convs[2])
        value = convs[2] * v_sig
        q_low, k_low = qk_ref[0, m][:, :HD], qk_ref[0, m][:, HD:]
        state = state_ref[0, m].astype(BF16)
        dstate = dstate_ref[0, m].astype(BF16)
        update = u_ref[0, m]
        d_out = dmix_ref[m].astype(BF16)
        d_right = y_ref[0, m] + mm(t_ref[0, m], last * mm(k_low, dstate, tb=True), ta=True)
        d_right_low = d_right.astype(BF16)
        d_scores = (mm(d_out, update, tb=True) * within).astype(BF16)
        grad_sys = -mm(d_right_low, update, tb=True) * strict
        keys_keys = mm(k_low, k_low, tb=True)
        d_kk = (beta * grad_sys).astype(BF16)
        carried = mm(k_low, state, tb=True)
        d_carried = ((-beta * live) * d_right).astype(BF16)
        d_query = live * mm(d_out, state) + mm(d_scores, k_low)
        d_key = (
            mm(d_scores, q_low, ta=True)
            + last * mm(update, dstate)
            + mm(d_carried, state)
            + mm(d_kk, k_low)
            + mm(d_kk, k_low, ta=True)
        )
        d_beta = jnp.sum(grad_sys * keys_keys, axis=-1, keepdims=True) + jnp.sum(
            d_right * (value - live * carried), axis=-1, keepdims=True
        )
        d_value = beta * d_right
        dbeta_ref[0, m] = d_beta * beta * (1.0 - beta)
        d_convs = [
            silu_unit_back(d_query, convs[0], query, q_scale, q_sig),
            silu_unit_back(d_key, convs[1], key, k_scale, k_sig),
            d_value * v_sig * (1.0 + convs[2] * (1.0 - v_sig)),
        ]
        tap_sums = []
        for j in range(3):
            part = proj[:, j * HD : (j + 1) * HD]
            d_conv = d_convs[j]
            tap_sums.append(jnp.sum(d_conv * part[HALO:], axis=0, keepdims=True))
            zeros = jnp.zeros((HALO, HD), F32)
            d_proj = jnp.concatenate([zeros, taps[4 * j : 4 * j + 1] * d_conv], axis=0)
            for i in range(1, 4):
                kept = keeps[i - 1] * d_conv
                tap_sums.append(
                    jnp.sum(kept * pltpu.roll(part, i, 0)[HALO:], axis=0, keepdims=True)
                )
                spread = jnp.concatenate([zeros, taps[4 * j + i : 4 * j + i + 1] * kept], axis=0)
                d_proj = d_proj + pltpu.roll(spread, HALO + tokens - i, 0)
            cols = slice(j * HD, (j + 1) * HD)
            front_ref[0, m, :, cols] = d_proj[:HALO]
            tail_ref[0, m, :, cols] = d_proj[tokens:]
            dmain_ref[m, :, cols] = d_proj[HALO:].astype(BF16)
        summed = jnp.concatenate(tap_sums + [jnp.zeros((4, HD), F32)], axis=0)
        if m == 0:
            dtaps_ref[0] = summed
        else:
            dtaps_ref[0] += summed


def grad_kernel(table_ref, left_ref, right_ref, out_ref):
    rows = out_ref.shape[2]
    blocks = []
    for pos in range(out_ref.shape[0]):
        start = pl.multiple_of(table_ref[pos] * rows, rows)
        blocks.append(left_ref[pl.ds(start, rows), :])
    sums = jnp.dot(
        jnp.concatenate(blocks, axis=0), right_ref[0], preferred_element_type=F32
    ).astype(BF16)
    for pos in range(out_ref.shape[0]):
        out_ref[pos, 0] = sums[pos * rows : (pos + 1) * rows]


def place_kernel(ids_ref, *refs):
    sems, out_ref = refs[-1], refs[-2]
    own, pieces = (refs[0], refs[1:-2]) if len(refs) == PIECES + 3 else (None, refs[:-2])
    copies = []
    if own is not None:
        copies.append(pltpu.make_async_copy(own, out_ref.at[0], sems.at[PIECES]))
    for j, piece in enumerate(pieces):
        slots = piece.shape[0]
        target = out_ref.at[pl.ds(out_ref.shape[0] - slots, slots), ids_ref[j]]
        copies.append(pltpu.make_async_copy(piece, target, sems.at[j]))
    for copy in copies:
        copy.start()
    for copy in copies:
        copy.wait()


def params(mib=56):
    return pltpu.CompilerParams(
        dimension_semantics=("arbitrary",), vmem_limit_bytes=mib * MIB
    )


def cost(flops, nbytes):
    return pl.CostEstimate(flops=int(flops), bytes_accessed=int(nbytes), transcendentals=0)


def whole(shape):
    return pl.BlockSpec(shape, lambda h: (0,) * len(shape))


def per_head(*dims):
    return pl.BlockSpec((1,) + dims, lambda h: (h,) + (0,) * len(dims))


def sds(shape, dtype):
    return jax.ShapeDtypeStruct(shape, dtype)


def mixer_local(x_ext, w_heads, taps, aux, seg_row, beta):
    micro, ext, width = x_ext.shape
    tokens = ext - HALO
    heads = taps.shape[0]
    per = heads // w_heads.shape[0]
    hm = (heads, micro)
    outs = [
        sds(hm + (ext, 3 * HD), F32),
        sds(hm + (tokens, 2 * HD), BF16),
        sds(hm + (tokens, tokens), BF16),
        sds(hm + (tokens, tokens), BF16),
        sds(hm + (tokens, HD), F32),
        sds(hm + (tokens, HD), BF16),
        sds(hm + (HD, HD), F32),
        sds(hm + (HD, HD), F32),
    ]
    return pl.pallas_call(
        local_kernel,
        grid=(heads,),
        in_specs=[
            whole(x_ext.shape),
            pl.BlockSpec((1, width, 3 * HD), lambda h: (h // per, 0, h % per)),
            per_head(16, HD),
            whole(aux.shape),
            whole(seg_row.shape),
            per_head(micro, tokens, 1),
        ],
        out_specs=[per_head(*o.shape[1:]) for o in outs],
        out_shape=outs,
        compiler_params=params(),
        cost_estimate=cost(heads * micro * 1.5e9, heads * micro * 3e6),
        name="mixer_local",
    )(x_ext, w_heads, taps, aux, seg_row, beta)


def mixer_output(qk, scores, base, mix, state, aux):
    heads, micro, tokens = qk.shape[:3]
    return pl.pallas_call(
        output_kernel,
        grid=(heads,),
        in_specs=[per_head(*a.shape[1:]) for a in (qk, scores, base, mix, state)]
        + [whole(aux.shape)],
        out_specs=[
            pl.BlockSpec((micro, tokens, HD), lambda h: (0, 0, h)),
            per_head(micro, tokens, HD),
        ],
        out_shape=[
            sds((micro, tokens, heads * HD), BF16),
            sds((heads, micro, tokens, HD), BF16),
        ],
        compiler_params=params(),
        cost_estimate=cost(heads * micro * 2e8, heads * micro * 1e6),
        name="mixer_output",
    )(qk, scores, base, mix, state, aux)


def mixer_back_local(d_mixed, qk, inv, scores, beta, aux):
    heads, micro, tokens = qk.shape[:3]
    return pl.pallas_call(
        back_local_kernel,
        grid=(heads,),
        in_specs=[pl.BlockSpec((micro, tokens, HD), lambda h: (0, 0, h))]
        + [per_head(*a.shape[1:]) for a in (qk, inv, scores, beta)]
        + [whole(aux.shape)],
        out_specs=[per_head(micro, tokens, HD), per_head(micro, HD, HD)],
        out_shape=[
            sds((heads, micro, tokens, HD), F32),
            sds((heads, micro, HD, HD), F32),
        ],
        compiler_params=params(),
        cost_estimate=cost(heads * micro * 2e8, heads * micro * 1e6),
        name="mixer_back_local",
    )(d_mixed, qk, inv, scores, beta, aux)


def mixer_back(d_mixed, y0, qk, inv, update, state, d_state, proj, scores, taps, beta, aux, seg_row):
    heads, micro, tokens = qk.shape[:3]
    columns = lambda n: pl.BlockSpec((micro, tokens, n), lambda h: (0, 0, h))
    return pl.pallas_call(
        back_kernel,
        grid=(heads,),
        in_specs=[columns(HD)]
        + [
            per_head(*a.shape[1:])
            for a in (y0, qk, inv, update, state, d_state, proj, scores, taps, beta)
        ]
        + [whole(aux.shape), whole(seg_row.shape)],
        out_specs=[
            columns(3 * HD),
            per_head(micro, HALO, 3 * HD),
            per_head(micro, HALO, 3 * HD),
            per_head(micro, tokens, 1),
            per_head(16, HD),
        ],
        out_shape=[
            sds((micro, tokens, heads * 3 * HD), BF16),
            sds((heads, micro, HALO, 3 * HD), F32),
            sds((heads, micro, HALO, 3 * HD), F32),
            sds((heads, micro, tokens, 1), F32),
            sds((heads, 16, HD), F32),
        ],
        compiler_params=params(),
        cost_estimate=cost(heads * micro * 1e9, heads * micro * 3e6),
        name="mixer_back",
    )(d_mixed, y0, qk, inv, update, state, d_state, proj, scores, taps, beta, aux, seg_row)


def grad_pieces(left, right, table):
    slots, tokens, n = right.shape
    count = table.shape[0]
    rows = left.shape[0] // PIECES
    return pl.pallas_call(
        grad_kernel,
        grid_spec=pltpu.PrefetchScalarGridSpec(
            num_scalar_prefetch=1,
            grid=(slots,),
            in_specs=[
                pl.BlockSpec(left.shape, lambda s, t: (0, 0)),
                pl.BlockSpec((1, tokens, n), lambda s, t: (s, 0, 0)),
            ],
            out_specs=pl.BlockSpec((count, 1, rows, n), lambda s, t: (0, s, 0, 0)),
        ),
        out_shape=sds((count, slots, rows, n), BF16),
        compiler_params=params(),
        cost_estimate=cost(2 * count * rows * tokens * n * slots, 2 * count * slots * rows * n),
        name="grad_pieces",
    )(table, left, right)


def place(pieces, ids, own=None):
    slots, rows, n = pieces[0].shape
    anywhere = pl.BlockSpec(memory_space=pl.ANY)
    args = ([] if own is None else [own.reshape(PIECES, rows, n)]) + list(pieces)
    shape = (slots + (own is not None), PIECES, rows, n)
    return pl.pallas_call(
        place_kernel,
        grid_spec=pltpu.PrefetchScalarGridSpec(
            num_scalar_prefetch=1,
            grid=(1,),
            in_specs=[anywhere] * len(args),
            out_specs=pl.BlockSpec(shape, lambda i, t: (0, 0, 0, 0)),
            scratch_shapes=[pltpu.SemaphoreType.DMA((PIECES + 1,))],
        ),
        out_shape=sds(shape, pieces[0].dtype),
        compiler_params=params(),
        cost_estimate=cost(0, 4 * shape[0] * PIECES * rows * n),
        name="place",
    )(jnp.stack(ids), *args)


def swap(x, mask_of, size):
    return lax.ppermute(x, "dp", [(i, i ^ mask_of(i)) for i in range(size)])


def first(i):
    return 4 if i & 1 else 2


def second(i):
    return 2 if i & 1 else 4


def across(i):
    return 1


def from_ahead(x, k, size):
    return lax.ppermute(x, "tensor", [(i, (i - k) % size) for i in range(size)])


def to_ahead(x, k, size):
    return lax.ppermute(x, "tensor", [(i, (i + k) % size) for i in range(size)])


def plane_gather(own, dp):
    b = swap(own, first, dp)
    c = swap(own, second, dp)
    d = swap(b, second, dp)
    near = [own, b, c, d]
    return near + [swap(piece, across, dp) for piece in near]


def piece_ids(own):
    core = own & 1
    f = jnp.where(core == 1, 4, 2)
    s = jnp.where(core == 1, 2, 4)
    return [own, own ^ f, own ^ s, own ^ 6, own ^ 1, own ^ 1 ^ s, own ^ 1 ^ f, own ^ 7]


def gather_quarters(quarter, dp, tensor, own):
    rows = quarter.shape[0] // PIECES
    n = quarter.shape[1]
    mine = lax.dynamic_slice_in_dim(quarter, own * rows, rows, 0)
    others = jnp.stack([from_ahead(mine, k, tensor) for k in range(1, tensor)])
    full = place(plane_gather(others, dp), piece_ids(own), quarter)
    return full.reshape(tensor, PIECES * rows, n)


def add(a, b):
    return (a.astype(F32) + b.astype(F32)).astype(BF16)


def reduce_quarters(left, right, dp, tensor, own):
    ids = piece_ids(own)
    theirs = grad_pieces(left, right, jnp.stack([ids[4], ids[6], ids[5], ids[7]]))
    got = swap(theirs, across, dp)
    mine = grad_pieces(left, right, jnp.stack([ids[0], ids[2], ids[1], ids[3]]))
    total = add(mine, got)
    total = add(total[:2], swap(total[2:], first, dp))
    total = add(total[0], swap(total[1], second, dp))
    parts = [total[0]] + [to_ahead(total[k], k, tensor) for k in range(1, tensor)]
    total = sum(p.astype(F32) for p in parts).astype(BF16)
    mask = PIECES
    while mask < dp:
        total = add(total, swap(total, lambda i: mask, dp))
        mask *= 2
    rows, n = total.shape
    full = place([piece[None] for piece in plane_gather(total, dp)], ids)
    return full.reshape(PIECES * rows, n).astype(F32)


def norm_rows(rows, gain):
    rstd = lax.rsqrt(jnp.mean(rows * rows, axis=-1, keepdims=True) + EPS)
    unit = rows * rstd
    return (unit * gain, unit, rstd)


def norm_back(grad, unit, rstd, gain):
    scaled = grad * gain
    d_rows = rstd * (scaled - unit * jnp.mean(scaled * unit, axis=-1, keepdims=True))
    return (d_rows, jnp.sum(grad * unit, axis=0))


def shards(dp, tensor, layer_input, segment, d_out, norm1_gain, w_query, w_key, w_value, w_beta,
           conv_weight, w_out, norm2_gain, w_gate, w_up, w_down):
    micro, _, tokens, width = layer_input.shape
    count = micro * tokens
    local_heads = w_query.shape[1] // HD
    heads = local_heads * tensor
    hidden_part = w_gate.shape[1]
    index = lax.axis_index("dp")
    own = index % PIECES
    place = lax.axis_index("tensor")
    gain1 = norm1_gain.astype(F32)
    gain2 = norm2_gain.astype(F32)

    rows = layer_input.reshape(count, width).astype(F32)
    normed1, unit1, rstd1 = norm_rows(rows, gain1)
    normed1 = normed1.astype(BF16)
    mixer_in = normed1.reshape(micro, tokens, width)
    ahead = [(i, i + 1) for i in range(tensor - 1)]
    behind = [(i + 1, i) for i in range(tensor - 1)]
    halo = lax.ppermute(mixer_in[:, tokens - HALO :], "tensor", ahead)
    x_ext = jnp.concatenate([halo, mixer_in], axis=1)

    heads_of = lambda w: w.reshape(width, local_heads, HD)
    w_qkv = jnp.concatenate([heads_of(w_query), heads_of(w_key), heads_of(w_value)], axis=2)
    w_qkv = w_qkv.reshape(width, local_heads * 3 * HD)
    small = jnp.concatenate([w_beta.T, conv_weight.reshape(-1, width)], axis=0)
    smalls = jnp.stack([small] + [from_ahead(small, k, tensor) for k in range(1, tensor)])
    mixer_w = gather_quarters(jnp.concatenate([w_qkv, w_out.T], axis=1), dp, tensor, own)
    ffn_w = gather_quarters(jnp.concatenate([w_gate, w_up, w_down.T], axis=1), dp, tensor, own)
    w_beta_all = smalls[:, :local_heads].reshape(heads, width)
    taps = smalls[:, local_heads:].reshape(tensor, 12, local_heads, HD).astype(F32)
    taps = jnp.swapaxes(taps, 1, 2).reshape(heads, 12, HD)
    taps = jnp.pad(taps, ((0, 0), (0, 4), (0, 0)))

    seg = jnp.pad(segment[:, 0], ((0, 0), (HALO, 0)), constant_values=-1)
    seg = lax.dynamic_slice_in_dim(seg, place * tokens, HALO + tokens, 1)
    seg_own = seg[:, HALO:]
    flags = [seg[:, HALO - i : HALO - i + tokens] == seg_own for i in (1, 2, 3)]
    flags += [seg_own == seg[:, HALO - 1 : HALO], seg_own == seg_own[:, -1:]]
    flags = [f.astype(F32) for f in flags] + [seg_own.astype(F32)]
    aux = jnp.stack(flags + [jnp.zeros_like(flags[0])] * 2, axis=-1)
    seg_row = jnp.broadcast_to(seg_own.astype(F32)[:, None], (micro, 8, tokens))

    b_proj = jnp.dot(normed1, w_beta_all.T, preferred_element_type=F32)
    beta = jax.nn.sigmoid(b_proj).reshape(micro, tokens, heads)
    beta = jnp.transpose(beta, (2, 0, 1))[..., None]
    proj, qk, inv, scores, base, mix, keep, gain = mixer_local(
        x_ext, mixer_w, taps, aux, seg_row, beta
    )
    exact = functools.partial(jnp.einsum, precision=lax.Precision.HIGHEST)
    out_state = gain
    for hop in range(tensor - 1):
        state = lax.ppermute(out_state.astype(BF16), "tensor", ahead).astype(F32)
        state = jnp.roll(state, -local_heads, axis=0)
        if hop < tensor - 2:
            out_state = exact("hmdf,hmfe->hmde", state, keep) + gain
    mixed, update = mixer_output(qk, scores, base, mix, state, aux)
    mixed = mixed.reshape(count, heads * HD)
    mixed_s = mixed.reshape(count, tensor, local_heads * HD)
    w_out_all = mixer_w[:, :, local_heads * 3 * HD :]
    attn = jnp.einsum("tsc,sdc->td", mixed_s, w_out_all, preferred_element_type=F32)
    mid = rows + attn

    normed2, unit2, rstd2 = norm_rows(mid, gain2)
    normed2 = normed2.astype(BF16)
    out_grad = d_out.reshape(count, width)
    w_gu = ffn_w[:, :, : 2 * hidden_part]
    w_dn = ffn_w[:, :, 2 * hidden_part :]
    gate_up = jnp.einsum("td,sdf->stf", normed2, w_gu, preferred_element_type=F32)
    gate, up_part = gate_up[:, :, :hidden_part], gate_up[:, :, hidden_part:]
    sigma = jax.nn.sigmoid(gate)
    hidden = (gate * sigma * up_part).astype(BF16)
    result = mid + jnp.einsum("stf,sdf->td", hidden, w_dn, preferred_element_type=F32)
    output = result.astype(BF16).reshape(micro, 1, tokens, width)
    d_hidden = jnp.einsum("td,sdf->stf", out_grad, w_dn, preferred_element_type=F32)
    d_gate = (d_hidden * up_part * sigma * (1.0 + gate * (1.0 - sigma))).astype(BF16)
    d_up = (d_hidden * gate * sigma).astype(BF16)
    d_gu = jnp.concatenate([d_gate, d_up], axis=2)
    d_normed2 = jnp.einsum("stf,sdf->td", d_gu, w_gu, preferred_element_type=F32)
    reduce = functools.partial(reduce_quarters, dp=dp, tensor=tensor, own=own)
    grad_dn = reduce(out_grad.T, hidden)
    grad_gu = reduce(normed2.T, d_gu)
    d_mid, gain2_part = norm_back(d_normed2, unit2, rstd2, gain2)
    d_mid = out_grad.astype(F32) + d_mid
    d_mid_low = d_mid.astype(BF16)

    grad_out = reduce(d_mid_low.T, jnp.swapaxes(mixed_s, 0, 1))
    d_mixed = jnp.einsum("td,sdc->tsc", d_mid_low, w_out_all, preferred_element_type=F32)
    d_mixed = d_mixed.reshape(micro, tokens, heads * HD)
    y0, back_gain = mixer_back_local(d_mixed, qk, inv, scores, beta, aux)
    out_state = back_gain
    for hop in range(tensor - 1):
        d_state = lax.ppermute(out_state.astype(BF16), "tensor", behind).astype(F32)
        d_state = jnp.roll(d_state, local_heads, axis=0)
        if hop < tensor - 2:
            out_state = exact("hmde,hmfe->hmdf", d_state, keep) + back_gain
    d_qkv, tail, front, d_beta, d_taps = mixer_back(
        d_mixed, y0, qk, inv, update, state, d_state, proj, scores, taps, beta, aux, seg_row
    )
    front = jnp.roll(lax.ppermute(front, "tensor", behind), local_heads, axis=0)
    tail = jnp.transpose(tail + front, (1, 2, 0, 3)).reshape(micro, HALO, -1).astype(BF16)
    d_qkv = lax.dynamic_update_slice(d_qkv, tail, (0, tokens - HALO, 0))
    d_qkv = d_qkv.reshape(count, tensor, local_heads * 3 * HD)
    d_b = jnp.transpose(d_beta[..., 0], (1, 2, 0)).reshape(count, heads).astype(BF16)
    grad_qkv = reduce(normed1.T, jnp.swapaxes(d_qkv, 0, 1))
    w_qkv_all = mixer_w[:, :, : local_heads * 3 * HD]
    d_normed1 = jnp.einsum("tsc,sdc->td", d_qkv, w_qkv_all, preferred_element_type=F32)
    d_normed1 = d_normed1 + jnp.dot(d_b, w_beta_all, preferred_element_type=F32)
    d_in, gain1_part = norm_back(d_normed1, unit1, rstd1, gain1)
    input_grad = (d_mid + d_in).astype(BF16).reshape(micro, 1, tokens, width)

    grad_b = jnp.einsum("th,td->hd", d_b, normed1, preferred_element_type=F32)
    part = width // tensor
    d_taps = d_taps[:, :12].reshape(tensor, local_heads, 12, HD)
    d_taps = jnp.swapaxes(d_taps, 1, 2).reshape(tensor, -1)
    packed = []
    for k in range(tensor):
        at = ((place + k) % tensor) * part
        packed.append(
            jnp.concatenate(
                [
                    grad_b[k * local_heads : (k + 1) * local_heads].reshape(-1),
                    d_taps[k],
                    lax.dynamic_slice_in_dim(gain1_part, at, part),
                    lax.dynamic_slice_in_dim(gain2_part, at, part),
                ]
            )
        )
    packed = [packed[0]] + [to_ahead(packed[k], k, tensor) for k in range(1, tensor)]
    packed = sum(packed)
    mask = 1
    while mask < dp:
        packed = packed + swap(packed, lambda i: mask, dp)
        mask *= 2
    cut = local_heads * width
    grad_beta = packed[:cut].reshape(local_heads, width).T
    grad_conv = packed[cut : cut + 12 * part].reshape(3, 4, part)
    cut += 12 * part
    grad_gain1 = packed[cut : cut + part]
    grad_gain2 = packed[cut + part : cut + 2 * part]
    grad_qkv = grad_qkv.reshape(width, local_heads, 3, HD)
    grad_q, grad_k, grad_v = (grad_qkv[:, :, j].reshape(width, -1) for j in range(3))
    return (
        output,
        input_grad,
        grad_gain1,
        grad_q,
        grad_k,
        grad_v,
        grad_beta,
        grad_conv,
        grad_out.T,
        grad_gain2,
        grad_gu[:, :hidden_part],
        grad_gu[:, hidden_part:],
        grad_dn.T,
    )


def solution(mesh):
    in_specs = (
        P(None, "dp", "tensor", None),
        P(None, "dp", None),
        P(None, "dp", "tensor", None),
        P(),
        P(None, "tensor"),
        P(None, "tensor"),
        P(None, "tensor"),
        P(None, "tensor"),
        P(None, None, "tensor"),
        P("tensor", None),
        P(),
        P(None, "tensor"),
        P(None, "tensor"),
        P("tensor", None),
    )
    out_specs = (
        P(None, "dp", "tensor", None),
        P(None, "dp", "tensor", None),
        P("tensor"),
        P(None, "tensor"),
        P(None, "tensor"),
        P(None, "tensor"),
        P(None, "tensor"),
        P(None, None, "tensor"),
        P("tensor", None),
        P("tensor"),
        P(None, "tensor"),
        P(None, "tensor"),
        P("tensor", None),
    )
    body = functools.partial(shards, mesh.shape["dp"], mesh.shape["tensor"])
    return jax.shard_map(body, mesh=mesh, in_specs=in_specs, out_specs=out_specs, check_vma=False)
```

```python
import functools

import jax
import jax.numpy as jnp
from jax import lax
from jax.experimental import pallas as pl
from jax.experimental.pallas import tpu as pltpu
from jax.sharding import PartitionSpec as P

HD = 128
HALO = 16
EXTRA = 16
LANES = 16
PIECES = 8
EPS = 1e-06
F32 = jnp.float32
BF16 = jnp.bfloat16
MIB = 1 << 20


def mm(a, b, ta=False, tb=False):
    dims = (((0 if ta else 1,), (1 if tb else 0,)), ((), ()))
    return lax.dot_general(a.astype(BF16), b.astype(BF16), dims, preferred_element_type=F32)


def interleave(makers):
    running = list(makers)
    while running:
        still = []
        for g in running:
            try:
                next(g)
                still.append(g)
            except StopIteration:
                pass
        running = still


def invert_unit(lows):
    size = lows[0].shape[0]
    row = lax.broadcasted_iota(jnp.int32, (size, size), 0)
    col = lax.broadcasted_iota(jnp.int32, (size, size), 1)
    eye = (row == col).astype(F32)
    invs = [eye - jnp.where((row >> 1) == (col >> 1), low, 0.0) for low in lows]
    step = 1
    while (2 << step) <= size:
        pair = ((row >> (step + 1)) == (col >> (step + 1))) & ((row >> step) != (col >> step))
        lefts = [mm(inv, jnp.where(pair, low, 0.0)) for inv, low in zip(invs, lows)]
        yield
        invs = [inv - mm(left, inv) for inv, left in zip(invs, lefts)]
        yield
        step += 1
    return invs


def short_conv(proj, taps, keeps):
    total = taps[0:1] * proj[HALO:]
    for i in range(1, 4):
        total = total + taps[i : i + 1] * (pltpu.roll(proj, i, 0)[HALO:] * keeps[i - 1])
    return total


def silu_unit(conv):
    sig = jax.nn.sigmoid(conv)
    act = conv * sig
    scale = lax.rsqrt(jnp.sum(act * act, axis=-1, keepdims=True) + EPS)
    return act * scale, scale, sig


def silu_unit_back(grad, conv, unit, scale, sig):
    d_act = scale * (grad - unit * jnp.sum(grad * unit, axis=-1, keepdims=True))
    return d_act * sig * (1.0 + conv * (1.0 - sig))


def flags(seg):
    own = seg[HALO:]
    equal = lambda a: jnp.where(own == a, 1.0, 0.0)
    keeps = [equal(pltpu.roll(jnp.broadcast_to(seg, (seg.shape[0], HD)), i, 0)[HALO:, 0:1]) for i in (1, 2, 3)]
    return keeps, equal(seg[HALO - 1 : HALO]), equal(seg[-1:])


def masks(seg, seg_row):
    n = seg_row.shape[1]
    row = lax.broadcasted_iota(jnp.int32, (n, n), 0)
    col = lax.broadcasted_iota(jnp.int32, (n, n), 1)
    same = seg[HALO:] == seg_row
    strict = jnp.where(same & (row > col), 1.0, 0.0)
    within = jnp.where(same & (row >= col), 1.0, 0.0)
    return strict, within


def pick(values, head):
    lane = lax.broadcasted_iota(jnp.int32, values.shape, 1)
    return jnp.sum(jnp.where(lane == head, values, 0.0), axis=-1, keepdims=True)


def piece_copies(ids_ref, own_ref, piece_refs, w_ref, sems):
    slots = [[pltpu.make_async_copy(own_ref, w_ref.at[0], sems.at[0, 0])]]
    for slot in range(1, w_ref.shape[0]):
        slots.append(
            [
                pltpu.make_async_copy(
                    piece.at[slot - 1], w_ref.at[slot, ids_ref[j]], sems.at[slot, j]
                )
                for j, piece in enumerate(piece_refs)
            ]
        )
    return slots


def local_kernel(ids_ref, x_ref, halo_ref, seg_ref, seg_row_ref, own_ref, *refs):
    pieces = refs[:PIECES]
    (w_ref, beta_ref, taps_ref, beta_w_ref, proj_ref, qk_ref, t_ref, p_ref, ub_ref, w_out_ref, m_ref,
     a_ref, s_ref, sems) = refs[PIECES:]
    slot = pl.program_id(0)
    per = taps_ref.shape[0]
    micro, tokens, width = x_ref.shape
    half = tokens // 2
    rows = width // PIECES
    copies = piece_copies(ids_ref, own_ref, pieces, w_ref, sems)

    @pl.when(slot == 0)
    def _():
        for group in copies:
            for copy in group:
                copy.start()
        beta_ref[...] = jnp.zeros_like(beta_ref)

    for k, group in enumerate(copies):

        @pl.when(slot == k)
        def _():
            for copy in group:
                copy.wait()

    def extra(piece, j):
        return w_ref[slot, piece, rows:, j * HD : (j + 1) * HD]

    beta_w = jnp.concatenate(
        [jnp.concatenate([extra(p, hh) for p in range(PIECES)], axis=1) for hh in range(per)], axis=0
    )
    beta_w_ref[0] = beta_w
    for hh in range(per):
        lines = [extra(per * (r % 4) + hh, per + r // 4)[0:1].astype(F32) for r in range(12)]
        taps_ref[hh] = jnp.concatenate(lines + [jnp.zeros((4, HD), F32)], axis=0)
    lane = lax.broadcasted_iota(jnp.int32, (tokens, HD), 1)

    weights = w_ref[slot, :, :rows].reshape(width, per * 3 * HD)
    shared = []
    for m in range(micro):
        x_ext = jnp.concatenate([halo_ref[m], x_ref[m]], axis=0)
        proj = jnp.dot(x_ext, weights, preferred_element_type=F32)
        seg = seg_ref[m]
        betas = jax.nn.sigmoid(mm(x_ref[m], beta_w, tb=True))
        shared.append((proj, betas, flags(seg), masks(seg, seg_row_ref[m, 0:1])))

    def instance(hh, m):
        proj, betas, (keeps, live, last), (strict, within) = shared[m]
        proj = proj[:, hh * 3 * HD : (hh + 1) * 3 * HD]
        taps = taps_ref[hh]
        proj_ref[hh, m] = proj
        convs = [
            short_conv(proj[:, j * HD : (j + 1) * HD], taps[4 * j : 4 * j + 4], keeps)
            for j in range(3)
        ]
        query = silu_unit(convs[0])[0]
        key = silu_unit(convs[1])[0]
        value = convs[2] * jax.nn.sigmoid(convs[2])
        beta = betas[:, hh * LANES : hh * LANES + 1]
        beta_ref[m] += jnp.where(lane == (slot * per + hh) * LANES, beta, 0.0)
        qk_ref[hh, m] = jnp.concatenate([query, key], axis=1).astype(BF16)
        yield
        low = beta * mm(key, key, tb=True) * strict
        scores = mm(query, key, tb=True) * within
        p_ref[hh, m] = scores.astype(BF16)
        yield
        top, bottom = yield from invert_unit([low[:half, :half], low[half:, half:]])
        cross = mm(bottom, low[half:, :half])
        yield
        cross = -mm(cross, top)
        yield
        inv = jnp.concatenate(
            [
                jnp.concatenate([top, jnp.zeros_like(top)], axis=1),
                jnp.concatenate([cross, bottom], axis=1),
            ],
            axis=0,
        ).astype(BF16)
        t_ref[hh, m] = inv
        both = mm(inv, jnp.concatenate([beta * value, (beta * live) * key], axis=1))
        yield
        late = (last * key).astype(BF16)
        sums = mm(both, late, ta=True)
        row = lax.broadcasted_iota(jnp.int32, (HD, HD), 0)
        col = lax.broadcasted_iota(jnp.int32, (HD, HD), 1)
        keep_state = jnp.where(row == col, live[tokens - 1 : tokens], 0.0)
        ub_ref[hh, m] = both[:, :HD]
        w_out_ref[hh, m] = both[:, HD:].astype(BF16)
        a_ref[hh, m] = sums[:HD]
        s_ref[hh, m] = sums[:HD].astype(BF16)
        m_ref[hh, m] = keep_state - sums[HD:]

    interleave([instance(hh, m) for hh in range(per) for m in range(micro)])


def hop_kernel(back, state_ref, keep_ref, gain_ref, out_ref):
    for h in range(gain_ref.shape[0]):
        for m in range(gain_ref.shape[1]):
            keep = keep_ref[h, m]
            high = keep.astype(BF16)
            rest = (keep - high.astype(F32)).astype(BF16)
            state = state_ref[h, m]
            moved = mm(state, high, tb=back) + mm(state, rest, tb=back)
            out_ref[h, m] = (moved + gain_ref[h, m]).astype(BF16)


def output_kernel(qk_ref, p_ref, ub_ref, w_ref, state_ref, seg_ref, mixed_ref, u_ref):
    per, micro = ub_ref.shape[:2]

    def instance(hh, m):
        live = flags(seg_ref[m])[1]
        state = state_ref[hh, m]
        update = ub_ref[hh, m] - mm(w_ref[hh, m], state, tb=True)
        update = update.astype(BF16)
        far = live * mm(qk_ref[hh, m][:, :HD], state, tb=True)
        yield
        mixed = far + mm(p_ref[hh, m], update)
        u_ref[hh, m] = update
        yield
        mixed_ref[m, :, hh * HD : (hh + 1) * HD] = mixed.astype(BF16)

    interleave([instance(hh, m) for hh in range(per) for m in range(micro)])


def back_local_kernel(dmix_ref, qk_ref, t_ref, p_ref, beta_ref, seg_ref, y_ref, b_ref, s_ref):
    per, micro = qk_ref.shape[:2]
    slot = pl.program_id(0)

    def instance(hh, m):
        live = flags(seg_ref[m])[1]
        d_out = dmix_ref[m, :, hh * HD : (hh + 1) * HD]
        part = mm(p_ref[hh, m], d_out, ta=True)
        yield
        y0 = mm(t_ref[hh, m], part, ta=True)
        yield
        y_ref[hh, m] = y0
        qk = qk_ref[hh, m]
        beta = pick(beta_ref[m], (slot * per + hh) * LANES)
        gain = mm(live * d_out, qk[:, :HD], ta=True) - mm((beta * live) * y0, qk[:, HD:], ta=True)
        b_ref[hh, m] = gain
        s_ref[hh, m] = gain.astype(BF16)

    interleave([instance(hh, m) for hh in range(per) for m in range(micro)])


def back_kernel(dmix_ref, y_ref, qk_ref, t_ref, u_ref, state_ref, dstate_ref, proj_ref,
                taps_ref, beta_ref, seg_ref, seg_row_ref,
                dmain_ref, tail_ref, front_ref, dbeta_ref, dtaps_ref):
    per, micro = qk_ref.shape[:2]
    tokens = qk_ref.shape[2]
    slot = pl.program_id(0)
    shared = [(flags(seg_ref[m]), masks(seg_ref[m], seg_row_ref[m, 0:1])) for m in range(micro)]
    lane = lax.broadcasted_iota(jnp.int32, (tokens, HD), 1)
    tap_totals = {}

    @pl.when(slot == 0)
    def _():
        dbeta_ref[...] = jnp.zeros_like(dbeta_ref)

    def instance(hh, m):
        (keeps, live, last), (strict, within) = shared[m]
        taps = taps_ref[hh]
        head = (slot * per + hh) * LANES
        proj = proj_ref[hh, m]
        beta = pick(beta_ref[m], head)
        q_low, k_low = qk_ref[hh, m][:, :HD], qk_ref[hh, m][:, HD:]
        state = state_ref[hh, m]
        dstate = dstate_ref[hh, m]
        update = u_ref[hh, m]
        d_out = dmix_ref[m, :, hh * HD : (hh + 1) * HD].astype(BF16)
        ahead = last * mm(k_low, dstate, tb=True)
        yield
        d_right = y_ref[hh, m] + mm(t_ref[hh, m], ahead, ta=True)
        d_right_low = d_right.astype(BF16)
        yield
        d_scores = (mm(d_out, update, tb=True) * within).astype(BF16)
        yield
        grad_sys = -mm(d_right_low, update, tb=True) * strict
        keys_keys = mm(k_low, k_low, tb=True)
        d_kk = (beta * grad_sys).astype(BF16)
        d_beta = jnp.sum(grad_sys * keys_keys, axis=-1, keepdims=True)
        yield
        carried = mm(k_low, state, tb=True)
        d_carried = ((-beta * live) * d_right).astype(BF16)
        d_query = live * mm(d_out, state) + mm(d_scores, k_low)
        yield
        d_key = (
            mm(d_scores, q_low, ta=True)
            + last * mm(update, dstate)
            + mm(d_carried, state)
            + mm(d_kk, k_low)
            + mm(d_kk, k_low, ta=True)
        )
        yield
        convs = [
            short_conv(proj[:, j * HD : (j + 1) * HD], taps[4 * j : 4 * j + 4], keeps)
            for j in range(3)
        ]
        query, q_scale, q_sig = silu_unit(convs[0])
        key, k_scale, k_sig = silu_unit(convs[1])
        v_sig = jax.nn.sigmoid(convs[2])
        value = convs[2] * v_sig
        d_beta = d_beta + jnp.sum(d_right * (value - live * carried), axis=-1, keepdims=True)
        dbeta_ref[m] += jnp.where(lane == head, d_beta * beta * (1.0 - beta), 0.0)
        d_value = beta * d_right
        d_convs = [
            silu_unit_back(d_query, convs[0], query, q_scale, q_sig),
            silu_unit_back(d_key, convs[1], key, k_scale, k_sig),
            d_value * v_sig * (1.0 + convs[2] * (1.0 - v_sig)),
        ]
        yield
        tap_sums = []
        for j in range(3):
            part = proj[:, j * HD : (j + 1) * HD]
            d_conv = d_convs[j]
            tap_sums.append(jnp.sum(d_conv * part[HALO:], axis=0, keepdims=True))
            zeros = jnp.zeros((HALO, HD), F32)
            d_proj = jnp.concatenate([zeros, taps[4 * j : 4 * j + 1] * d_conv], axis=0)
            for i in range(1, 4):
                kept = keeps[i - 1] * d_conv
                tap_sums.append(
                    jnp.sum(kept * pltpu.roll(part, i, 0)[HALO:], axis=0, keepdims=True)
                )
                spread = jnp.concatenate([zeros, taps[4 * j + i : 4 * j + i + 1] * kept], axis=0)
                d_proj = d_proj + pltpu.roll(spread, HALO + tokens - i, 0)
            at = (3 * hh + j) * HD
            front_ref[m, :, at : at + HD] = d_proj[:HALO]
            tail_ref[m, :, at : at + HD] = d_proj[tokens:]
            dmain_ref[m, :, at : at + HD] = d_proj[HALO:].astype(BF16)
            yield
        tap_totals[hh, m] = jnp.concatenate(tap_sums + [jnp.zeros((4, HD), F32)], axis=0)

    interleave([instance(hh, m) for hh in range(per) for m in range(micro)])
    for hh in range(per):
        dtaps_ref[hh] = sum(tap_totals[hh, m] for m in range(micro))


def flip(v):
    return v.astype(F32).T.astype(BF16)


def pack_mixer_kernel(table_ref, q_ref, k_ref, v_ref, beta_ref, conv_ref, out_ref):
    piece = table_ref[pl.program_id(0)]
    rows, n = q_ref.shape
    per = n // HD
    parts = []
    for hh in range(per):
        parts += [r[:, hh * HD : (hh + 1) * HD] for r in (q_ref, k_ref, v_ref)]
    out_ref[0, :rows] = jnp.concatenate(parts, axis=1)
    conv = conv_ref[...].astype(F32)
    lines = [beta_ref[hh : hh + 1].astype(F32) for hh in range(per)]
    for j in range(conv.shape[0]):
        line = jnp.zeros((1, HD), F32)
        for p in range(PIECES):
            own = conv[j, p // per : p // per + 1, p % per * HD : (p % per + 1) * HD]
            line = line + jnp.where(piece == p, own, 0.0)
        lines.append(line)
    lines.append(jnp.zeros((1, 3 * n - HD * len(lines)), F32))
    line = jnp.concatenate(lines, axis=1)
    row = lax.broadcasted_iota(jnp.int32, (EXTRA, 3 * n), 0)
    out_ref[0, rows:] = jnp.where(row == 0, line, 0.0).astype(BF16)


def pack_ffn_kernel(table_ref, gate_ref, up_ref, down_ref, out_w_ref, out_ref):
    hidden, rows = gate_ref.shape
    main = hidden // HD * HD
    out_ref[0, :, :main] = flip(gate_ref[:main])
    out_ref[0, :, main : 2 * main] = flip(up_ref[:main])
    rest = jnp.concatenate([gate_ref[main:], up_ref[main:]], axis=0)
    out_ref[0, :, 2 * main : 2 * hidden] = flip(rest)
    wide = main + HD
    down = jnp.concatenate([down_ref[...].astype(F32), jnp.zeros((wide - hidden, rows), F32)], axis=0)
    out_ref[0, :, 2 * hidden : 2 * hidden + wide] = down.T.astype(BF16)
    out_ref[0, :, 2 * hidden + wide :] = flip(out_w_ref[...])


def flip_pieces(table_ref, src_ref, dst_ref):
    rows = src_ref.shape[1] // PIECES
    for pos in range(PIECES):
        start = pl.multiple_of(table_ref[pos] * rows, rows)
        dst_ref[pos * rows : (pos + 1) * rows] = flip(src_ref[:, pl.ds(start, rows)])


def ffn_kernel(hidden, ids_ref, table_ref, mixed_ref, rows_ref, dout_ref, gain_ref, own_ref, *refs):
    pieces, refs = refs[:PIECES], refs[PIECES:]
    out_ref, dmid_ref, dlow_ref, dmixed_ref, gpart_ref = refs[:5]
    (w_ref, wo_ref, x_ref, xt_ref, dt_ref, mid_ref, res_ref, dn_ref, grad_ref, sems, o_sems,
     g_sems) = refs[-12:]
    grad_refs = refs[5:-12]
    step = pl.program_id(0)
    slots = wo_ref.shape[0]
    width = rows_ref.shape[1]
    rows = width // PIECES
    main = hidden // HD * HD
    wide = main + HD
    cut = 2 * hidden + wide
    part = mixed_ref.shape[1]
    ring = w_ref.shape[0]
    order = reduce_order(slots)

    def brought(slot, target, start, size, sem):
        columns = pl.ds(start, size)
        if slot == 0:
            return [pltpu.make_async_copy(own_ref.at[:, :, columns], target, sem.at[0])]
        return [
            pltpu.make_async_copy(piece.at[slot - 1, :, columns], target.at[ids_ref[j]], sem.at[j])
            for j, piece in enumerate(pieces)
        ]

    outs = [brought(k, wo_ref.at[k], cut, part, o_sems.at[k]) for k in range(slots)]
    mains = [brought(k, w_ref.at[i % ring], 0, cut, sems.at[i % ring]) for i, k in enumerate(order)]

    def leaving(i):
        return [
            pltpu.make_async_copy(grad_ref.at[i % 2, h], grad_refs[2 * i + h], g_sems.at[i % 2, h])
            for h in range(2)
        ]

    @pl.when(step == 0)
    def _():
        for group in outs + mains[:ring]:
            for copy in group:
                copy.start()
        mid_ref[...] = rows_ref[...].astype(F32)
        dn_ref[...] = jnp.zeros_like(dn_ref)
        flip_pieces(table_ref, dout_ref, dt_ref)

    for i in range(slots):

        @pl.when(step == i)
        def _():
            for copy in outs[i]:
                copy.wait()

        @pl.when(step == slots + i)
        def _():
            for copy in mains[i]:
                copy.wait()
            if i >= 2:
                for copy in leaving(i - 2):
                    copy.wait()

    @pl.when(step < slots)
    def _():
        mid_ref[...] += mm(mixed_ref[...], wo_ref[step].reshape(width, part), tb=True)

    def norm():
        mid = mid_ref[...]
        rstd = lax.rsqrt(jnp.mean(mid * mid, axis=-1, keepdims=True) + EPS)
        return mid * rstd, rstd

    @pl.when(step == slots - 1)
    def _():
        unit, _ = norm()
        x_ref[...] = (unit * gain_ref[...]).astype(BF16)
        flip_pieces(table_ref, x_ref, xt_ref)
        res_ref[...] = mid_ref[...]

    @pl.when(step >= slots)
    def _():
        at = lax.rem(step - slots, ring)
        w_gu = w_ref[at, :, :, : 2 * hidden].reshape(width, 2 * hidden)
        w_dn = w_ref[at, :, :, 2 * hidden :].reshape(width, wide)
        both = mm(x_ref[...], w_gu)
        rest = both[:, 2 * main :]
        gate = jnp.concatenate([both[:, :main], rest], axis=1)
        up = jnp.concatenate([both[:, main : 2 * main], pltpu.roll(rest, HD // 2, 1)], axis=1)
        sig = jax.nn.sigmoid(gate)
        act = gate * sig
        hid = (act * up).astype(BF16)
        d_hid = mm(dout_ref[...], w_dn)
        d_gate = (d_hid * up * (sig * (1.0 + gate * (1.0 - sig)))).astype(BF16)
        d_up = (d_hid * act).astype(BF16)
        last = d_gate[:, main:].astype(F32) + pltpu.roll(d_up[:, main:].astype(F32), HD // 2, 1)
        d_gu = jnp.concatenate([d_gate[:, :main], d_up[:, :main], last.astype(BF16)], axis=1)
        res_ref[...] += mm(hid, w_dn, tb=True)
        dn_ref[...] += mm(d_gu, w_gu, tb=True)
        to = lax.rem(step - slots, 2)
        shape = (PIECES // 2, rows)
        for h in range(2):
            span = slice(h * width // 2, (h + 1) * width // 2)
            grad_ref[to, h, :, :, : 2 * hidden] = (
                mm(xt_ref[span], d_gu).astype(BF16).reshape(shape + (2 * hidden,))
            )
            grad_ref[to, h, :, :, 2 * hidden :] = (
                mm(dt_ref[span], hid).astype(BF16).reshape(shape + (wide,))
            )

    for i in range(slots):

        @pl.when(step == slots + i)
        def _():
            for copy in leaving(i):
                copy.start()
            if i + ring < slots:
                for copy in mains[i + ring]:
                    copy.start()

    @pl.when(step == 2 * slots - 1)
    def _():
        out_ref[...] = res_ref[...].astype(BF16)
        unit, rstd = norm()
        grad = dn_ref[...]
        gpart_ref[...] = jnp.broadcast_to(jnp.sum(grad * unit, axis=0, keepdims=True), gpart_ref.shape)
        scaled = grad * gain_ref[...]
        d_mid = dout_ref[...].astype(F32) + rstd * (
            scaled - unit * jnp.mean(scaled * unit, axis=-1, keepdims=True)
        )
        dmid_ref[...] = d_mid
        low = d_mid.astype(BF16)
        dlow_ref[...] = low
        for k in range(slots):
            dmixed_ref[:, k * part : (k + 1) * part] = mm(low, wo_ref[k].reshape(width, part))
        for i in range(max(slots - 2, 0), slots):
            for copy in leaving(i):
                copy.wait()


def grad_mixer_kernel(table_ref, x_ref, dqkv_ref, dlow_ref, mixed_ref, *refs):
    xt_ref, lt_ref, grad_ref, g_sems = refs[-4:]
    grad_refs = refs[:-4]
    step = pl.program_id(0)
    width = x_ref.shape[1]
    rows = width // PIECES
    n = dqkv_ref.shape[1]
    slots = len(grad_refs) // 2

    def leaving(i):
        return [
            pltpu.make_async_copy(grad_ref.at[i % 2, h], grad_refs[2 * i + h], g_sems.at[i % 2, h])
            for h in range(2)
        ]

    @pl.when(step == 0)
    def _():
        flip_pieces(table_ref, x_ref, xt_ref)
        flip_pieces(table_ref, dlow_ref, lt_ref)

    for i in range(2, slots):

        @pl.when(step == i)
        def _():
            for copy in leaving(i - 2):
                copy.wait()

    to = lax.rem(step, 2)
    for h in range(2):
        span = slice(h * width // 2, (h + 1) * width // 2)
        shape = (PIECES // 2, rows)
        grad_ref[to, h, :, :, :n] = mm(xt_ref[span], dqkv_ref[...]).astype(BF16).reshape(shape + (n,))
        out = mm(lt_ref[span], mixed_ref[...]).astype(BF16)
        grad_ref[to, h, :, :, n:] = out.reshape(shape + (out.shape[1],))

    for i in range(slots):

        @pl.when(step == i)
        def _():
            for copy in leaving(i):
                copy.start()
            if i == slots - 1:
                for j in range(max(slots - 2, 0), slots):
                    for copy in leaving(j):
                        copy.wait()


def bring(ids_ref, pieces, w_ref, sems):
    @pl.when(pl.program_id(0) == 0)
    def _():
        copies = [
            pltpu.make_async_copy(piece, w_ref.at[ids_ref[j]], sems.at[j])
            for j, piece in enumerate(pieces)
        ]
        for copy in copies:
            copy.start()
        for copy in copies:
            copy.wait()


def finish_ffn_kernel(hidden, ids_ref, *refs):
    gate_ref, up_ref, down_ref, w_ref, sems = refs[PIECES:]
    bring(ids_ref, refs[:PIECES], w_ref, sems)
    step = pl.program_id(0)
    main = hidden // HD * HD
    wide = main + HD
    take = lambda at, n: w_ref[step, :, at : at + n].astype(F32).T
    gate_ref[:main] = take(0, main)
    up_ref[:main] = take(main, main)
    rest = take(2 * main, HD)
    gate_ref[main:] = rest[: HD // 2]
    up_ref[main:] = rest[HD // 2 :]
    down_ref[...] = take(2 * hidden, wide)[:hidden]


def finish_mixer_kernel(ids_ref, *refs):
    outs, out_w_ref, w_ref, sems = refs[PIECES:-3], refs[-3], refs[-2], refs[-1]
    bring(ids_ref, refs[:PIECES], w_ref, sems)
    step = pl.program_id(0)
    n = outs[0].shape[1]
    for hh in range(n // HD):
        for j, out in enumerate(outs):
            at = (3 * hh + j) * HD
            out[:, hh * HD : (hh + 1) * HD] = w_ref[step, :, at : at + HD].astype(F32)
    out_w_ref[...] = w_ref[step, :, 3 * n :].astype(F32).T


def input_kernel(dqkv_ref, w_ref, db_ref, beta_w_ref, rows_ref, dmid_ref, gain_ref, out_ref, gpart_ref, acc_ref):
    step = pl.program_id(0)

    @pl.when(step == 0)
    def _():
        acc_ref[...] = mm(db_ref[...], beta_w_ref[...])

    width, n = acc_ref.shape[1], dqkv_ref.shape[1]
    weights = w_ref[0, :, : width // PIECES].reshape(width, n)
    acc_ref[...] += mm(dqkv_ref[...], weights, tb=True)

    @pl.when(step == pl.num_programs(0) - 1)
    def _():
        grad = acc_ref[...]
        rows = rows_ref[...].astype(F32)
        rstd = lax.rsqrt(jnp.mean(rows * rows, axis=-1, keepdims=True) + EPS)
        unit = rows * rstd
        gpart_ref[...] = jnp.broadcast_to(jnp.sum(grad * unit, axis=0, keepdims=True), gpart_ref.shape)
        scaled = grad * gain_ref[...]
        out_ref[...] = (
            dmid_ref[...]
            + rstd * (scaled - unit * jnp.mean(scaled * unit, axis=-1, keepdims=True))
        ).astype(BF16)


def params(mib=60):
    return pltpu.CompilerParams(
        dimension_semantics=("arbitrary",), vmem_limit_bytes=mib * MIB
    )


def cost(flops, nbytes):
    return pl.CostEstimate(flops=int(flops), bytes_accessed=int(nbytes), transcendentals=0)


ANYWHERE = pl.BlockSpec(memory_space=pl.ANY)


def whole(shape):
    return pl.BlockSpec(tuple(shape), lambda *_: (0,) * len(shape), pipeline_mode=pl.Buffered(1))


def reduce_order(slots):
    return list(range(slots - 2, 0, -1)) + [slots - 1, 0]


def lead(n, shape):
    return pl.BlockSpec((n,) + tuple(shape[1:]), lambda h, *_: (h,) + (0,) * (len(shape) - 1))


def rolled(n, shape, shift, steps):
    return pl.BlockSpec(
        (n,) + tuple(shape[1:]), lambda h, *_: ((h + shift) % steps,) + (0,) * (len(shape) - 1)
    )


def sds(shape, dtype):
    return jax.ShapeDtypeStruct(tuple(shape), dtype)


def call(kernel, grid, in_specs, out_specs, out_shape, estimate, name, scratch=(), prefetch=0):
    return pl.pallas_call(
        kernel,
        grid_spec=pltpu.PrefetchScalarGridSpec(
            num_scalar_prefetch=prefetch,
            grid=(grid,),
            in_specs=in_specs,
            out_specs=out_specs,
            scratch_shapes=list(scratch),
        ),
        out_shape=out_shape,
        compiler_params=params(),
        cost_estimate=cost(*estimate),
        name=name,
    )


def pack_mixer(table, w_query, w_key, w_value, beta_t, conv):
    width, n = w_query.shape
    rows = width // PIECES
    spec = pl.BlockSpec((rows, n), lambda i, t: (t[i], 0))
    count = table.shape[0]
    return call(
        pack_mixer_kernel, count,
        [spec] * 3 + [pl.BlockSpec((beta_t.shape[0], rows), lambda i, t: (0, t[i])), whole(conv.shape)],
        pl.BlockSpec((1, rows + EXTRA, 3 * n), lambda i, t: (i, 0, 0)),
        sds((count, rows + EXTRA, 3 * n), BF16), (0, 12 * count * rows * n), "pack_mixer", prefetch=1,
    )(table, w_query, w_key, w_value, beta_t, conv)


def pack_ffn(table, gate_t, up_t, w_down, w_out):
    hidden, width = gate_t.shape
    rows = width // PIECES
    n = 2 * hidden + hidden // HD * HD + HD + w_out.shape[0]
    count = table.shape[0]
    return call(
        pack_ffn_kernel, count,
        [pl.BlockSpec((w.shape[0], rows), lambda i, t: (0, t[i])) for w in (gate_t, up_t, w_down, w_out)],
        pl.BlockSpec((1, rows, n), lambda i, t: (i, 0, 0)),
        sds((count, rows, n), BF16), (0, 4 * count * rows * n), "pack_ffn", prefetch=1,
    )(table, gate_t, up_t, w_down, w_out)


def mixer_local(ids, x, halo, seg, seg_row, own, pieces, heads):
    micro, tokens, width = x.shape
    slots = pieces[0].shape[0] + 1
    per = heads // slots
    hm = (heads, micro)
    rows, n = own.shape[1:]
    outs = [
        sds((slots, PIECES, rows, n), BF16),
        sds((micro, tokens, HD), F32),
        sds((heads, 16, HD), F32),
        sds((slots, per * LANES, width), BF16),
        sds(hm + (HALO + tokens, 3 * HD), F32),
        sds(hm + (tokens, 2 * HD), BF16),
        sds(hm + (tokens, tokens), BF16),
        sds(hm + (tokens, tokens), BF16),
        sds(hm + (tokens, HD), F32),
        sds(hm + (tokens, HD), BF16),
        sds(hm + (HD, HD), F32),
        sds(hm + (HD, HD), F32),
        sds(hm + (HD, HD), BF16),
    ]
    return call(
        local_kernel, slots,
        [whole(x.shape), whole(halo.shape), whole(seg.shape), whole(seg_row.shape)]
        + [ANYWHERE] * (1 + PIECES),
        [whole(o.shape) for o in outs[:2]] + [lead(per, outs[2].shape), lead(1, outs[3].shape)]
        + [lead(per, o.shape) for o in outs[4:]],
        outs, (heads * micro * 1e9, heads * micro * 2e6), "mixer_local",
        [pltpu.SemaphoreType.DMA((slots, PIECES))], prefetch=1,
    )(ids, x, halo, seg, seg_row, own, *pieces)


def hop(state, keep, gain, slots, back):
    per = gain.shape[0] // slots
    shift = slots - 1 if back else 1
    return call(
        functools.partial(hop_kernel, back), slots,
        [rolled(per, state.shape, shift, slots), lead(per, keep.shape), lead(per, gain.shape)],
        lead(per, gain.shape), sds(gain.shape, BF16),
        (gain.size * 512, gain.size * 12), "hop",
    )(state, keep, gain)


def mixer_output(qk, scores, base, mix, state, seg, slots):
    heads, micro, tokens = qk.shape[:3]
    per = heads // slots
    return call(
        output_kernel, slots,
        [lead(per, a.shape) for a in (qk, scores, base, mix)]
        + [rolled(per, state.shape, 1, slots), whole(seg.shape)],
        [pl.BlockSpec((micro, tokens, per * HD), lambda h: (0, 0, h)), lead(per, base.shape)],
        [sds((micro, tokens, heads * HD), BF16), sds(base.shape, BF16)],
        (heads * micro * 5e7, heads * micro * 5e5), "mixer_output",
    )(qk, scores, base, mix, state, seg)


def mixer_back_local(d_mixed, qk, inv, scores, beta, seg, slots):
    heads, micro, tokens = qk.shape[:3]
    per = heads // slots
    outs = [sds((heads, micro, tokens, HD), F32), sds((heads, micro, HD, HD), F32)]
    outs.append(sds((heads, micro, HD, HD), BF16))
    return call(
        back_local_kernel, slots,
        [pl.BlockSpec((micro, tokens, per * HD), lambda h: (0, 0, h))]
        + [lead(per, a.shape) for a in (qk, inv, scores)]
        + [whole(beta.shape), whole(seg.shape)],
        [lead(per, o.shape) for o in outs], outs,
        (heads * micro * 5e7, heads * micro * 5e5), "mixer_back_local",
    )(d_mixed, qk, inv, scores, beta, seg)


def mixer_back(d_mixed, y0, qk, inv, update, state, d_state, proj, taps, beta, seg, seg_row, slots):
    heads, micro, tokens = qk.shape[:3]
    per = heads // slots
    columns = lambda rows, n: pl.BlockSpec((micro, rows, per * n), lambda h: (0, 0, h))
    return call(
        back_kernel, slots,
        [columns(tokens, HD)]
        + [lead(per, a.shape) for a in (y0, qk, inv, update)]
        + [rolled(per, state.shape, 1, slots), rolled(per, d_state.shape, slots - 1, slots)]
        + [lead(per, proj.shape), lead(per, taps.shape)]
        + [whole(a.shape) for a in (beta, seg, seg_row)],
        [columns(tokens, 3 * HD), columns(HALO, 3 * HD), columns(HALO, 3 * HD), whole(beta.shape),
         lead(per, taps.shape)],
        [
            sds((micro, tokens, heads * 3 * HD), BF16),
            sds((micro, HALO, heads * 3 * HD), F32),
            sds((micro, HALO, heads * 3 * HD), F32),
            sds(beta.shape, F32),
            sds(taps.shape, F32),
        ],
        (heads * micro * 5e8, heads * micro * 2e6), "mixer_back",
    )(d_mixed, y0, qk, inv, update, state, d_state, proj, taps, beta, seg, seg_row)


def grads_out(slots, rows, n):
    shape = (PIECES // 2, rows, n)
    return (
        [sds(shape, BF16)] * (2 * slots),
        [pltpu.VMEM((2, 2) + shape, BF16)],
        pltpu.SemaphoreType.DMA((2, 2)),
    )


def ffn(ids, table, mixed, rows, d_out, gain, own, pieces, hidden):
    count, width = rows.shape
    slots = pieces[0].shape[0] + 1
    wide = hidden // HD * HD + HD
    part = mixed.shape[1] // slots
    piece = width // PIECES
    full = whole((count, width))
    grads, room, g_sems = grads_out(slots, piece, 2 * hidden + wide)
    outs = [
        sds((count, width), BF16), sds((count, width), F32), sds((count, width), BF16),
        sds((count, mixed.shape[1]), F32), sds((8, width), F32),
    ]
    ring = 2
    return call(
        functools.partial(ffn_kernel, hidden), 2 * slots,
        [pl.BlockSpec((count, part), lambda s, *_: (0, jnp.minimum(s, slots - 1))),
         full, full, whole(gain.shape)] + [ANYWHERE] * (1 + PIECES),
        [full, full, full, whole((count, mixed.shape[1])), whole((8, width))] + [ANYWHERE] * len(grads),
        outs + grads, (26 * count * width * hidden * slots, 6e7), "ffn",
        [
            pltpu.VMEM((ring, PIECES, piece, 2 * hidden + wide), BF16),
            pltpu.VMEM((slots, PIECES, piece, part), BF16),
            pltpu.VMEM((count, width), BF16),
            pltpu.VMEM((width, count), BF16),
            pltpu.VMEM((width, count), BF16),
            pltpu.VMEM((count, width), F32),
            pltpu.VMEM((count, width), F32),
            pltpu.VMEM((count, width), F32),
        ]
        + room
        + [
            pltpu.SemaphoreType.DMA((ring, PIECES)),
            pltpu.SemaphoreType.DMA((slots, PIECES)),
            g_sems,
        ],
        prefetch=2,
    )(ids, table, mixed, rows, d_out, gain, own, *pieces)


def grad_mixer(table, x, d_qkv, d_low, mixed, slots):
    count, width = x.shape
    n, part = d_qkv.shape[1] // slots, mixed.shape[1] // slots
    grads, room, g_sems = grads_out(slots, width // PIECES, n + part)
    order = reduce_order(slots)

    def at(s):
        return sum(jnp.where(s == i, k, 0) for i, k in enumerate(order))

    columns = lambda size: pl.BlockSpec((count, size), lambda s, t: (0, at(s)))
    return call(
        grad_mixer_kernel, slots,
        [whole(x.shape), columns(n), whole(d_low.shape), columns(part)],
        [ANYWHERE] * len(grads), grads,
        (2 * width * count * (n + part) * slots, 2 * width * (n + part) * slots), "grad_mixer",
        [pltpu.VMEM((width, count), BF16)] * 2 + room + [g_sems], prefetch=1,
    )(table, x, d_qkv, d_low, mixed)


def finish_ffn(ids, pieces, hidden):
    rows, n = pieces[0].shape
    width = rows * PIECES
    return call(
        functools.partial(finish_ffn_kernel, hidden), PIECES, [ANYWHERE] * PIECES,
        [pl.BlockSpec((hidden, rows), lambda i, t: (0, i))] * 3,
        [sds((hidden, width), F32)] * 3,
        (0, 6 * n * width), "finish_ffn",
        [pltpu.VMEM((PIECES, rows, n), BF16), pltpu.SemaphoreType.DMA((PIECES,))], prefetch=1,
    )(ids, *pieces)


def finish_mixer(ids, pieces, n):
    rows, total = pieces[0].shape
    width = rows * PIECES
    part = total - 3 * n
    return call(
        finish_mixer_kernel, PIECES, [ANYWHERE] * PIECES,
        [pl.BlockSpec((rows, n), lambda i, t: (i, 0))] * 3 + [pl.BlockSpec((part, rows), lambda i, t: (0, i))],
        [sds((width, n), F32)] * 3 + [sds((part, width), F32)],
        (0, 6 * total * width), "finish_mixer",
        [pltpu.VMEM((PIECES, rows, total), BF16), pltpu.SemaphoreType.DMA((PIECES,))], prefetch=1,
    )(ids, *pieces)


def input_back(d_qkv, w, d_b, beta_w, rows, d_mid, gain):
    count, width = rows.shape
    slots, n = w.shape[0], w.shape[3]
    full = whole((count, width))
    return call(
        input_kernel, slots,
        [pl.BlockSpec((count, n), lambda s: (0, s)), lead(1, w.shape),
         whole(d_b.shape), whole(beta_w.shape), full, full, whole(gain.shape)],
        [full, whole((8, width))],
        [sds((count, width), BF16), sds((8, width), F32)],
        (2 * count * width * n * slots, 2 * slots * width * n), "input_back",
        [pltpu.VMEM((count, width), F32)],
    )(d_qkv, w, d_b, beta_w, rows, d_mid, gain)


def swap(x, mask_of, size):
    return lax.ppermute(x, "dp", [(i, i ^ mask_of(i)) for i in range(size)])


def first(i):
    return 4 if i & 1 else 2


def second(i):
    return 2 if i & 1 else 4


def across(i):
    return 1


def from_ahead(x, k, size):
    return lax.ppermute(x, "tensor", [(i, (i - k) % size) for i in range(size)])


def to_ahead(x, k, size):
    return lax.ppermute(x, "tensor", [(i, (i + k) % size) for i in range(size)])


def plane_gather(own, dp):
    b = swap(own, first, dp)
    c = swap(own, second, dp)
    d = swap(b, second, dp)
    near = [own, b, c, d]
    return near + [swap(piece, across, dp) for piece in near]


def piece_ids(own):
    core = own & 1
    f = jnp.where(core == 1, 4, 2)
    s = jnp.where(core == 1, 2, 4)
    return jnp.stack([own, own ^ f, own ^ s, own ^ 6, own ^ 1, own ^ 1 ^ s, own ^ 1 ^ f, own ^ 7])


def sync(*xs):
    return lax.optimization_barrier(xs)


def add(a, b):
    return (a.astype(F32) + b.astype(F32)).astype(BF16)


class Reduction:
    def __init__(self, grads, order, dp, tensor):
        self.order, self.dp, self.tensor = order, dp, tensor
        self.theirs, self.ours = list(grads[0::2]), list(grads[1::2])
        self.across_in = [swap(g, across, dp) for g in self.theirs]
        self.first_in, self.second_in, self.parts = {}, {}, {}
        self.last = None

    def tie(self, *xs):
        if self.last is None:
            self.last = self.ours[0]
            *xs, self.ours[0] = sync(*xs, self.last)
            return xs
        *xs, self.last = sync(*xs, self.last)
        return xs

    def add(self, kept, came):
        if self.last is not None:
            kept, came, _ = sync(kept, came, self.last)
        self.last = add(kept, came)
        return self.last

    def across(self, i):
        total = self.add(self.ours[i], self.across_in[i])
        self.first_in[i] = (total[:2], swap(total[2:], first, self.dp))

    def first(self, i):
        total = self.add(*self.first_in[i])
        self.second_in[i] = (total[0], swap(total[1], second, self.dp))

    def second(self, i):
        slot = self.order[i]
        total = self.add(*self.second_in[i])
        if slot and slot < self.tensor - 1:
            if slot + 1 < self.tensor - 1:
                total = self.add(total, self.parts[slot + 1])
            self.parts[slot] = to_ahead(total, 1, self.tensor)
        else:
            self.parts[slot] = to_ahead(total, slot, self.tensor) if slot else total

    def result(self):
        parts = [self.parts[0]] + [self.parts[k] for k in {1, self.tensor - 1}]
        self.last = sum(p.astype(F32) for p in parts).astype(BF16)
        return self.last


def reduce_far(total, dp):
    mask = PIECES
    while mask < dp:
        total = add(total, swap(total, lambda i: mask, dp))
        mask *= 2
    return total


def norm_rows(rows, gain):
    rstd = lax.rsqrt(jnp.mean(rows * rows, axis=-1, keepdims=True) + EPS)
    return rows * rstd * gain


def project_t(left, right):
    return jnp.einsum("th,td->hd", left, right, preferred_element_type=F32)


def shards(dp, tensor, layer_input, segment, d_out, norm1_gain, w_query, w_key, w_value, w_beta,
           conv_weight, w_out, norm2_gain, w_gate, w_up, w_down):
    micro, _, tokens, width = layer_input.shape
    count = micro * tokens
    local_heads = w_query.shape[1] // HD
    heads = local_heads * tensor
    hidden = w_gate.shape[1]
    own = lax.axis_index("dp") % PIECES
    place = lax.axis_index("tensor")
    ids = piece_ids(own)
    gain1 = norm1_gain.astype(F32)[None]
    gain2 = norm2_gain.astype(F32)[None]
    mine = own[None].astype(jnp.int32)
    every = jnp.arange(PIECES, dtype=jnp.int32)

    pack = (w_query, w_key, w_value, w_beta.T, conv_weight)
    pack_f = (w_gate.T, w_up.T, w_down, w_out)
    piece = pack_mixer(mine, *pack)[0]
    others = [from_ahead(piece, k, tensor) for k in range(1, tensor)]
    rows = layer_input.reshape(count, width)
    _, rows, mine, every = sync(piece, rows, mine, every)
    normed1 = norm_rows(rows.astype(F32), gain1).astype(BF16)
    mixer_in = normed1.reshape(micro, tokens, width)
    ahead = [(i, i + 1) for i in range(tensor - 1)]
    behind = [(i + 1, i) for i in range(tensor - 1)]
    halo = lax.ppermute(mixer_in[:, tokens - HALO :], "tensor", ahead)
    mixer_own = pack_mixer(every, *pack)
    piece = pack_ffn(mine, *pack_f)[0]

    *others, halo, mixer_own, piece, every = sync(*others, halo, mixer_own, piece, every)
    mixer_others = jnp.stack(others)
    b, c = swap(mixer_others, first, dp), swap(mixer_others, second, dp)
    ffn_others = {k: from_ahead(piece, k, tensor) for k in (1, tensor - 1)}
    ffn_own = pack_ffn(every, *pack_f)
    mixer_others, b, c, ffn_own = sync(mixer_others, b, c, ffn_own)
    d = swap(b, second, dp)
    mixer_pieces = [mixer_others, b, c] + [swap(x, across, dp) for x in (mixer_others, b, c)]
    d, *mixer_pieces = sync(d, *mixer_pieces)
    mixer_pieces = mixer_pieces[:3] + [d] + mixer_pieces[3:] + [swap(d, across, dp)]
    ffn_others[1], *mixer_pieces = sync(ffn_others[1], *mixer_pieces)
    for k in range(2, tensor - 1):
        ffn_others[k] = from_ahead(ffn_others[k - 1], 1, tensor)

    seg = jnp.pad(segment[:, 0].astype(F32), ((0, 0), (HALO, 0)), constant_values=-1)
    seg = lax.dynamic_slice_in_dim(seg, place * tokens, HALO + tokens, 1)
    seg_row = jnp.broadcast_to(seg[:, None, HALO:], (micro, 8, tokens))
    seg = seg[..., None]

    part = local_heads * HD
    (mixer_w, beta, taps, beta_w, proj, qk, inv, scores, base, mix, keep, gain, state) = mixer_local(
        ids, mixer_in, halo, seg, seg_row, mixer_own, mixer_pieces, heads
    )
    state, *others = sync(state, *(ffn_others[k] for k in range(1, tensor)))
    near = [jnp.stack(others)]
    near += [swap(near[0], first, dp), swap(near[0], second, dp)]
    state = hop(lax.ppermute(state, "tensor", ahead), keep, gain, tensor, False)
    state, *near = sync(state, *near)
    near.append(swap(near[1], second, dp))
    far = [swap(piece, across, dp) for piece in near[:3]]
    for step in range(1, tensor - 1):
        state = lax.ppermute(state, "tensor", ahead)
        if step < tensor - 2:
            state = hop(state, keep, gain, tensor, False)
    state, near[3] = sync(state, near[3])
    far.append(swap(near[3], across, dp))
    mixed, update = mixer_output(qk, scores, base, mix, state, seg, tensor)
    mixed = mixed.reshape(count, heads * HD)

    out_grad = d_out.reshape(count, width)
    table = jnp.stack([ids[i] for i in (4, 6, 5, 7, 0, 2, 1, 3)])
    output, d_mid, d_mid_low, d_mixed, gain2_part, *grads = ffn(
        ids, table, mixed, rows, out_grad, gain2, ffn_own, near + far, hidden
    )
    order = reduce_order(tensor)
    red = Reduction(grads, order, dp, tensor)

    d_mixed = d_mixed.reshape(micro, tokens, heads * HD)
    y0, back_gain, d_state = mixer_back_local(d_mixed, qk, inv, scores, beta, seg, tensor)
    (d_state,) = red.tie(d_state)
    recv = lax.ppermute(d_state, "tensor", behind)
    red.across(0)
    red.across(1)
    (recv,) = red.tie(recv)
    recv = lax.ppermute(hop(recv, keep, back_gain, tensor, True), "tensor", behind)
    red.across(2)
    red.first(0)
    red.across(3)
    (recv,) = red.tie(recv)
    recv = lax.ppermute(hop(recv, keep, back_gain, tensor, True), "tensor", behind)
    red.first(1)
    red.second(0)
    red.first(2)
    (recv,) = red.tie(recv)
    d_qkv, tail, front, d_beta, d_taps = mixer_back(
        d_mixed, y0, qk, inv, update, state, recv, proj, taps, beta, seg, seg_row, tensor
    )
    front, d_beta = red.tie(front, d_beta)
    front = lax.ppermute(front, "tensor", behind)
    red.second(1)
    red.first(3)
    red.second(2)
    (front,) = red.tie(front)
    front = jnp.roll(front, 3 * part, axis=2)
    d_qkv = lax.dynamic_update_slice(d_qkv, (tail + front).astype(BF16), (0, tokens - HALO, 0))
    d_qkv = d_qkv.reshape(count, heads * 3 * HD)
    d_b = d_beta.reshape(count, HD).astype(BF16)
    grads = grad_mixer(table, normed1, d_qkv, d_mid_low, mixed, tensor)
    mix_red = Reduction(grads, order, dp, tensor)
    mix_red.ours[0], d_qkv = sync(mix_red.ours[0], d_qkv)
    input_grad, gain1_part = input_back(
        d_qkv, mixer_w, d_b, beta_w.reshape(-1, width), rows, d_mid, gain1
    )
    (gain1_part,) = red.tie(gain1_part)
    red.second(3)
    total = reduce_far(red.result(), dp)
    total, gain1_part = sync(total, gain1_part)
    near = [total, swap(total, first, dp), swap(total, second, dp)]
    (gain1_part,) = mix_red.tie(gain1_part)
    mix_red.across(0)
    mix_red.across(1)
    mix_red.across(2)
    mix_red.across(3)
    *near, mix_red.last = sync(*near, mix_red.last)
    near.append(swap(near[1], second, dp))
    far = [swap(piece, across, dp) for piece in near[:3]]
    mix_red.first(0)
    mix_red.first(1)
    mix_red.first(2)
    mix_red.first(3)
    near[3], mix_red.last = sync(near[3], mix_red.last)
    far.append(swap(near[3], across, dp))
    mix_red.second(0)
    mix_red.second(1)
    mix_red.second(2)
    mix_red.second(3)
    *pieces, mix_red.last = sync(*near, *far, mix_red.last)
    grad_gate, grad_up, grad_down = finish_ffn(ids, pieces, hidden)
    total = reduce_far(mix_red.result(), dp)
    grad_q, grad_k, grad_v, grad_out = finish_mixer(ids, plane_gather(total, dp), part)

    grad_b = project_t(d_b, normed1)[::LANES]
    span = width // tensor
    d_taps = d_taps[:, :12].reshape(tensor, local_heads, 12, HD)
    d_taps = jnp.swapaxes(d_taps, 1, 2).reshape(tensor, -1)
    packed = []
    for k in range(tensor):
        at = ((place + k) % tensor) * span
        packed.append(
            jnp.concatenate(
                [
                    grad_b[k * local_heads : (k + 1) * local_heads].reshape(-1),
                    d_taps[k],
                    lax.dynamic_slice_in_dim(gain1_part[0], at, span),
                    lax.dynamic_slice_in_dim(gain2_part[0], at, span),
                ]
            )
        )
    packed = sum([packed[0]] + [to_ahead(packed[k], k, tensor) for k in range(1, tensor)])
    mask = 1
    while mask < dp:
        packed = packed + swap(packed, lambda i: mask, dp)
        mask *= 2
    cut = local_heads * width
    grad_beta = packed[:cut].reshape(local_heads, width).T
    grad_conv = packed[cut : cut + 12 * span].reshape(3, 4, span)
    cut += 12 * span
    grad_gain1 = packed[cut : cut + span]
    grad_gain2 = packed[cut + span : cut + 2 * span]
    return (
        output.reshape(micro, 1, tokens, width),
        input_grad.reshape(micro, 1, tokens, width),
        grad_gain1,
        grad_q,
        grad_k,
        grad_v,
        grad_beta,
        grad_conv,
        grad_out,
        grad_gain2,
        grad_gate.T,
        grad_up.T,
        grad_down,
    )


def solution(mesh):
    in_specs = (
        P(None, "dp", "tensor", None),
        P(None, "dp", None),
        P(None, "dp", "tensor", None),
        P(),
        P(None, "tensor"),
        P(None, "tensor"),
        P(None, "tensor"),
        P(None, "tensor"),
        P(None, None, "tensor"),
        P("tensor", None),
        P(),
        P(None, "tensor"),
        P(None, "tensor"),
        P("tensor", None),
    )
    out_specs = (
        P(None, "dp", "tensor", None),
        P(None, "dp", "tensor", None),
        P("tensor"),
        P(None, "tensor"),
        P(None, "tensor"),
        P(None, "tensor"),
        P(None, "tensor"),
        P(None, None, "tensor"),
        P("tensor", None),
        P("tensor"),
        P(None, "tensor"),
        P(None, "tensor"),
        P("tensor", None),
    )
    body = functools.partial(shards, mesh.shape["dp"], mesh.shape["tensor"])
    return jax.shard_map(body, mesh=mesh, in_specs=in_specs, out_specs=out_specs, check_vma=False)
```

```python
import functools

import jax
import jax.numpy as jnp
from jax import lax
from jax.experimental import pallas as pl
from jax.experimental.pallas import tpu as pltpu
from jax.sharding import PartitionSpec as P

HD = 128
HALO = 16
EXTRA = 16
LANES = 16
PIECES = 8
EPS = 1e-06
F32 = jnp.float32
BF16 = jnp.bfloat16
MIB = 1 << 20


def mm(a, b, ta=False, tb=False):
    dims = (((0 if ta else 1,), (1 if tb else 0,)), ((), ()))
    return lax.dot_general(a.astype(BF16), b.astype(BF16), dims, preferred_element_type=F32)


def interleave(makers):
    running = list(makers)
    while running:
        still = []
        for g in running:
            try:
                next(g)
                still.append(g)
            except StopIteration:
                pass
        running = still


def invert_unit(lows):
    size = lows[0].shape[0]
    row = lax.broadcasted_iota(jnp.int32, (size, size), 0)
    col = lax.broadcasted_iota(jnp.int32, (size, size), 1)
    eye = (row == col).astype(F32)
    invs = [eye - jnp.where((row >> 1) == (col >> 1), low, 0.0) for low in lows]
    step = 1
    while (2 << step) <= size:
        pair = ((row >> (step + 1)) == (col >> (step + 1))) & ((row >> step) != (col >> step))
        lefts = [mm(inv, jnp.where(pair, low, 0.0)) for inv, low in zip(invs, lows)]
        yield
        invs = [inv - mm(left, inv) for inv, left in zip(invs, lefts)]
        yield
        step += 1
    return invs


def short_conv(proj, taps, keeps):
    total = taps[0:1] * proj[HALO:]
    for i in range(1, 4):
        total = total + taps[i : i + 1] * (pltpu.roll(proj, i, 0)[HALO:] * keeps[i - 1])
    return total


def silu_unit(conv):
    sig = jax.nn.sigmoid(conv)
    act = conv * sig
    scale = lax.rsqrt(jnp.sum(act * act, axis=-1, keepdims=True) + EPS)
    return act * scale, scale, sig


def silu_unit_back(grad, conv, unit, scale, sig):
    d_act = scale * (grad - unit * jnp.sum(grad * unit, axis=-1, keepdims=True))
    return d_act * sig * (1.0 + conv * (1.0 - sig))


def flags(seg):
    own = seg[HALO:]
    equal = lambda a: jnp.where(own == a, 1.0, 0.0)
    keeps = [equal(pltpu.roll(jnp.broadcast_to(seg, (seg.shape[0], HD)), i, 0)[HALO:, 0:1]) for i in (1, 2, 3)]
    return keeps, equal(seg[HALO - 1 : HALO]), equal(seg[-1:])


def masks(seg, seg_row):
    n = seg_row.shape[1]
    row = lax.broadcasted_iota(jnp.int32, (n, n), 0)
    col = lax.broadcasted_iota(jnp.int32, (n, n), 1)
    same = seg[HALO:] == seg_row
    strict = jnp.where(same & (row > col), 1.0, 0.0)
    within = jnp.where(same & (row >= col), 1.0, 0.0)
    return strict, within


def pick(values, head):
    lane = lax.broadcasted_iota(jnp.int32, values.shape, 1)
    return jnp.sum(jnp.where(lane == head, values, 0.0), axis=-1, keepdims=True)


def piece_copies(ids_ref, own_ref, piece_refs, w_ref, sems):
    slots = [[pltpu.make_async_copy(own_ref, w_ref.at[0], sems.at[0, 0])]]
    for slot in range(1, w_ref.shape[0]):
        slots.append(
            [
                pltpu.make_async_copy(
                    piece.at[slot - 1], w_ref.at[slot, ids_ref[j]], sems.at[slot, j]
                )
                for j, piece in enumerate(piece_refs)
            ]
        )
    return slots


def local_kernel(ids_ref, x_ref, halo_ref, seg_ref, seg_row_ref, own_ref, *refs):
    pieces = refs[:PIECES]
    (w_ref, beta_ref, taps_ref, beta_w_ref, proj_ref, qk_ref, t_ref, p_ref, ub_ref, w_out_ref, m_ref,
     a_ref, s_ref, sems) = refs[PIECES:]
    slot = pl.program_id(0)
    per = taps_ref.shape[0]
    micro, tokens, width = x_ref.shape
    half = tokens // 2
    rows = width // PIECES
    copies = piece_copies(ids_ref, own_ref, pieces, w_ref, sems)

    @pl.when(slot == 0)
    def _():
        for group in copies:
            for copy in group:
                copy.start()
        beta_ref[...] = jnp.zeros_like(beta_ref)

    for k, group in enumerate(copies):

        @pl.when(slot == k)
        def _():
            for copy in group:
                copy.wait()

    def extra(piece, j):
        return w_ref[slot, piece, rows:, j * HD : (j + 1) * HD]

    beta_w = jnp.concatenate(
        [jnp.concatenate([extra(p, hh) for p in range(PIECES)], axis=1) for hh in range(per)], axis=0
    )
    beta_w_ref[0] = beta_w
    for hh in range(per):
        lines = [extra(per * (r % 4) + hh, per + r // 4)[0:1].astype(F32) for r in range(12)]
        taps_ref[hh] = jnp.concatenate(lines + [jnp.zeros((4, HD), F32)], axis=0)
    lane = lax.broadcasted_iota(jnp.int32, (tokens, HD), 1)

    weights = w_ref[slot, :, :rows].reshape(width, per * 3 * HD)
    shared = []
    for m in range(micro):
        x_ext = jnp.concatenate([halo_ref[m], x_ref[m]], axis=0)
        proj = jnp.dot(x_ext, weights, preferred_element_type=F32)
        seg = seg_ref[m]
        betas = jax.nn.sigmoid(mm(x_ref[m], beta_w, tb=True))
        shared.append((proj, betas, flags(seg), masks(seg, seg_row_ref[m, 0:1])))

    def instance(hh, m):
        proj, betas, (keeps, live, last), (strict, within) = shared[m]
        proj = proj[:, hh * 3 * HD : (hh + 1) * 3 * HD]
        taps = taps_ref[hh]
        proj_ref[hh, m] = proj
        convs = [
            short_conv(proj[:, j * HD : (j + 1) * HD], taps[4 * j : 4 * j + 4], keeps)
            for j in range(3)
        ]
        query = silu_unit(convs[0])[0]
        key = silu_unit(convs[1])[0]
        value = convs[2] * jax.nn.sigmoid(convs[2])
        beta = betas[:, hh * LANES : hh * LANES + 1]
        beta_ref[m] += jnp.where(lane == (slot * per + hh) * LANES, beta, 0.0)
        qk_ref[hh, m] = jnp.concatenate([query, key], axis=1).astype(BF16)
        yield
        low = beta * mm(key, key, tb=True) * strict
        scores = mm(query, key, tb=True) * within
        p_ref[hh, m] = scores.astype(BF16)
        yield
        top, bottom = yield from invert_unit([low[:half, :half], low[half:, half:]])
        cross = mm(bottom, low[half:, :half])
        yield
        cross = -mm(cross, top)
        yield
        inv = jnp.concatenate(
            [
                jnp.concatenate([top, jnp.zeros_like(top)], axis=1),
                jnp.concatenate([cross, bottom], axis=1),
            ],
            axis=0,
        ).astype(BF16)
        t_ref[hh, m] = inv
        both = mm(inv, jnp.concatenate([beta * value, (beta * live) * key], axis=1))
        yield
        late = (last * key).astype(BF16)
        sums = mm(both, late, ta=True)
        row = lax.broadcasted_iota(jnp.int32, (HD, HD), 0)
        col = lax.broadcasted_iota(jnp.int32, (HD, HD), 1)
        keep_state = jnp.where(row == col, live[tokens - 1 : tokens], 0.0)
        ub_ref[hh, m] = both[:, :HD]
        w_out_ref[hh, m] = both[:, HD:].astype(BF16)
        a_ref[hh, m] = sums[:HD]
        s_ref[hh, m] = sums[:HD].astype(BF16)
        m_ref[hh, m] = (keep_state - sums[HD:]).astype(BF16)

    interleave([instance(hh, m) for hh in range(per) for m in range(micro)])


def hop_kernel(back, state_ref, keep_ref, gain_ref, out_ref):
    for h in range(gain_ref.shape[0]):
        for m in range(gain_ref.shape[1]):
            moved = mm(state_ref[h, m], keep_ref[h, m], tb=back)
            out_ref[h, m] = (moved + gain_ref[h, m]).astype(BF16)


def output_kernel(qk_ref, p_ref, ub_ref, w_ref, state_ref, seg_ref, mixed_ref, u_ref):
    per, micro = ub_ref.shape[:2]

    def instance(hh, m):
        live = flags(seg_ref[m])[1]
        state = state_ref[hh, m]
        update = ub_ref[hh, m] - mm(w_ref[hh, m], state, tb=True)
        update = update.astype(BF16)
        far = live * mm(qk_ref[hh, m][:, :HD], state, tb=True)
        yield
        mixed = far + mm(p_ref[hh, m], update)
        u_ref[hh, m] = update
        yield
        mixed_ref[m, :, hh * HD : (hh + 1) * HD] = mixed.astype(BF16)

    interleave([instance(hh, m) for hh in range(per) for m in range(micro)])


def back_local_kernel(dmix_ref, qk_ref, t_ref, p_ref, beta_ref, seg_ref, y_ref, b_ref, s_ref):
    per, micro = qk_ref.shape[:2]
    slot = pl.program_id(0)

    def instance(hh, m):
        live = flags(seg_ref[m])[1]
        d_out = dmix_ref[m, :, hh * HD : (hh + 1) * HD]
        part = mm(p_ref[hh, m], d_out, ta=True)
        yield
        y0 = mm(t_ref[hh, m], part, ta=True)
        yield
        y_ref[hh, m] = y0
        qk = qk_ref[hh, m]
        beta = pick(beta_ref[m], (slot * per + hh) * LANES)
        gain = mm(live * d_out, qk[:, :HD], ta=True) - mm((beta * live) * y0, qk[:, HD:], ta=True)
        b_ref[hh, m] = gain
        s_ref[hh, m] = gain.astype(BF16)

    interleave([instance(hh, m) for hh in range(per) for m in range(micro)])


def back_kernel(dmix_ref, y_ref, qk_ref, t_ref, u_ref, state_ref, dstate_ref, proj_ref,
                taps_ref, beta_ref, seg_ref, seg_row_ref,
                dmain_ref, dbeta_ref, dtaps_ref):
    per, micro = qk_ref.shape[:2]
    tokens = qk_ref.shape[2]
    slot = pl.program_id(0)
    shared = [(flags(seg_ref[m]), masks(seg_ref[m], seg_row_ref[m, 0:1])) for m in range(micro)]
    lane = lax.broadcasted_iota(jnp.int32, (tokens, HD), 1)
    tap_totals = {}

    @pl.when(slot == 0)
    def _():
        dbeta_ref[...] = jnp.zeros_like(dbeta_ref)

    def instance(hh, m):
        (keeps, live, last), (strict, within) = shared[m]
        taps = taps_ref[hh]
        head = (slot * per + hh) * LANES
        proj = proj_ref[hh, m]
        beta = pick(beta_ref[m], head)
        q_low, k_low = qk_ref[hh, m][:, :HD], qk_ref[hh, m][:, HD:]
        state = state_ref[hh, m]
        dstate = dstate_ref[hh, m]
        update = u_ref[hh, m]
        d_out = dmix_ref[m, :, hh * HD : (hh + 1) * HD].astype(BF16)
        ahead = last * mm(k_low, dstate, tb=True)
        yield
        d_right = y_ref[hh, m] + mm(t_ref[hh, m], ahead, ta=True)
        d_right_low = d_right.astype(BF16)
        yield
        d_scores = (mm(d_out, update, tb=True) * within).astype(BF16)
        yield
        grad_sys = -mm(d_right_low, update, tb=True) * strict
        keys_keys = mm(k_low, k_low, tb=True)
        d_kk = (beta * grad_sys).astype(BF16)
        d_beta = jnp.sum(grad_sys * keys_keys, axis=-1, keepdims=True)
        yield
        carried = mm(k_low, state, tb=True)
        d_carried = ((-beta * live) * d_right).astype(BF16)
        d_query = live * mm(d_out, state) + mm(d_scores, k_low)
        yield
        d_key = (
            mm(d_scores, q_low, ta=True)
            + last * mm(update, dstate)
            + mm(d_carried, state)
            + mm(d_kk, k_low)
            + mm(d_kk, k_low, ta=True)
        )
        yield
        convs = [
            short_conv(proj[:, j * HD : (j + 1) * HD], taps[4 * j : 4 * j + 4], keeps)
            for j in range(3)
        ]
        query, q_scale, q_sig = silu_unit(convs[0])
        key, k_scale, k_sig = silu_unit(convs[1])
        v_sig = jax.nn.sigmoid(convs[2])
        value = convs[2] * v_sig
        d_beta = d_beta + jnp.sum(d_right * (value - live * carried), axis=-1, keepdims=True)
        dbeta_ref[m] += jnp.where(lane == head, d_beta * beta * (1.0 - beta), 0.0)
        d_value = beta * d_right
        d_convs = [
            silu_unit_back(d_query, convs[0], query, q_scale, q_sig),
            silu_unit_back(d_key, convs[1], key, k_scale, k_sig),
            d_value * v_sig * (1.0 + convs[2] * (1.0 - v_sig)),
        ]
        yield
        tap_sums = []
        for j in range(3):
            part = proj[:, j * HD : (j + 1) * HD]
            d_conv = d_convs[j]
            tap_sums.append(jnp.sum(d_conv * part[HALO:], axis=0, keepdims=True))
            zeros = jnp.zeros((HALO, HD), F32)
            d_proj = jnp.concatenate([zeros, taps[4 * j : 4 * j + 1] * d_conv], axis=0)
            for i in range(1, 4):
                kept = keeps[i - 1] * d_conv
                tap_sums.append(
                    jnp.sum(kept * pltpu.roll(part, i, 0)[HALO:], axis=0, keepdims=True)
                )
                spread = jnp.concatenate([zeros, taps[4 * j + i : 4 * j + i + 1] * kept], axis=0)
                d_proj = d_proj + pltpu.roll(spread, HALO + tokens - i, 0)
            at = (3 * hh + j) * HD
            dmain_ref[m, :, at : at + HD] = d_proj.astype(BF16)
            yield
        tap_totals[hh, m] = jnp.concatenate(tap_sums + [jnp.zeros((4, HD), F32)], axis=0)

    interleave([instance(hh, m) for hh in range(per) for m in range(micro)])
    for hh in range(per):
        dtaps_ref[hh] = sum(tap_totals[hh, m] for m in range(micro))


def flip(v):
    return v.astype(F32).T.astype(BF16)


def pack_mixer_kernel(table_ref, q_ref, k_ref, v_ref, beta_ref, conv_ref, out_ref):
    piece = table_ref[pl.program_id(0)]
    rows, n = q_ref.shape
    per = n // HD
    parts = []
    for hh in range(per):
        parts += [r[:, hh * HD : (hh + 1) * HD] for r in (q_ref, k_ref, v_ref)]
    out_ref[0, :rows] = jnp.concatenate(parts, axis=1)
    conv = conv_ref[...].astype(F32)
    lines = [beta_ref[hh : hh + 1].astype(F32) for hh in range(per)]
    for j in range(conv.shape[0]):
        line = jnp.zeros((1, HD), F32)
        for p in range(PIECES):
            own = conv[j, p // per : p // per + 1, p % per * HD : (p % per + 1) * HD]
            line = line + jnp.where(piece == p, own, 0.0)
        lines.append(line)
    lines.append(jnp.zeros((1, 3 * n - HD * len(lines)), F32))
    line = jnp.concatenate(lines, axis=1)
    row = lax.broadcasted_iota(jnp.int32, (EXTRA, 3 * n), 0)
    out_ref[0, rows:] = jnp.where(row == 0, line, 0.0).astype(BF16)


def pack_ffn_kernel(table_ref, gate_ref, up_ref, down_ref, out_w_ref, out_ref):
    hidden, rows = gate_ref.shape
    main = hidden // HD * HD
    out_ref[0, :, :main] = flip(gate_ref[:main])
    out_ref[0, :, main : 2 * main] = flip(up_ref[:main])
    rest = jnp.concatenate([gate_ref[main:], up_ref[main:]], axis=0)
    out_ref[0, :, 2 * main : 2 * hidden] = flip(rest)
    wide = main + HD
    down = jnp.concatenate([down_ref[...].astype(F32), jnp.zeros((wide - hidden, rows), F32)], axis=0)
    out_ref[0, :, 2 * hidden : 2 * hidden + wide] = down.T.astype(BF16)
    out_ref[0, :, 2 * hidden + wide :] = flip(out_w_ref[...])


def flip_pieces(table_ref, src_ref, dst_ref):
    rows = src_ref.shape[1] // PIECES
    for pos in range(PIECES):
        start = pl.multiple_of(table_ref[pos] * rows, rows)
        dst_ref[pos * rows : (pos + 1) * rows] = flip(src_ref[:, pl.ds(start, rows)])


def ffn_kernel(hidden, ids_ref, table_ref, mixed_ref, rows_ref, dout_ref, gain_ref, own_ref, *refs):
    pieces, refs = refs[:PIECES], refs[PIECES:]
    out_ref, dmid_ref, dlow_ref, dmixed_ref, gpart_ref = refs[:5]
    (w_ref, wo_ref, x_ref, xt_ref, dt_ref, mid_ref, res_ref, dn_ref, grad_ref, sems, o_sems,
     g_sems) = refs[-12:]
    grad_refs = refs[5:-12]
    step = pl.program_id(0)
    slots = wo_ref.shape[0]
    width = rows_ref.shape[1]
    rows = width // PIECES
    main = hidden // HD * HD
    wide = main + HD
    cut = 2 * hidden + wide
    part = mixed_ref.shape[1]
    ring = w_ref.shape[0]
    order = reduce_order(slots)

    def brought(slot, target, start, size, sem):
        columns = pl.ds(start, size)
        if slot == 0:
            return [pltpu.make_async_copy(own_ref.at[:, :, columns], target, sem.at[0])]
        return [
            pltpu.make_async_copy(piece.at[slot - 1, :, columns], target.at[ids_ref[j]], sem.at[j])
            for j, piece in enumerate(pieces)
        ]

    outs = [brought(k, wo_ref.at[k], cut, part, o_sems.at[k]) for k in range(slots)]
    mains = [brought(k, w_ref.at[i % ring], 0, cut, sems.at[i % ring]) for i, k in enumerate(order)]

    def leaving(i):
        return [
            pltpu.make_async_copy(
                grad_ref.at[i % 2, h], grad_refs[i // 2 * 2 + h].at[:, i % 2], g_sems.at[i % 2, h]
            )
            for h in range(2)
        ]

    @pl.when(step == 0)
    def _():
        for group in outs + mains[:ring]:
            for copy in group:
                copy.start()
        mid_ref[...] = rows_ref[...].astype(F32)
        dn_ref[...] = jnp.zeros_like(dn_ref)
        flip_pieces(table_ref, dout_ref, dt_ref)

    for i in range(slots):

        @pl.when(step == i)
        def _():
            for copy in outs[i]:
                copy.wait()

        @pl.when(step == slots + i)
        def _():
            for copy in mains[i]:
                copy.wait()
            if i >= 2:
                for copy in leaving(i - 2):
                    copy.wait()

    @pl.when(step < slots)
    def _():
        mid_ref[...] += mm(mixed_ref[...], wo_ref[step].reshape(width, part), tb=True)

    def norm():
        mid = mid_ref[...]
        rstd = lax.rsqrt(jnp.mean(mid * mid, axis=-1, keepdims=True) + EPS)
        return mid * rstd, rstd

    @pl.when(step == slots - 1)
    def _():
        unit, _ = norm()
        x_ref[...] = (unit * gain_ref[...]).astype(BF16)
        flip_pieces(table_ref, x_ref, xt_ref)
        res_ref[...] = mid_ref[...]

    @pl.when(step >= slots)
    def _():
        at = lax.rem(step - slots, ring)
        w_gu = w_ref[at, :, :, : 2 * hidden].reshape(width, 2 * hidden)
        w_dn = w_ref[at, :, :, 2 * hidden :].reshape(width, wide)
        both = mm(x_ref[...], w_gu)
        rest = both[:, 2 * main :]
        gate = jnp.concatenate([both[:, :main], rest], axis=1)
        up = jnp.concatenate([both[:, main : 2 * main], pltpu.roll(rest, HD // 2, 1)], axis=1)
        sig = jax.nn.sigmoid(gate)
        act = gate * sig
        hid = (act * up).astype(BF16)
        d_hid = mm(dout_ref[...], w_dn)
        d_gate = (d_hid * up * (sig * (1.0 + gate * (1.0 - sig)))).astype(BF16)
        d_up = (d_hid * act).astype(BF16)
        last = d_gate[:, main:].astype(F32) + pltpu.roll(d_up[:, main:].astype(F32), HD // 2, 1)
        d_gu = jnp.concatenate([d_gate[:, :main], d_up[:, :main], last.astype(BF16)], axis=1)
        res_ref[...] += mm(hid, w_dn, tb=True)
        dn_ref[...] += mm(d_gu, w_gu, tb=True)
        to = lax.rem(step - slots, 2)
        shape = (PIECES // 2, rows)
        for h in range(2):
            span = slice(h * width // 2, (h + 1) * width // 2)
            grad_ref[to, h, :, :, : 2 * hidden] = (
                mm(xt_ref[span], d_gu).astype(BF16).reshape(shape + (2 * hidden,))
            )
            grad_ref[to, h, :, :, 2 * hidden :] = (
                mm(dt_ref[span], hid).astype(BF16).reshape(shape + (wide,))
            )

    for i in range(slots):

        @pl.when(step == slots + i)
        def _():
            for copy in leaving(i):
                copy.start()
            if i + ring < slots:
                for copy in mains[i + ring]:
                    copy.start()

    @pl.when(step == 2 * slots - 1)
    def _():
        out_ref[...] = res_ref[...].astype(BF16)
        unit, rstd = norm()
        grad = dn_ref[...]
        gpart_ref[...] = jnp.broadcast_to(jnp.sum(grad * unit, axis=0, keepdims=True), gpart_ref.shape)
        scaled = grad * gain_ref[...]
        d_mid = dout_ref[...].astype(F32) + rstd * (
            scaled - unit * jnp.mean(scaled * unit, axis=-1, keepdims=True)
        )
        dmid_ref[...] = d_mid
        low = d_mid.astype(BF16)
        dlow_ref[...] = low
        for k in range(slots):
            dmixed_ref[:, k * part : (k + 1) * part] = mm(low, wo_ref[k].reshape(width, part))
        for i in range(max(slots - 2, 0), slots):
            for copy in leaving(i):
                copy.wait()


def grad_mixer_kernel(xt_ref, dqkv_ref, lt_ref, mixed_ref, *refs):
    grad_ref, g_sems = refs[-2:]
    grad_refs = refs[:-2]
    step = pl.program_id(0)
    width = xt_ref.shape[0]
    rows = width // PIECES
    n = dqkv_ref.shape[1]
    slots = pl.num_programs(0)

    def leaving(i):
        return [
            pltpu.make_async_copy(
                grad_ref.at[i % 2, h], grad_refs[i // 2 * 2 + h].at[:, i % 2], g_sems.at[i % 2, h]
            )
            for h in range(2)
        ]

    for i in range(2, slots):

        @pl.when(step == i)
        def _():
            for copy in leaving(i - 2):
                copy.wait()

    to = lax.rem(step, 2)
    for h in range(2):
        span = slice(h * width // 2, (h + 1) * width // 2)
        shape = (PIECES // 2, rows)
        grad_ref[to, h, :, :, :n] = mm(xt_ref[span], dqkv_ref[...]).astype(BF16).reshape(shape + (n,))
        out = mm(lt_ref[span], mixed_ref[...]).astype(BF16)
        grad_ref[to, h, :, :, n:] = out.reshape(shape + (out.shape[1],))

    for i in range(slots):

        @pl.when(step == i)
        def _():
            for copy in leaving(i):
                copy.start()
            if i == slots - 1:
                for j in range(max(slots - 2, 0), slots):
                    for copy in leaving(j):
                        copy.wait()


def bring(ids_ref, pieces, w_ref, sems):
    @pl.when(pl.program_id(0) == 0)
    def _():
        copies = [
            pltpu.make_async_copy(piece, w_ref.at[ids_ref[j]], sems.at[j])
            for j, piece in enumerate(pieces)
        ]
        for copy in copies:
            copy.start()
        for copy in copies:
            copy.wait()


def finish_ffn_kernel(hidden, ids_ref, *refs):
    gate_ref, up_ref, down_ref, w_ref, sems = refs[PIECES:]
    bring(ids_ref, refs[:PIECES], w_ref, sems)
    step = pl.program_id(0)
    main = hidden // HD * HD
    wide = main + HD
    take = lambda at, n: w_ref[step, :, at : at + n].astype(F32).T
    gate_ref[:main] = take(0, main)
    up_ref[:main] = take(main, main)
    rest = take(2 * main, HD)
    gate_ref[main:] = rest[: HD // 2]
    up_ref[main:] = rest[HD // 2 :]
    down_ref[...] = take(2 * hidden, wide)[:hidden]


def finish_mixer_kernel(ids_ref, *refs):
    outs, out_w_ref, w_ref, sems = refs[PIECES:-3], refs[-3], refs[-2], refs[-1]
    bring(ids_ref, refs[:PIECES], w_ref, sems)
    step = pl.program_id(0)
    n = outs[0].shape[1]
    for hh in range(n // HD):
        for j, out in enumerate(outs):
            at = (3 * hh + j) * HD
            out[:, hh * HD : (hh + 1) * HD] = w_ref[step, :, at : at + HD].astype(F32)
    out_w_ref[...] = w_ref[step, :, 3 * n :].astype(F32).T


def input_kernel(dqkv_ref, w_ref, db_ref, beta_w_ref, front_ref, out_ref):
    step = pl.program_id(0)
    width, n = out_ref.shape[2], dqkv_ref.shape[2]
    weights = w_ref[0, :, : width // PIECES].reshape(width, n)
    for m in range(out_ref.shape[0]):
        grad = mm(dqkv_ref[m], weights, tb=True)
        more = mm(db_ref[m], beta_w_ref[0])

        @pl.when(step == 0)
        def _():
            front_ref[m] = grad[:HALO]
            out_ref[m] = grad[HALO:] + more

        @pl.when(step > 0)
        def _():
            front_ref[m] += grad[:HALO]
            out_ref[m] += grad[HALO:] + more


def norm_kernel(grad_ref, front_ref, rows_ref, dmid_ref, gain_ref, out_ref, gpart_ref):
    tokens = grad_ref.shape[1]
    cut = tokens - HALO
    total = jnp.zeros((1, grad_ref.shape[2]), F32)
    for m in range(grad_ref.shape[0]):
        grad = jnp.concatenate([grad_ref[m, :cut], grad_ref[m, cut:] + front_ref[m]], axis=0)
        rows = rows_ref[m * tokens : (m + 1) * tokens].astype(F32)
        rstd = lax.rsqrt(jnp.mean(rows * rows, axis=-1, keepdims=True) + EPS)
        unit = rows * rstd
        total = total + jnp.sum(grad * unit, axis=0, keepdims=True)
        scaled = grad * gain_ref[...]
        out_ref[m * tokens : (m + 1) * tokens] = (
            dmid_ref[m * tokens : (m + 1) * tokens]
            + rstd * (scaled - unit * jnp.mean(scaled * unit, axis=-1, keepdims=True))
        ).astype(BF16)
    gpart_ref[...] = jnp.broadcast_to(total, gpart_ref.shape)


def params(mib=60):
    return pltpu.CompilerParams(
        dimension_semantics=("arbitrary",), vmem_limit_bytes=mib * MIB
    )


def cost(flops, nbytes):
    return pl.CostEstimate(flops=int(flops), bytes_accessed=int(nbytes), transcendentals=0)


ANYWHERE = pl.BlockSpec(memory_space=pl.ANY)


def whole(shape):
    return pl.BlockSpec(tuple(shape), lambda *_: (0,) * len(shape), pipeline_mode=pl.Buffered(1))


def reduce_order(slots):
    return list(range(slots - 2, 0, -1)) + [slots - 1, 0]


def lead(n, shape):
    return pl.BlockSpec((n,) + tuple(shape[1:]), lambda h, *_: (h,) + (0,) * (len(shape) - 1))


def rolled(n, shape, shift, steps):
    return pl.BlockSpec(
        (n,) + tuple(shape[1:]), lambda h, *_: ((h + shift) % steps,) + (0,) * (len(shape) - 1)
    )


def sds(shape, dtype):
    return jax.ShapeDtypeStruct(tuple(shape), dtype)


def call(kernel, grid, in_specs, out_specs, out_shape, estimate, name, scratch=(), prefetch=0, mib=60):
    return pl.pallas_call(
        kernel,
        grid_spec=pltpu.PrefetchScalarGridSpec(
            num_scalar_prefetch=prefetch,
            grid=(grid,),
            in_specs=in_specs,
            out_specs=out_specs,
            scratch_shapes=list(scratch),
        ),
        out_shape=out_shape,
        compiler_params=params(mib),
        cost_estimate=cost(*estimate),
        name=name,
    )


def pack_mixer(table, w_query, w_key, w_value, beta_t, conv):
    width, n = w_query.shape
    rows = width // PIECES
    spec = pl.BlockSpec((rows, n), lambda i, t: (t[i], 0))
    count = table.shape[0]
    return call(
        pack_mixer_kernel, count,
        [spec] * 3 + [pl.BlockSpec((beta_t.shape[0], rows), lambda i, t: (0, t[i])), whole(conv.shape)],
        pl.BlockSpec((1, rows + EXTRA, 3 * n), lambda i, t: (i, 0, 0)),
        sds((count, rows + EXTRA, 3 * n), BF16), (0, 12 * count * rows * n), "pack_mixer", prefetch=1,
    )(table, w_query, w_key, w_value, beta_t, conv)


def pack_ffn(table, gate_t, up_t, w_down, w_out):
    hidden, width = gate_t.shape
    rows = width // PIECES
    n = 2 * hidden + hidden // HD * HD + HD + w_out.shape[0]
    count = table.shape[0]
    return call(
        pack_ffn_kernel, count,
        [pl.BlockSpec((w.shape[0], rows), lambda i, t: (0, t[i])) for w in (gate_t, up_t, w_down, w_out)],
        pl.BlockSpec((1, rows, n), lambda i, t: (i, 0, 0)),
        sds((count, rows, n), BF16), (0, 4 * count * rows * n), "pack_ffn", prefetch=1,
    )(table, gate_t, up_t, w_down, w_out)


def mixer_local(ids, x, halo, seg, seg_row, own, pieces, heads):
    micro, tokens, width = x.shape
    slots = pieces[0].shape[0] + 1
    per = heads // slots
    hm = (heads, micro)
    rows, n = own.shape[1:]
    outs = [
        sds((slots, PIECES, rows, n), BF16),
        sds((micro, tokens, HD), F32),
        sds((heads, 16, HD), F32),
        sds((slots, per * LANES, width), BF16),
        sds(hm + (HALO + tokens, 3 * HD), F32),
        sds(hm + (tokens, 2 * HD), BF16),
        sds(hm + (tokens, tokens), BF16),
        sds(hm + (tokens, tokens), BF16),
        sds(hm + (tokens, HD), F32),
        sds(hm + (tokens, HD), BF16),
        sds(hm + (HD, HD), BF16),
        sds(hm + (HD, HD), F32),
        sds(hm + (HD, HD), BF16),
    ]
    return call(
        local_kernel, slots,
        [whole(x.shape), whole(halo.shape), whole(seg.shape), whole(seg_row.shape)]
        + [ANYWHERE] * (1 + PIECES),
        [whole(o.shape) for o in outs[:2]] + [lead(per, outs[2].shape), lead(1, outs[3].shape)]
        + [lead(per, o.shape) for o in outs[4:]],
        outs, (heads * micro * 1e9, heads * micro * 2e6), "mixer_local",
        [pltpu.SemaphoreType.DMA((slots, PIECES))], prefetch=1,
    )(ids, x, halo, seg, seg_row, own, *pieces)


def hop(state, keep, gain, slots, back):
    per = gain.shape[0] // slots
    shift = slots - 1 if back else 1
    return call(
        functools.partial(hop_kernel, back), slots,
        [rolled(per, state.shape, shift, slots), lead(per, keep.shape), lead(per, gain.shape)],
        lead(per, gain.shape), sds(gain.shape, BF16),
        (gain.size * 512, gain.size * 12), "hop", mib=12,
    )(state, keep, gain)


def mixer_output(qk, scores, base, mix, state, seg, slots):
    heads, micro, tokens = qk.shape[:3]
    per = heads // slots
    return call(
        output_kernel, slots,
        [lead(per, a.shape) for a in (qk, scores, base, mix)]
        + [rolled(per, state.shape, 1, slots), whole(seg.shape)],
        [pl.BlockSpec((micro, tokens, per * HD), lambda h: (0, 0, h)), lead(per, base.shape)],
        [sds((micro, tokens, heads * HD), BF16), sds(base.shape, BF16)],
        (heads * micro * 5e7, heads * micro * 5e5), "mixer_output",
    )(qk, scores, base, mix, state, seg)


def mixer_back_local(d_mixed, qk, inv, scores, beta, seg, slots):
    heads, micro, tokens = qk.shape[:3]
    per = heads // slots
    outs = [sds((heads, micro, tokens, HD), F32), sds((heads, micro, HD, HD), F32)]
    outs.append(sds((heads, micro, HD, HD), BF16))
    return call(
        back_local_kernel, slots,
        [pl.BlockSpec((micro, tokens, per * HD), lambda h: (0, 0, h))]
        + [lead(per, a.shape) for a in (qk, inv, scores)]
        + [whole(beta.shape), whole(seg.shape)],
        [lead(per, o.shape) for o in outs], outs,
        (heads * micro * 5e7, heads * micro * 5e5), "mixer_back_local",
    )(d_mixed, qk, inv, scores, beta, seg)


def mixer_back(d_mixed, y0, qk, inv, update, state, d_state, proj, taps, beta, seg, seg_row, slots):
    heads, micro, tokens = qk.shape[:3]
    per = heads // slots
    columns = lambda rows, n: pl.BlockSpec((micro, rows, per * n), lambda h: (0, 0, h))
    return call(
        back_kernel, slots,
        [columns(tokens, HD)]
        + [lead(per, a.shape) for a in (y0, qk, inv, update)]
        + [rolled(per, state.shape, 1, slots), rolled(per, d_state.shape, slots - 1, slots)]
        + [lead(per, proj.shape), lead(per, taps.shape)]
        + [whole(a.shape) for a in (beta, seg, seg_row)],
        [columns(HALO + tokens, 3 * HD), whole(beta.shape), lead(per, taps.shape)],
        [
            sds((micro, HALO + tokens, heads * 3 * HD), BF16),
            sds(beta.shape, F32),
            sds(taps.shape, F32),
        ],
        (heads * micro * 5e8, heads * micro * 2e6), "mixer_back",
    )(d_mixed, y0, qk, inv, update, state, d_state, proj, taps, beta, seg, seg_row)


def grads_out(slots, rows, n):
    shape = (PIECES // 2, rows, n)
    return (
        [sds((PIECES // 2, 2, rows, n), BF16)] * slots,
        [pltpu.VMEM((2, 2) + shape, BF16)],
        pltpu.SemaphoreType.DMA((2, 2)),
    )


def ffn(ids, table, mixed, rows, d_out, gain, own, pieces, hidden):
    count, width = rows.shape
    slots = pieces[0].shape[0] + 1
    wide = hidden // HD * HD + HD
    part = mixed.shape[1] // slots
    piece = width // PIECES
    full = whole((count, width))
    grads, room, g_sems = grads_out(slots, piece, 2 * hidden + wide)
    outs = [
        sds((count, width), BF16), sds((count, width), F32), sds((count, width), BF16),
        sds((count, mixed.shape[1]), F32), sds((8, width), F32),
    ]
    ring = 2
    return call(
        functools.partial(ffn_kernel, hidden), 2 * slots,
        [pl.BlockSpec((count, part), lambda s, *_: (0, jnp.minimum(s, slots - 1))),
         full, full, whole(gain.shape)] + [ANYWHERE] * (1 + PIECES),
        [full, full, full, whole((count, mixed.shape[1])), whole((8, width))] + [ANYWHERE] * len(grads),
        outs + grads, (26 * count * width * hidden * slots, 6e7), "ffn",
        [
            pltpu.VMEM((ring, PIECES, piece, 2 * hidden + wide), BF16),
            pltpu.VMEM((slots, PIECES, piece, part), BF16),
            pltpu.VMEM((count, width), BF16),
            pltpu.VMEM((width, count), BF16),
            pltpu.VMEM((width, count), BF16),
            pltpu.VMEM((count, width), F32),
            pltpu.VMEM((count, width), F32),
            pltpu.VMEM((count, width), F32),
        ]
        + room
        + [
            pltpu.SemaphoreType.DMA((ring, PIECES)),
            pltpu.SemaphoreType.DMA((slots, PIECES)),
            g_sems,
        ],
        prefetch=2,
    )(ids, table, mixed, rows, d_out, gain, own, *pieces)


def grad_mixer(xt, d_qkv, lt, mixed, slots):
    width = xt.shape[0]
    n, part = d_qkv.shape[1] // slots, mixed.shape[1] // slots
    grads, room, g_sems = grads_out(slots, width // PIECES, n + part)
    order = reduce_order(slots)

    def at(s):
        return sum(jnp.where(s == i, k, 0) for i, k in enumerate(order))

    columns = lambda a, size: pl.BlockSpec((a.shape[0], size), lambda s: (0, at(s)))
    return call(
        grad_mixer_kernel, slots,
        [whole(xt.shape), columns(d_qkv, n), whole(lt.shape), columns(mixed, part)],
        [ANYWHERE] * len(grads), grads,
        (2 * width * mixed.shape[0] * (n + part) * slots, 2 * width * (n + part) * slots), "grad_mixer",
        room + [g_sems],
    )(xt, d_qkv, lt, mixed)


def finish_ffn(ids, pieces, hidden):
    rows, n = pieces[0].shape
    width = rows * PIECES
    return call(
        functools.partial(finish_ffn_kernel, hidden), PIECES, [ANYWHERE] * PIECES,
        [pl.BlockSpec((hidden, rows), lambda i, t: (0, i))] * 3,
        [sds((hidden, width), F32)] * 3,
        (0, 6 * n * width), "finish_ffn",
        [pltpu.VMEM((PIECES, rows, n), BF16), pltpu.SemaphoreType.DMA((PIECES,))], prefetch=1,
    )(ids, *pieces)


def flip_kernel(table_ref, x_ref, y_ref, xt_ref, yt_ref):
    flip_pieces(table_ref, x_ref, xt_ref)
    flip_pieces(table_ref, y_ref, yt_ref)


def flipped(table, x, y):
    outs = [sds(a.shape[::-1], BF16) for a in (x, y)]
    return call(
        flip_kernel, 1, [whole(x.shape), whole(y.shape)], [whole(o.shape) for o in outs], outs,
        (0, 8 * x.size), "flip", prefetch=1,
    )(table, x, y)


def finish_mixer(ids, pieces, n):
    rows, total = pieces[0].shape
    width = rows * PIECES
    part = total - 3 * n
    return call(
        finish_mixer_kernel, PIECES, [ANYWHERE] * PIECES,
        [pl.BlockSpec((rows, n), lambda i, t: (i, 0))] * 3 + [pl.BlockSpec((part, rows), lambda i, t: (0, i))],
        [sds((width, n), F32)] * 3 + [sds((part, width), F32)],
        (0, 6 * total * width), "finish_mixer",
        [pltpu.VMEM((PIECES, rows, total), BF16), pltpu.SemaphoreType.DMA((PIECES,))], prefetch=1,
    )(ids, *pieces)


def input_back(d_qkv, w, d_b, beta_w):
    micro, ext, _ = d_qkv.shape
    slots, _, _, n = w.shape
    width = beta_w.shape[2]
    outs = [sds((micro, HALO, width), F32), sds((micro, ext - HALO, width), F32)]
    lanes = beta_w.shape[1]
    return call(
        input_kernel, slots,
        [pl.BlockSpec((micro, ext, n), lambda s: (0, 0, s)), lead(1, w.shape),
         whole(d_b.shape[:2] + (HD,)), lead(1, (slots, HD, width))],
        [whole(o.shape) for o in outs], outs,
        (2 * micro * ext * width * n * slots, 2 * slots * width * n), "input_back",
    )(d_qkv, w, d_b, jnp.stack([jnp.pad(beta_w[k], ((k * lanes, HD - (k + 1) * lanes), (0, 0))) for k in range(slots)]))


def input_norm(grad, front, rows, d_mid, gain):
    outs = [sds(rows.shape, BF16), sds((8, rows.shape[1]), F32)]
    return call(
        norm_kernel, 1, [whole(a.shape) for a in (grad, front, rows, d_mid, gain)],
        [whole(o.shape) for o in outs], outs, (0, 12 * rows.size), "input_norm",
    )(grad, front, rows, d_mid, gain)


def swap(x, mask_of, size):
    return lax.ppermute(x, "dp", [(i, i ^ mask_of(i)) for i in range(size)])


def first(i):
    return 4 if i & 1 else 2


def second(i):
    return 2 if i & 1 else 4


def across(i):
    return 1


def from_ahead(x, k, size):
    return lax.ppermute(x, "tensor", [(i, (i - k) % size) for i in range(size)])


def to_ahead(x, k, size):
    return lax.ppermute(x, "tensor", [(i, (i + k) % size) for i in range(size)])


def plane_gather(own, dp):
    b = swap(own, first, dp)
    c = swap(own, second, dp)
    d = swap(b, second, dp)
    near = [own, b, c, d]
    return near + [swap(piece, across, dp) for piece in near]


def piece_ids(own):
    core = own & 1
    f = jnp.where(core == 1, 4, 2)
    s = jnp.where(core == 1, 2, 4)
    return jnp.stack([own, own ^ f, own ^ s, own ^ 6, own ^ 1, own ^ 1 ^ s, own ^ 1 ^ f, own ^ 7])


def sync(*xs):
    return lax.optimization_barrier(xs)


def add(a, b):
    return (a.astype(F32) + b.astype(F32)).astype(BF16)


class Pending:
    def __init__(self):
        self.kept = {}

    def tie(self, *xs):
        keys = list(self.kept)
        values = sync(*xs, *(self.kept[k] for k in keys))
        self.kept = dict(zip(keys, values[len(xs) :]))
        return values[0] if len(xs) == 1 else values[: len(xs)]

    def tie_all(self, *trees):
        leaves, shape = jax.tree.flatten(trees)
        return jax.tree.unflatten(shape, self.tie(*leaves))


class Gather:
    def __init__(self, own, dp):
        self.dp, self.step = dp, 0
        self.pieces = [own, swap(own, first, dp), swap(own, second, dp), swap(own, across, dp)]

    def round(self):
        if self.step == 0:
            own, b, c, far = self.pieces
            both = swap(jnp.stack([b, c]), across, self.dp)
            self.pieces = [own, b, c, far, swap(b, second, self.dp), both]
        else:
            self.pieces.append(swap(self.pieces[4], across, self.dp))
        self.step += 1

    def ordered(self):
        own, b, c, far, d, both, far_d = self.pieces
        return [own, b, c, d, far, both[0], both[1], far_d]


class Reduction:
    def __init__(self, pending, name, grads, order, dp, tensor):
        self.pending, self.name = pending, name
        self.order, self.dp, self.tensor = order, dp, tensor
        self.came, self.parts = {}, {}
        for i in range(len(order) // 2):
            self.came["one", i] = swap(grads[2 * i], across, dp)
            pending.kept[name, "one", i] = grads[2 * i + 1]

    def add(self, step, i):
        came = self.pending.tie(self.came.pop((step, i)))
        return add(self.pending.kept.pop((self.name, step, i)), came)

    def across(self, i):
        total = self.add("one", i)
        self.pending.kept[self.name, "two", i] = total[:2]
        self.came["two", i] = swap(total[2:], first, self.dp)

    def first(self, i):
        total = self.add("two", i)
        self.pending.kept[self.name, "three", i] = total[0]
        self.came["three", i] = swap(total[1], second, self.dp)

    def second(self, i):
        total = self.add("three", i)
        for slot, part in zip(self.order[2 * i : 2 * i + 2], (total[0], total[1])):
            self.pending.kept[self.name, "part", slot] = part
        if i == 0:
            slot = self.order[0]
            self.parts[slot] = to_ahead(self.pending.kept.pop((self.name, "part", slot)), 1, self.tensor)

    def along(self):
        slot = self.order[-2]
        self.parts[slot] = to_ahead(self.pending.kept.pop((self.name, "part", slot)), slot, self.tensor)
        for slot in self.order[1:-2]:
            part = add(
                self.pending.kept.pop((self.name, "part", slot)),
                self.pending.tie(self.parts.pop(slot + 1)),
            )
            self.parts[slot] = to_ahead(part, 1, self.tensor)

    def result(self):
        parts = [self.pending.kept.pop((self.name, "part", 0))]
        parts += [self.parts[k] for k in sorted({1, self.tensor - 1})]
        return sum(p.astype(F32) for p in parts).astype(BF16)


def reduce_far(total, dp):
    mask = PIECES
    while mask < dp:
        total = add(total, swap(total, lambda i: mask, dp))
        mask *= 2
    return total


def norm_rows(rows, gain):
    rstd = lax.rsqrt(jnp.mean(rows * rows, axis=-1, keepdims=True) + EPS)
    return rows * rstd * gain


def project_t(left, right):
    return jnp.einsum("th,td->hd", left, right, preferred_element_type=F32)


def shards(dp, tensor, layer_input, segment, d_out, norm1_gain, w_query, w_key, w_value, w_beta,
           conv_weight, w_out, norm2_gain, w_gate, w_up, w_down):
    micro, _, tokens, width = layer_input.shape
    count = micro * tokens
    local_heads = w_query.shape[1] // HD
    heads = local_heads * tensor
    hidden = w_gate.shape[1]
    own = lax.axis_index("dp") % PIECES
    place = lax.axis_index("tensor")
    ids = piece_ids(own)
    gain1 = norm1_gain.astype(F32)[None]
    gain2 = norm2_gain.astype(F32)[None]
    mine = own[None].astype(jnp.int32)
    every = jnp.arange(PIECES, dtype=jnp.int32)

    pack = (w_query, w_key, w_value, w_beta.T, conv_weight)
    pack_f = (w_gate.T, w_up.T, w_down, w_out)
    piece = pack_mixer(mine, *pack)[0]
    others = [from_ahead(piece, k, tensor) for k in range(1, tensor)]
    rows = layer_input.reshape(count, width)
    _, rows, mine, every = sync(piece, rows, mine, every)
    normed1 = norm_rows(rows.astype(F32), gain1).astype(BF16)
    mixer_in = normed1.reshape(micro, tokens, width)
    ahead = [(i, i + 1) for i in range(tensor - 1)]
    behind = [(i + 1, i) for i in range(tensor - 1)]
    halo = lax.ppermute(mixer_in[:, tokens - HALO :], "tensor", ahead)
    mixer_own = pack_mixer(every, *pack)
    piece = pack_ffn(mine, *pack_f)[0]

    *others, halo, mixer_own, piece, every = sync(*others, halo, mixer_own, piece, every)
    mixer_others = jnp.stack(others)
    b, c = swap(mixer_others, first, dp), swap(mixer_others, second, dp)
    ffn_all = lax.all_gather(piece, "tensor")
    ffn_own = pack_ffn(every, *pack_f)
    mixer_others, b, c, ffn_own = sync(mixer_others, b, c, ffn_own)
    d = swap(b, second, dp)
    mixer_pieces = [mixer_others, b, c] + [swap(x, across, dp) for x in (mixer_others, b, c)]
    d, *mixer_pieces = sync(d, *mixer_pieces)
    mixer_pieces = mixer_pieces[:3] + [d] + mixer_pieces[3:] + [swap(d, across, dp)]

    x_ext = jnp.concatenate([halo, mixer_in], axis=1)

    seg = jnp.pad(segment[:, 0].astype(F32), ((0, 0), (HALO, 0)), constant_values=-1)
    seg = lax.dynamic_slice_in_dim(seg, place * tokens, HALO + tokens, 1)
    seg_row = jnp.broadcast_to(seg[:, None, HALO:], (micro, 8, tokens))
    seg = seg[..., None]

    part = local_heads * HD
    (mixer_w, beta, taps, beta_w, proj, qk, inv, scores, base, mix, keep, gain, state) = mixer_local(
        ids, mixer_in, halo, seg, seg_row, mixer_own, mixer_pieces, heads
    )
    state, ffn_all = sync(state, ffn_all)
    others = jnp.stack(
        [lax.dynamic_index_in_dim(ffn_all, (place + k) % tensor, 0, False) for k in range(1, tensor)]
    )
    recv = lax.ppermute(state, "tensor", ahead)
    near = [others, swap(others, first, dp), swap(others, second, dp)]
    far = [swap(others, across, dp)]
    recv = lax.ppermute(hop(recv, keep, gain, tensor, False), "tensor", ahead)
    recv = hop(recv, keep, gain, tensor, False)
    near[0], recv = sync(near[0], recv)
    recv = lax.ppermute(recv, "tensor", ahead)
    near[:3] = sync(*near)
    near.append(swap(near[1], second, dp))
    far += [swap(near[1], across, dp), swap(near[2], across, dp)]
    state, near[3] = sync(recv, near[3])
    far.append(swap(near[3], across, dp))
    mixed, update = mixer_output(qk, scores, base, mix, state, seg, tensor)
    mixed = mixed.reshape(count, heads * HD)

    out_grad = d_out.reshape(count, width)
    table = jnp.stack([ids[i] for i in (4, 6, 5, 7, 0, 2, 1, 3)])
    output, d_mid, d_mid_low, d_mixed, gain2_part, *grads = ffn(
        ids, table, mixed, rows, out_grad, gain2, ffn_own, near + far, hidden
    )
    order = reduce_order(tensor)
    pending = Pending()
    red = Reduction(pending, "f", grads, order, dp, tensor)

    d_mixed = d_mixed.reshape(micro, tokens, heads * HD)
    y0, back_gain, d_state = mixer_back_local(d_mixed, qk, inv, scores, beta, seg, tensor)
    recv = lax.ppermute(d_state, "tensor", behind)
    pending.tie(d_state)
    red.across(0)
    recv = lax.ppermute(hop(pending.tie(recv), keep, back_gain, tensor, True), "tensor", behind)
    red.across(1)
    xt, lt = flipped(table, *pending.tie(x_ext.reshape(-1, width), d_mid_low))
    pending.kept["xt"] = xt
    recv = lax.ppermute(hop(pending.tie(recv), keep, back_gain, tensor, True), "tensor", behind)
    red.first(0)
    d_qkv, d_beta, d_taps = mixer_back(
        d_mixed, y0, qk, inv, update, state, pending.tie(recv), proj, taps, beta, seg, seg_row, tensor
    )
    d_beta = pending.tie(d_beta)
    grads = grad_mixer(
        pending.kept.pop("xt"), d_qkv.reshape(-1, heads * 3 * HD), lt, mixed, tensor
    )
    mix = Reduction(pending, "m", grads, order, dp, tensor)
    red.second(0)
    red.first(1)
    mix.across(0)
    mix.across(1)
    d_qkv, d_beta, d_taps, gain2_part = pending.tie(d_qkv, d_beta, d_taps, gain2_part)
    d_b = d_beta.astype(BF16)
    front, d_normed1 = input_back(d_qkv, mixer_w, d_b, beta_w)
    front = lax.ppermute(front, "tensor", behind)
    d_normed1 = pending.tie(d_normed1)
    red.second(1)
    red.along()
    mix.first(0)
    mix.first(1)
    total = pending.tie(reduce_far(red.result(), dp))
    gather = Gather(total, dp)
    mix.second(0)
    mix.second(1)
    mix.along()
    d_normed1, front = pending.tie(d_normed1, front)
    input_grad, gain1_part = input_norm(d_normed1, front, rows, d_mid, gain1)
    gain1_part = pending.tie(gain1_part)

    span = width // tensor
    grad_b = project_t(d_b.reshape(count, HD), normed1)[::LANES].reshape(tensor, -1)
    d_taps = d_taps[:, :12].reshape(tensor, local_heads, 12, HD)
    d_taps = jnp.swapaxes(d_taps, 1, 2).reshape(tensor, -1)
    gains = jnp.concatenate([g[0].reshape(tensor, span) for g in (gain1_part, gain2_part)], axis=1)
    gains = lax.dynamic_slice_in_dim(jnp.concatenate([gains, gains]), place, tensor, 0)
    small = jnp.concatenate([grad_b, d_taps, gains], axis=1)
    small_in = swap(small, across, dp)

    gather.pieces, small_in, small = pending.tie_all(gather.pieces, small_in, small)
    gather.round()
    small = small + small_in
    total = reduce_far(mix.result(), dp)
    mixer_gather = Gather(total, dp)
    small_in = swap(small, lambda i: 2, dp)
    gather.pieces, small_in, small = pending.tie_all(gather.pieces, small_in, small)
    gather.round()
    small = small + small_in
    mixer_gather.pieces, small = pending.tie_all(mixer_gather.pieces, small)
    mixer_gather.round()
    small_in = swap(small, lambda i: 4, dp)
    gather.pieces, small_in, small = pending.tie_all(gather.pieces, small_in, small)
    small = small + small_in
    mask = PIECES
    while mask < dp:
        small = small + swap(small, lambda i: mask, dp)
        mask *= 2
    small_in = [to_ahead(small[k], k, tensor) for k in range(1, tensor)]
    gather.pieces, mixer_gather.pieces = pending.tie_all(gather.pieces, mixer_gather.pieces)
    mixer_gather.round()
    grad_gate, grad_up, grad_down = finish_ffn(ids, gather.ordered(), hidden)
    small = sum(small_in, small[0])
    grad_q, grad_k, grad_v, grad_out = finish_mixer(ids, mixer_gather.ordered(), part)
    cut = local_heads * width
    grad_beta = small[:cut].reshape(local_heads, width).T
    grad_conv = small[cut : cut + 12 * span].reshape(3, 4, span)
    cut += 12 * span
    grad_gain1 = small[cut : cut + span]
    grad_gain2 = small[cut + span :]
    return (
        output.reshape(micro, 1, tokens, width),
        input_grad.reshape(micro, 1, tokens, width),
        grad_gain1,
        grad_q,
        grad_k,
        grad_v,
        grad_beta,
        grad_conv,
        grad_out,
        grad_gain2,
        grad_gate.T,
        grad_up.T,
        grad_down,
    )


def solution(mesh):
    in_specs = (
        P(None, "dp", "tensor", None),
        P(None, "dp", None),
        P(None, "dp", "tensor", None),
        P(),
        P(None, "tensor"),
        P(None, "tensor"),
        P(None, "tensor"),
        P(None, "tensor"),
        P(None, None, "tensor"),
        P("tensor", None),
        P(),
        P(None, "tensor"),
        P(None, "tensor"),
        P("tensor", None),
    )
    out_specs = (
        P(None, "dp", "tensor", None),
        P(None, "dp", "tensor", None),
        P("tensor"),
        P(None, "tensor"),
        P(None, "tensor"),
        P(None, "tensor"),
        P(None, "tensor"),
        P(None, None, "tensor"),
        P("tensor", None),
        P("tensor"),
        P(None, "tensor"),
        P(None, "tensor"),
        P("tensor", None),
    )
    body = functools.partial(shards, mesh.shape["dp"], mesh.shape["tensor"])
    return jax.shard_map(body, mesh=mesh, in_specs=in_specs, out_specs=out_specs, check_vma=False)
```

```python
import functools

import jax
import jax.numpy as jnp
from jax import lax
from jax.experimental import pallas as pl
from jax.experimental.pallas import tpu as pltpu
from jax.sharding import PartitionSpec as P

HD = 128
HALO = 16
EXTRA = 16
LANES = 16
PIECES = 8
EPS = 1e-06
F32 = jnp.float32
BF16 = jnp.bfloat16
MIB = 1 << 20


def mm(a, b, ta=False, tb=False):
    dims = (((0 if ta else 1,), (1 if tb else 0,)), ((), ()))
    return lax.dot_general(a.astype(BF16), b.astype(BF16), dims, preferred_element_type=F32)


def interleave(makers):
    running = list(makers)
    while running:
        still = []
        for g in running:
            try:
                next(g)
                still.append(g)
            except StopIteration:
                pass
        running = still


def invert_unit(lows):
    size = lows[0].shape[0]
    row = lax.broadcasted_iota(jnp.int32, (size, size), 0)
    col = lax.broadcasted_iota(jnp.int32, (size, size), 1)
    eye = (row == col).astype(F32)
    invs = [eye - jnp.where((row >> 1) == (col >> 1), low, 0.0) for low in lows]
    step = 1
    while (2 << step) <= size:
        pair = ((row >> (step + 1)) == (col >> (step + 1))) & ((row >> step) != (col >> step))
        lefts = [mm(inv, jnp.where(pair, low, 0.0)) for inv, low in zip(invs, lows)]
        yield
        invs = [inv - mm(left, inv) for inv, left in zip(invs, lefts)]
        yield
        step += 1
    return invs


def short_conv(proj, taps, keeps):
    total = taps[0:1] * proj[HALO:]
    for i in range(1, 4):
        total = total + taps[i : i + 1] * (pltpu.roll(proj, i, 0)[HALO:] * keeps[i - 1])
    return total


def silu_unit(conv):
    sig = jax.nn.sigmoid(conv)
    act = conv * sig
    scale = lax.rsqrt(jnp.sum(act * act, axis=-1, keepdims=True) + EPS)
    return act * scale, scale, sig


def silu_unit_back(grad, conv, unit, scale, sig):
    d_act = scale * (grad - unit * jnp.sum(grad * unit, axis=-1, keepdims=True))
    return d_act * sig * (1.0 + conv * (1.0 - sig))


def flags(seg):
    own = seg[HALO:]
    equal = lambda a: jnp.where(own == a, 1.0, 0.0)
    keeps = [equal(pltpu.roll(jnp.broadcast_to(seg, (seg.shape[0], HD)), i, 0)[HALO:, 0:1]) for i in (1, 2, 3)]
    return keeps, equal(seg[HALO - 1 : HALO]), equal(seg[-1:])


def masks(seg, seg_row):
    n = seg_row.shape[1]
    row = lax.broadcasted_iota(jnp.int32, (n, n), 0)
    col = lax.broadcasted_iota(jnp.int32, (n, n), 1)
    same = seg[HALO:] == seg_row
    strict = jnp.where(same & (row > col), 1.0, 0.0)
    within = jnp.where(same & (row >= col), 1.0, 0.0)
    return strict, within


def pick(values, head):
    lane = lax.broadcasted_iota(jnp.int32, values.shape, 1)
    return jnp.sum(jnp.where(lane == head, values, 0.0), axis=-1, keepdims=True)


def piece_copies(ids_ref, own_ref, piece_refs, w_ref, sems):
    slots = [[pltpu.make_async_copy(own_ref, w_ref.at[0], sems.at[0, 0])]]
    for slot in range(1, w_ref.shape[0]):
        slots.append(
            [
                pltpu.make_async_copy(
                    piece.at[slot - 1], w_ref.at[slot, ids_ref[j]], sems.at[slot, j]
                )
                for j, piece in enumerate(piece_refs)
            ]
        )
    return slots


def local_kernel(ids_ref, x_ref, halo_ref, seg_ref, seg_row_ref, own_ref, *refs):
    pieces = refs[:PIECES]
    (w_ref, beta_ref, taps_ref, beta_w_ref, proj_ref, qk_ref, t_ref, p_ref, ub_ref, w_out_ref, m_ref,
     a_ref, s_ref, sems) = refs[PIECES:]
    slot = pl.program_id(0)
    per = taps_ref.shape[0]
    micro, tokens, width = x_ref.shape
    half = tokens // 2
    rows = width // PIECES
    copies = piece_copies(ids_ref, own_ref, pieces, w_ref, sems)

    @pl.when(slot == 0)
    def _():
        for group in copies:
            for copy in group:
                copy.start()
        beta_ref[...] = jnp.zeros_like(beta_ref)

    for k, group in enumerate(copies):

        @pl.when(slot == k)
        def _():
            for copy in group:
                copy.wait()

    def extra(piece, j):
        return w_ref[slot, piece, rows:, j * HD : (j + 1) * HD]

    beta_w = jnp.concatenate(
        [jnp.concatenate([extra(p, hh) for p in range(PIECES)], axis=1) for hh in range(per)], axis=0
    )
    beta_w_ref[0] = beta_w
    for hh in range(per):
        lines = [extra(per * (r % 4) + hh, per + r // 4)[0:1].astype(F32) for r in range(12)]
        taps_ref[hh] = jnp.concatenate(lines + [jnp.zeros((4, HD), F32)], axis=0)
    lane = lax.broadcasted_iota(jnp.int32, (tokens, HD), 1)

    weights = w_ref[slot, :, :rows].reshape(width, per * 3 * HD)
    shared = []
    for m in range(micro):
        x_ext = jnp.concatenate([halo_ref[m], x_ref[m]], axis=0)
        proj = jnp.dot(x_ext, weights, preferred_element_type=F32)
        seg = seg_ref[m]
        betas = jax.nn.sigmoid(mm(x_ref[m], beta_w, tb=True))
        shared.append((proj, betas, flags(seg), masks(seg, seg_row_ref[m, 0:1])))

    def instance(hh, m):
        proj, betas, (keeps, live, last), (strict, within) = shared[m]
        proj = proj[:, hh * 3 * HD : (hh + 1) * 3 * HD]
        taps = taps_ref[hh]
        proj_ref[hh, m] = proj
        convs = [
            short_conv(proj[:, j * HD : (j + 1) * HD], taps[4 * j : 4 * j + 4], keeps)
            for j in range(3)
        ]
        query = silu_unit(convs[0])[0]
        key = silu_unit(convs[1])[0]
        value = convs[2] * jax.nn.sigmoid(convs[2])
        beta = betas[:, hh * LANES : hh * LANES + 1]
        beta_ref[m] += jnp.where(lane == (slot * per + hh) * LANES, beta, 0.0)
        qk_ref[hh, m] = jnp.concatenate([query, key], axis=1).astype(BF16)
        yield
        low = beta * mm(key, key, tb=True) * strict
        scores = mm(query, key, tb=True) * within
        p_ref[hh, m] = scores.astype(BF16)
        yield
        top, bottom = yield from invert_unit([low[:half, :half], low[half:, half:]])
        cross = mm(bottom, low[half:, :half])
        yield
        cross = -mm(cross, top)
        yield
        inv = jnp.concatenate(
            [
                jnp.concatenate([top, jnp.zeros_like(top)], axis=1),
                jnp.concatenate([cross, bottom], axis=1),
            ],
            axis=0,
        ).astype(BF16)
        t_ref[hh, m] = inv
        both = mm(inv, jnp.concatenate([beta * value, (beta * live) * key], axis=1))
        yield
        late = (last * key).astype(BF16)
        sums = mm(both, late, ta=True)
        row = lax.broadcasted_iota(jnp.int32, (HD, HD), 0)
        col = lax.broadcasted_iota(jnp.int32, (HD, HD), 1)
        keep_state = jnp.where(row == col, live[tokens - 1 : tokens], 0.0)
        ub_ref[hh, m] = both[:, :HD]
        w_out_ref[hh, m] = both[:, HD:].astype(BF16)
        a_ref[hh, m] = sums[:HD]
        s_ref[hh, m] = sums[:HD].astype(BF16)
        m_ref[hh, m] = (keep_state - sums[HD:]).astype(BF16)

    interleave([instance(hh, m) for hh in range(per) for m in range(micro)])


def hop_kernel(back, state_ref, keep_ref, gain_ref, out_ref):
    for h in range(gain_ref.shape[0]):
        for m in range(gain_ref.shape[1]):
            moved = mm(state_ref[h, m], keep_ref[h, m], tb=back)
            out_ref[h, m] = (moved + gain_ref[h, m]).astype(BF16)


def output_kernel(qk_ref, p_ref, ub_ref, w_ref, state_ref, seg_ref, mixed_ref, u_ref):
    per, micro = ub_ref.shape[:2]

    def instance(hh, m):
        live = flags(seg_ref[m])[1]
        state = state_ref[hh, m]
        update = ub_ref[hh, m] - mm(w_ref[hh, m], state, tb=True)
        update = update.astype(BF16)
        far = live * mm(qk_ref[hh, m][:, :HD], state, tb=True)
        yield
        mixed = far + mm(p_ref[hh, m], update)
        u_ref[hh, m] = update
        yield
        mixed_ref[m, :, hh * HD : (hh + 1) * HD] = mixed.astype(BF16)

    interleave([instance(hh, m) for hh in range(per) for m in range(micro)])


def back_local_kernel(dmix_ref, qk_ref, t_ref, p_ref, beta_ref, seg_ref, y_ref, b_ref, s_ref):
    per, micro = qk_ref.shape[:2]
    slot = pl.program_id(0)

    def instance(hh, m):
        live = flags(seg_ref[m])[1]
        d_out = dmix_ref[m, :, hh * HD : (hh + 1) * HD]
        part = mm(p_ref[hh, m], d_out, ta=True)
        yield
        y0 = mm(t_ref[hh, m], part, ta=True)
        yield
        y_ref[hh, m] = y0
        qk = qk_ref[hh, m]
        beta = pick(beta_ref[m], (slot * per + hh) * LANES)
        gain = mm(live * d_out, qk[:, :HD], ta=True) - mm((beta * live) * y0, qk[:, HD:], ta=True)
        b_ref[hh, m] = gain
        s_ref[hh, m] = gain.astype(BF16)

    interleave([instance(hh, m) for hh in range(per) for m in range(micro)])


def back_kernel(dmix_ref, y_ref, qk_ref, t_ref, u_ref, state_ref, dstate_ref, proj_ref,
                taps_ref, beta_ref, seg_ref, seg_row_ref,
                dmain_ref, dbeta_ref, dtaps_ref):
    per, micro = qk_ref.shape[:2]
    tokens = qk_ref.shape[2]
    slot = pl.program_id(0)
    shared = [(flags(seg_ref[m]), masks(seg_ref[m], seg_row_ref[m, 0:1])) for m in range(micro)]
    lane = lax.broadcasted_iota(jnp.int32, (tokens, HD), 1)
    tap_totals = {}

    @pl.when(slot == 0)
    def _():
        dbeta_ref[...] = jnp.zeros_like(dbeta_ref)

    def instance(hh, m):
        (keeps, live, last), (strict, within) = shared[m]
        taps = taps_ref[hh]
        head = (slot * per + hh) * LANES
        proj = proj_ref[hh, m]
        beta = pick(beta_ref[m], head)
        q_low, k_low = qk_ref[hh, m][:, :HD], qk_ref[hh, m][:, HD:]
        state = state_ref[hh, m]
        dstate = dstate_ref[hh, m]
        update = u_ref[hh, m]
        d_out = dmix_ref[m, :, hh * HD : (hh + 1) * HD].astype(BF16)
        ahead = last * mm(k_low, dstate, tb=True)
        yield
        d_right = y_ref[hh, m] + mm(t_ref[hh, m], ahead, ta=True)
        d_right_low = d_right.astype(BF16)
        yield
        d_scores = (mm(d_out, update, tb=True) * within).astype(BF16)
        yield
        grad_sys = -mm(d_right_low, update, tb=True) * strict
        keys_keys = mm(k_low, k_low, tb=True)
        d_kk = (beta * grad_sys).astype(BF16)
        d_beta = jnp.sum(grad_sys * keys_keys, axis=-1, keepdims=True)
        yield
        carried = mm(k_low, state, tb=True)
        d_carried = ((-beta * live) * d_right).astype(BF16)
        d_query = live * mm(d_out, state) + mm(d_scores, k_low)
        yield
        d_key = (
            mm(d_scores, q_low, ta=True)
            + last * mm(update, dstate)
            + mm(d_carried, state)
            + mm(d_kk, k_low)
            + mm(d_kk, k_low, ta=True)
        )
        yield
        convs = [
            short_conv(proj[:, j * HD : (j + 1) * HD], taps[4 * j : 4 * j + 4], keeps)
            for j in range(3)
        ]
        query, q_scale, q_sig = silu_unit(convs[0])
        key, k_scale, k_sig = silu_unit(convs[1])
        v_sig = jax.nn.sigmoid(convs[2])
        value = convs[2] * v_sig
        d_beta = d_beta + jnp.sum(d_right * (value - live * carried), axis=-1, keepdims=True)
        dbeta_ref[m] += jnp.where(lane == head, d_beta * beta * (1.0 - beta), 0.0)
        d_value = beta * d_right
        d_convs = [
            silu_unit_back(d_query, convs[0], query, q_scale, q_sig),
            silu_unit_back(d_key, convs[1], key, k_scale, k_sig),
            d_value * v_sig * (1.0 + convs[2] * (1.0 - v_sig)),
        ]
        yield
        tap_sums = []
        for j in range(3):
            part = proj[:, j * HD : (j + 1) * HD]
            d_conv = d_convs[j]
            tap_sums.append(jnp.sum(d_conv * part[HALO:], axis=0, keepdims=True))
            zeros = jnp.zeros((HALO, HD), F32)
            d_proj = jnp.concatenate([zeros, taps[4 * j : 4 * j + 1] * d_conv], axis=0)
            for i in range(1, 4):
                kept = keeps[i - 1] * d_conv
                tap_sums.append(
                    jnp.sum(kept * pltpu.roll(part, i, 0)[HALO:], axis=0, keepdims=True)
                )
                spread = jnp.concatenate([zeros, taps[4 * j + i : 4 * j + i + 1] * kept], axis=0)
                d_proj = d_proj + pltpu.roll(spread, HALO + tokens - i, 0)
            at = (3 * hh + j) * HD
            dmain_ref[m, :, at : at + HD] = d_proj.astype(BF16)
            yield
        tap_totals[hh, m] = jnp.concatenate(tap_sums + [jnp.zeros((4, HD), F32)], axis=0)

    interleave([instance(hh, m) for hh in range(per) for m in range(micro)])
    for hh in range(per):
        dtaps_ref[hh] = sum(tap_totals[hh, m] for m in range(micro))


def flip(v):
    return v.astype(F32).T.astype(BF16)


def pack_mixer_kernel(table_ref, q_ref, k_ref, v_ref, beta_ref, conv_ref, out_ref):
    piece = table_ref[pl.program_id(0)]
    rows, n = q_ref.shape
    per = n // HD
    parts = []
    for hh in range(per):
        parts += [r[:, hh * HD : (hh + 1) * HD] for r in (q_ref, k_ref, v_ref)]
    out_ref[0, :rows] = jnp.concatenate(parts, axis=1)
    conv = conv_ref[...].astype(F32)
    lines = [beta_ref[hh : hh + 1].astype(F32) for hh in range(per)]
    for j in range(conv.shape[0]):
        line = jnp.zeros((1, HD), F32)
        for p in range(PIECES):
            own = conv[j, p // per : p // per + 1, p % per * HD : (p % per + 1) * HD]
            line = line + jnp.where(piece == p, own, 0.0)
        lines.append(line)
    lines.append(jnp.zeros((1, 3 * n - HD * len(lines)), F32))
    line = jnp.concatenate(lines, axis=1)
    row = lax.broadcasted_iota(jnp.int32, (EXTRA, 3 * n), 0)
    out_ref[0, rows:] = jnp.where(row == 0, line, 0.0).astype(BF16)


def pack_ffn_kernel(table_ref, gate_ref, up_ref, down_ref, out_w_ref, gu_ref, do_ref):
    hidden, rows = gate_ref.shape
    main = hidden // HD * HD
    gu_ref[0, :, :main] = flip(gate_ref[:main])
    gu_ref[0, :, main : 2 * main] = flip(up_ref[:main])
    gu_ref[0, :, 2 * main :] = flip(jnp.concatenate([gate_ref[main:], up_ref[main:]], axis=0))
    wide = main + HD
    down = jnp.concatenate([down_ref[...].astype(F32), jnp.zeros((wide - hidden, rows), F32)], axis=0)
    do_ref[0, :, :wide] = down.T.astype(BF16)
    do_ref[0, :, wide:] = flip(out_w_ref[...])


def flip_pieces(table_ref, src_ref, dst_ref):
    rows = src_ref.shape[1] // PIECES
    for pos in range(PIECES):
        start = pl.multiple_of(table_ref[pos] * rows, rows)
        dst_ref[pos * rows : (pos + 1) * rows] = flip(src_ref[:, pl.ds(start, rows)])


def ordered(pieces):
    own, b, c, far, d, both, far_d = pieces
    return [own, b, c, d, far, both.at[0], both.at[1], far_d]


def ffn_kernel(hidden, ids_ref, table_ref, mixed_ref, rows_ref, dout_ref, gain_ref, *refs):
    owns, groups, refs = refs[:2], [ordered(refs[2:9]), ordered(refs[9:16])], refs[16:]
    out_ref, dmid_ref, dlow_ref, dmixed_ref, gpart_ref = refs[:5]
    (w_ref, wo_ref, x_ref, xt_ref, dt_ref, mid_ref, res_ref, dn_ref, grad_ref, sems, o_sems,
     g_sems) = refs[-12:]
    grad_refs = refs[5:-12]
    step = pl.program_id(0)
    slots = wo_ref.shape[0]
    width = rows_ref.shape[1]
    rows = width // PIECES
    main = hidden // HD * HD
    wide = main + HD
    cut = 2 * hidden + wide
    part = mixed_ref.shape[1]
    ring = w_ref.shape[0]
    order = reduce_order(slots)

    def brought(slot, group, at, target, start, size, sem):
        to = lambda ref: ref.at[:, pl.ds(start, size)]
        if slot == 0:
            return [pltpu.make_async_copy(owns[group].at[:, :, pl.ds(at, size)], target.at[:, :, pl.ds(start, size)], sem.at[0])]
        return [
            pltpu.make_async_copy(piece.at[slot - 1, :, pl.ds(at, size)], to(target.at[ids_ref[j]]), sem.at[j])
            for j, piece in enumerate(groups[group])
        ]

    outs = [brought(k, 1, wide, wo_ref.at[k], 0, part, o_sems.at[k]) for k in range(slots)]
    mains = [
        brought(k, 0, 0, w_ref.at[i % ring], 0, 2 * hidden, sems.at[0, i % ring])
        + brought(k, 1, 0, w_ref.at[i % ring], 2 * hidden, wide, sems.at[1, i % ring])
        for i, k in enumerate(order)
    ]

    def leaving(i):
        return [
            pltpu.make_async_copy(
                grad_ref.at[i % 2, h], grad_refs[i // 2 * 2 + h].at[:, i % 2], g_sems.at[i % 2, h]
            )
            for h in range(2)
        ]

    @pl.when(step == 0)
    def _():
        for group in outs + mains[:ring]:
            for copy in group:
                copy.start()
        mid_ref[...] = rows_ref[...].astype(F32)
        dn_ref[...] = jnp.zeros_like(dn_ref)
        flip_pieces(table_ref, dout_ref, dt_ref)

    for i in range(slots):

        @pl.when(step == i)
        def _():
            for copy in outs[i]:
                copy.wait()

        @pl.when(step == slots + i)
        def _():
            for copy in mains[i]:
                copy.wait()
            if i >= 2:
                for copy in leaving(i - 2):
                    copy.wait()

    @pl.when(step < slots)
    def _():
        mid_ref[...] += mm(mixed_ref[...], wo_ref[step].reshape(width, part), tb=True)

    def norm():
        mid = mid_ref[...]
        rstd = lax.rsqrt(jnp.mean(mid * mid, axis=-1, keepdims=True) + EPS)
        return mid * rstd, rstd

    @pl.when(step == slots - 1)
    def _():
        unit, _ = norm()
        x_ref[...] = (unit * gain_ref[...]).astype(BF16)
        flip_pieces(table_ref, x_ref, xt_ref)
        res_ref[...] = mid_ref[...]

    @pl.when(step >= slots)
    def _():
        at = lax.rem(step - slots, ring)
        w_gu = w_ref[at, :, :, : 2 * hidden].reshape(width, 2 * hidden)
        w_dn = w_ref[at, :, :, 2 * hidden :].reshape(width, wide)
        both = mm(x_ref[...], w_gu)
        rest = both[:, 2 * main :]
        gate = jnp.concatenate([both[:, :main], rest], axis=1)
        up = jnp.concatenate([both[:, main : 2 * main], pltpu.roll(rest, HD // 2, 1)], axis=1)
        sig = jax.nn.sigmoid(gate)
        act = gate * sig
        hid = (act * up).astype(BF16)
        d_hid = mm(dout_ref[...], w_dn)
        d_gate = (d_hid * up * (sig * (1.0 + gate * (1.0 - sig)))).astype(BF16)
        d_up = (d_hid * act).astype(BF16)
        last = d_gate[:, main:].astype(F32) + pltpu.roll(d_up[:, main:].astype(F32), HD // 2, 1)
        d_gu = jnp.concatenate([d_gate[:, :main], d_up[:, :main], last.astype(BF16)], axis=1)
        res_ref[...] += mm(hid, w_dn, tb=True)
        dn_ref[...] += mm(d_gu, w_gu, tb=True)
        to = lax.rem(step - slots, 2)
        shape = (PIECES // 2, rows)
        for h in range(2):
            span = slice(h * width // 2, (h + 1) * width // 2)
            grad_ref[to, h, :, :, : 2 * hidden] = (
                mm(xt_ref[span], d_gu).astype(BF16).reshape(shape + (2 * hidden,))
            )
            grad_ref[to, h, :, :, 2 * hidden :] = (
                mm(dt_ref[span], hid).astype(BF16).reshape(shape + (wide,))
            )

    for i in range(slots):

        @pl.when(step == slots + i)
        def _():
            for copy in leaving(i):
                copy.start()
            if i + ring < slots:
                for copy in mains[i + ring]:
                    copy.start()

    @pl.when(step == 2 * slots - 1)
    def _():
        out_ref[...] = res_ref[...].astype(BF16)
        unit, rstd = norm()
        grad = dn_ref[...]
        gpart_ref[...] = jnp.broadcast_to(jnp.sum(grad * unit, axis=0, keepdims=True), gpart_ref.shape)
        scaled = grad * gain_ref[...]
        d_mid = dout_ref[...].astype(F32) + rstd * (
            scaled - unit * jnp.mean(scaled * unit, axis=-1, keepdims=True)
        )
        dmid_ref[...] = d_mid
        low = d_mid.astype(BF16)
        dlow_ref[...] = low
        for k in range(slots):
            dmixed_ref[:, k * part : (k + 1) * part] = mm(low, wo_ref[k].reshape(width, part))
        for i in range(max(slots - 2, 0), slots):
            for copy in leaving(i):
                copy.wait()


def grad_mixer_kernel(xt_ref, dqkv_ref, lt_ref, mixed_ref, *refs):
    grad_ref, g_sems = refs[-2:]
    grad_refs = refs[:-2]
    step = pl.program_id(0)
    width = xt_ref.shape[0]
    rows = width // PIECES
    n = dqkv_ref.shape[1]
    slots = pl.num_programs(0)

    def leaving(i):
        return [
            pltpu.make_async_copy(
                grad_ref.at[i % 2, h], grad_refs[i // 2 * 2 + h].at[:, i % 2], g_sems.at[i % 2, h]
            )
            for h in range(2)
        ]

    for i in range(2, slots):

        @pl.when(step == i)
        def _():
            for copy in leaving(i - 2):
                copy.wait()

    to = lax.rem(step, 2)
    for h in range(2):
        span = slice(h * width // 2, (h + 1) * width // 2)
        shape = (PIECES // 2, rows)
        grad_ref[to, h, :, :, :n] = mm(xt_ref[span], dqkv_ref[...]).astype(BF16).reshape(shape + (n,))
        out = mm(lt_ref[span], mixed_ref[...]).astype(BF16)
        grad_ref[to, h, :, :, n:] = out.reshape(shape + (out.shape[1],))

    for i in range(slots):

        @pl.when(step == i)
        def _():
            for copy in leaving(i):
                copy.start()
            if i == slots - 1:
                for j in range(max(slots - 2, 0), slots):
                    for copy in leaving(j):
                        copy.wait()


def bring(ids_ref, pieces, w_ref, sems):
    @pl.when(pl.program_id(0) == 0)
    def _():
        copies = [
            pltpu.make_async_copy(piece, w_ref.at[ids_ref[j]], sems.at[j])
            for j, piece in enumerate(pieces)
        ]
        for copy in copies:
            copy.start()
        for copy in copies:
            copy.wait()


def finish_ffn_kernel(hidden, ids_ref, *refs):
    gate_ref, up_ref, down_ref, w_ref, sems = refs[PIECES:]
    bring(ids_ref, refs[:PIECES], w_ref, sems)
    step = pl.program_id(0)
    main = hidden // HD * HD
    wide = main + HD
    take = lambda at, n: w_ref[step, :, at : at + n].astype(F32).T
    gate_ref[:main] = take(0, main)
    up_ref[:main] = take(main, main)
    rest = take(2 * main, HD)
    gate_ref[main:] = rest[: HD // 2]
    up_ref[main:] = rest[HD // 2 :]
    down_ref[...] = take(2 * hidden, wide)[:hidden]


def finish_mixer_kernel(ids_ref, *refs):
    outs, out_w_ref, w_ref, sems = refs[PIECES:-3], refs[-3], refs[-2], refs[-1]
    bring(ids_ref, refs[:PIECES], w_ref, sems)
    step = pl.program_id(0)
    n = outs[0].shape[1]
    for hh in range(n // HD):
        for j, out in enumerate(outs):
            at = (3 * hh + j) * HD
            out[:, hh * HD : (hh + 1) * HD] = w_ref[step, :, at : at + HD].astype(F32)
    out_w_ref[...] = w_ref[step, :, 3 * n :].astype(F32).T


def input_kernel(dqkv_ref, w_ref, db_ref, beta_w_ref, front_ref, out_ref):
    step = pl.program_id(0)
    width, n = out_ref.shape[2], dqkv_ref.shape[2]
    weights = w_ref[0, :, : width // PIECES].reshape(width, n)
    for m in range(out_ref.shape[0]):
        grad = mm(dqkv_ref[m], weights, tb=True)
        more = mm(db_ref[m], beta_w_ref[0])

        @pl.when(step == 0)
        def _():
            front_ref[m] = grad[:HALO]
            out_ref[m] = grad[HALO:] + more

        @pl.when(step > 0)
        def _():
            front_ref[m] += grad[:HALO]
            out_ref[m] += grad[HALO:] + more


def norm_kernel(grad_ref, front_ref, rows_ref, dmid_ref, gain_ref, out_ref, gpart_ref):
    tokens = grad_ref.shape[1]
    cut = tokens - HALO
    total = jnp.zeros((1, grad_ref.shape[2]), F32)
    for m in range(grad_ref.shape[0]):
        grad = jnp.concatenate([grad_ref[m, :cut], grad_ref[m, cut:] + front_ref[m]], axis=0)
        rows = rows_ref[m * tokens : (m + 1) * tokens].astype(F32)
        rstd = lax.rsqrt(jnp.mean(rows * rows, axis=-1, keepdims=True) + EPS)
        unit = rows * rstd
        total = total + jnp.sum(grad * unit, axis=0, keepdims=True)
        scaled = grad * gain_ref[...]
        out_ref[m * tokens : (m + 1) * tokens] = (
            dmid_ref[m * tokens : (m + 1) * tokens]
            + rstd * (scaled - unit * jnp.mean(scaled * unit, axis=-1, keepdims=True))
        ).astype(BF16)
    gpart_ref[...] = jnp.broadcast_to(total, gpart_ref.shape)


def params(mib=60):
    return pltpu.CompilerParams(
        dimension_semantics=("arbitrary",), vmem_limit_bytes=mib * MIB
    )


def cost(flops, nbytes):
    return pl.CostEstimate(flops=int(flops), bytes_accessed=int(nbytes), transcendentals=0)


ANYWHERE = pl.BlockSpec(memory_space=pl.ANY)


def whole(shape):
    return pl.BlockSpec(tuple(shape), lambda *_: (0,) * len(shape), pipeline_mode=pl.Buffered(1))


def reduce_order(slots):
    return list(range(slots - 2, 0, -1)) + [slots - 1, 0]


def lead(n, shape):
    return pl.BlockSpec((n,) + tuple(shape[1:]), lambda h, *_: (h,) + (0,) * (len(shape) - 1))


def rolled(n, shape, shift, steps):
    return pl.BlockSpec(
        (n,) + tuple(shape[1:]), lambda h, *_: ((h + shift) % steps,) + (0,) * (len(shape) - 1)
    )


def sds(shape, dtype):
    return jax.ShapeDtypeStruct(tuple(shape), dtype)


def call(kernel, grid, in_specs, out_specs, out_shape, estimate, name, scratch=(), prefetch=0, mib=60):
    return pl.pallas_call(
        kernel,
        grid_spec=pltpu.PrefetchScalarGridSpec(
            num_scalar_prefetch=prefetch,
            grid=(grid,),
            in_specs=in_specs,
            out_specs=out_specs,
            scratch_shapes=list(scratch),
        ),
        out_shape=out_shape,
        compiler_params=params(mib),
        cost_estimate=cost(*estimate),
        name=name,
    )


def pack_mixer(table, w_query, w_key, w_value, beta_t, conv):
    width, n = w_query.shape
    rows = width // PIECES
    spec = pl.BlockSpec((rows, n), lambda i, t: (t[i], 0))
    count = table.shape[0]
    return call(
        pack_mixer_kernel, count,
        [spec] * 3 + [pl.BlockSpec((beta_t.shape[0], rows), lambda i, t: (0, t[i])), whole(conv.shape)],
        pl.BlockSpec((1, rows + EXTRA, 3 * n), lambda i, t: (i, 0, 0)),
        sds((count, rows + EXTRA, 3 * n), BF16), (0, 12 * count * rows * n), "pack_mixer", prefetch=1,
    )(table, w_query, w_key, w_value, beta_t, conv)


def pack_ffn(table, gate_t, up_t, w_down, w_out):
    hidden, width = gate_t.shape
    rows = width // PIECES
    n = hidden // HD * HD + HD + w_out.shape[0]
    count = table.shape[0]
    return call(
        pack_ffn_kernel, count,
        [pl.BlockSpec((w.shape[0], rows), lambda i, t: (0, t[i])) for w in (gate_t, up_t, w_down, w_out)],
        [pl.BlockSpec((1, rows, m), lambda i, t: (i, 0, 0)) for m in (2 * hidden, n)],
        [sds((count, rows, m), BF16) for m in (2 * hidden, n)], (0, 0), "pack_ffn", prefetch=1,
    )(table, gate_t, up_t, w_down, w_out)


def mixer_local(ids, x, halo, seg, seg_row, own, pieces, heads):
    micro, tokens, width = x.shape
    slots = pieces[0].shape[0] + 1
    per = heads // slots
    hm = (heads, micro)
    rows, n = own.shape[1:]
    outs = [
        sds((slots, PIECES, rows, n), BF16),
        sds((micro, tokens, HD), F32),
        sds((heads, 16, HD), F32),
        sds((slots, per * LANES, width), BF16),
        sds(hm + (HALO + tokens, 3 * HD), F32),
        sds(hm + (tokens, 2 * HD), BF16),
        sds(hm + (tokens, tokens), BF16),
        sds(hm + (tokens, tokens), BF16),
        sds(hm + (tokens, HD), F32),
        sds(hm + (tokens, HD), BF16),
        sds(hm + (HD, HD), BF16),
        sds(hm + (HD, HD), F32),
        sds(hm + (HD, HD), BF16),
    ]
    return call(
        local_kernel, slots,
        [whole(x.shape), whole(halo.shape), whole(seg.shape), whole(seg_row.shape)]
        + [ANYWHERE] * (1 + PIECES),
        [whole(o.shape) for o in outs[:2]] + [lead(per, outs[2].shape), lead(1, outs[3].shape)]
        + [lead(per, o.shape) for o in outs[4:]],
        outs, (heads * micro * 1e9, heads * micro * 2e6), "mixer_local",
        [pltpu.SemaphoreType.DMA((slots, PIECES))], prefetch=1,
    )(ids, x, halo, seg, seg_row, own, *pieces)


def hop(state, keep, gain, slots, back):
    per = gain.shape[0] // slots
    shift = slots - 1 if back else 1
    return call(
        functools.partial(hop_kernel, back), slots,
        [rolled(per, state.shape, shift, slots), lead(per, keep.shape), lead(per, gain.shape)],
        lead(per, gain.shape), sds(gain.shape, BF16),
        (gain.size * 512, gain.size * 12), "hop", mib=12,
    )(state, keep, gain)


def mixer_output(qk, scores, base, mix, state, seg, slots):
    heads, micro, tokens = qk.shape[:3]
    per = heads // slots
    return call(
        output_kernel, slots,
        [lead(per, a.shape) for a in (qk, scores, base, mix)]
        + [rolled(per, state.shape, 1, slots), whole(seg.shape)],
        [pl.BlockSpec((micro, tokens, per * HD), lambda h: (0, 0, h)), lead(per, base.shape)],
        [sds((micro, tokens, heads * HD), BF16), sds(base.shape, BF16)],
        (heads * micro * 5e7, heads * micro * 5e5), "mixer_output",
    )(qk, scores, base, mix, state, seg)


def mixer_back_local(d_mixed, qk, inv, scores, beta, seg, slots):
    heads, micro, tokens = qk.shape[:3]
    per = heads // slots
    outs = [sds((heads, micro, tokens, HD), F32), sds((heads, micro, HD, HD), F32)]
    outs.append(sds((heads, micro, HD, HD), BF16))
    return call(
        back_local_kernel, slots,
        [pl.BlockSpec((micro, tokens, per * HD), lambda h: (0, 0, h))]
        + [lead(per, a.shape) for a in (qk, inv, scores)]
        + [whole(beta.shape), whole(seg.shape)],
        [lead(per, o.shape) for o in outs], outs,
        (heads * micro * 5e7, heads * micro * 5e5), "mixer_back_local",
    )(d_mixed, qk, inv, scores, beta, seg)


def mixer_back(d_mixed, y0, qk, inv, update, state, d_state, proj, taps, beta, seg, seg_row, slots):
    heads, micro, tokens = qk.shape[:3]
    per = heads // slots
    columns = lambda rows, n: pl.BlockSpec((micro, rows, per * n), lambda h: (0, 0, h))
    return call(
        back_kernel, slots,
        [columns(tokens, HD)]
        + [lead(per, a.shape) for a in (y0, qk, inv, update)]
        + [rolled(per, state.shape, 1, slots), rolled(per, d_state.shape, slots - 1, slots)]
        + [lead(per, proj.shape), lead(per, taps.shape)]
        + [whole(a.shape) for a in (beta, seg, seg_row)],
        [columns(HALO + tokens, 3 * HD), whole(beta.shape), lead(per, taps.shape)],
        [
            sds((micro, HALO + tokens, heads * 3 * HD), BF16),
            sds(beta.shape, F32),
            sds(taps.shape, F32),
        ],
        (heads * micro * 5e8, heads * micro * 2e6), "mixer_back",
    )(d_mixed, y0, qk, inv, update, state, d_state, proj, taps, beta, seg, seg_row)


def grads_out(slots, rows, n):
    shape = (PIECES // 2, rows, n)
    return (
        [sds((PIECES // 2, 2, rows, n), BF16)] * slots,
        [pltpu.VMEM((2, 2) + shape, BF16)],
        pltpu.SemaphoreType.DMA((2, 2)),
    )


def ffn(ids, table, mixed, rows, d_out, gain, own, pieces, hidden):
    count, width = rows.shape
    slots = pieces[0].shape[0] + 1
    assert len(pieces) == 14
    wide = hidden // HD * HD + HD
    part = mixed.shape[1] // slots
    piece = width // PIECES
    full = whole((count, width))
    grads, room, g_sems = grads_out(slots, piece, 2 * hidden + wide)
    outs = [
        sds((count, width), BF16), sds((count, width), F32), sds((count, width), BF16),
        sds((count, mixed.shape[1]), F32), sds((8, width), F32),
    ]
    ring = 2
    return call(
        functools.partial(ffn_kernel, hidden), 2 * slots,
        [pl.BlockSpec((count, part), lambda s, *_: (0, jnp.minimum(s, slots - 1))),
         full, full, whole(gain.shape)] + [ANYWHERE] * 16,
        [full, full, full, whole((count, mixed.shape[1])), whole((8, width))] + [ANYWHERE] * len(grads),
        outs + grads, (26 * count * width * hidden * slots, 6e7), "ffn",
        [
            pltpu.VMEM((ring, PIECES, piece, 2 * hidden + wide), BF16),
            pltpu.VMEM((slots, PIECES, piece, part), BF16),
            pltpu.VMEM((count, width), BF16),
            pltpu.VMEM((width, count), BF16),
            pltpu.VMEM((width, count), BF16),
            pltpu.VMEM((count, width), F32),
            pltpu.VMEM((count, width), F32),
            pltpu.VMEM((count, width), F32),
        ]
        + room
        + [
            pltpu.SemaphoreType.DMA((2, ring, PIECES)),
            pltpu.SemaphoreType.DMA((slots, PIECES)),
            g_sems,
        ],
        prefetch=2,
    )(ids, table, mixed, rows, d_out, gain, *own, *pieces)


def grad_mixer(xt, d_qkv, lt, mixed, slots):
    width = xt.shape[0]
    n, part = d_qkv.shape[1] // slots, mixed.shape[1] // slots
    grads, room, g_sems = grads_out(slots, width // PIECES, n + part)
    order = reduce_order(slots)

    def at(s):
        return sum(jnp.where(s == i, k, 0) for i, k in enumerate(order))

    columns = lambda a, size: pl.BlockSpec((a.shape[0], size), lambda s: (0, at(s)))
    return call(
        grad_mixer_kernel, slots,
        [whole(xt.shape), columns(d_qkv, n), whole(lt.shape), columns(mixed, part)],
        [ANYWHERE] * len(grads), grads,
        (2 * width * mixed.shape[0] * (n + part) * slots, 2 * width * (n + part) * slots), "grad_mixer",
        room + [g_sems],
    )(xt, d_qkv, lt, mixed)


def finish_ffn(ids, pieces, hidden):
    rows, n = pieces[0].shape
    width = rows * PIECES
    return call(
        functools.partial(finish_ffn_kernel, hidden), PIECES, [ANYWHERE] * PIECES,
        [pl.BlockSpec((hidden, rows), lambda i, t: (0, i))] * 3,
        [sds((hidden, width), F32)] * 3,
        (0, 6 * n * width), "finish_ffn",
        [pltpu.VMEM((PIECES, rows, n), BF16), pltpu.SemaphoreType.DMA((PIECES,))], prefetch=1,
    )(ids, *pieces)


def flip_kernel(table_ref, x_ref, y_ref, xt_ref, yt_ref):
    flip_pieces(table_ref, x_ref, xt_ref)
    flip_pieces(table_ref, y_ref, yt_ref)


def flipped(table, x, y):
    outs = [sds(a.shape[::-1], BF16) for a in (x, y)]
    return call(
        flip_kernel, 1, [whole(x.shape), whole(y.shape)], [whole(o.shape) for o in outs], outs,
        (0, 8 * x.size), "flip", prefetch=1,
    )(table, x, y)


def finish_mixer(ids, pieces, n):
    rows, total = pieces[0].shape
    width = rows * PIECES
    part = total - 3 * n
    return call(
        finish_mixer_kernel, PIECES, [ANYWHERE] * PIECES,
        [pl.BlockSpec((rows, n), lambda i, t: (i, 0))] * 3 + [pl.BlockSpec((part, rows), lambda i, t: (0, i))],
        [sds((width, n), F32)] * 3 + [sds((part, width), F32)],
        (0, 6 * total * width), "finish_mixer",
        [pltpu.VMEM((PIECES, rows, total), BF16), pltpu.SemaphoreType.DMA((PIECES,))], prefetch=1,
    )(ids, *pieces)


def input_back(d_qkv, w, d_b, beta_w):
    micro, ext, _ = d_qkv.shape
    slots, _, _, n = w.shape
    width = beta_w.shape[2]
    outs = [sds((micro, HALO, width), F32), sds((micro, ext - HALO, width), F32)]
    lanes = beta_w.shape[1]
    return call(
        input_kernel, slots,
        [pl.BlockSpec((micro, ext, n), lambda s: (0, 0, s)), lead(1, w.shape),
         whole(d_b.shape[:2] + (HD,)), lead(1, (slots, HD, width))],
        [whole(o.shape) for o in outs], outs,
        (2 * micro * ext * width * n * slots, 2 * slots * width * n), "input_back",
    )(d_qkv, w, d_b, jnp.stack([jnp.pad(beta_w[k], ((k * lanes, HD - (k + 1) * lanes), (0, 0))) for k in range(slots)]))


def input_norm(grad, front, rows, d_mid, gain):
    outs = [sds(rows.shape, BF16), sds((8, rows.shape[1]), F32)]
    return call(
        norm_kernel, 1, [whole(a.shape) for a in (grad, front, rows, d_mid, gain)],
        [whole(o.shape) for o in outs], outs, (0, 12 * rows.size), "input_norm",
    )(grad, front, rows, d_mid, gain)


def swap(x, mask_of, size):
    return lax.ppermute(x, "dp", [(i, i ^ mask_of(i)) for i in range(size)])


def first(i):
    return 4 if i & 1 else 2


def second(i):
    return 2 if i & 1 else 4


def across(i):
    return 1


def from_ahead(x, k, size):
    return lax.ppermute(x, "tensor", [(i, (i - k) % size) for i in range(size)])


def to_ahead(x, k, size):
    return lax.ppermute(x, "tensor", [(i, (i + k) % size) for i in range(size)])


def plane_gather(own, dp):
    b = swap(own, first, dp)
    c = swap(own, second, dp)
    d = swap(b, second, dp)
    near = [own, b, c, d]
    return near + [swap(piece, across, dp) for piece in near]


def piece_ids(own):
    core = own & 1
    f = jnp.where(core == 1, 4, 2)
    s = jnp.where(core == 1, 2, 4)
    return jnp.stack([own, own ^ f, own ^ s, own ^ 6, own ^ 1, own ^ 1 ^ s, own ^ 1 ^ f, own ^ 7])


def sync(*xs):
    return lax.optimization_barrier(xs)


def add(a, b):
    return (a.astype(F32) + b.astype(F32)).astype(BF16)


class Pending:
    def __init__(self):
        self.kept = {}

    def tie(self, *xs):
        keys = list(self.kept)
        values = sync(*xs, *(self.kept[k] for k in keys))
        self.kept = dict(zip(keys, values[len(xs) :]))
        return values[0] if len(xs) == 1 else values[: len(xs)]

    def tie_all(self, *trees):
        leaves, shape = jax.tree.flatten(trees)
        return jax.tree.unflatten(shape, self.tie(*leaves))


class Gather:
    def __init__(self, own, dp):
        self.dp, self.step = dp, 0
        self.pieces = [own, swap(own, first, dp), swap(own, second, dp), swap(own, across, dp)]

    def round(self):
        if self.step == 0:
            own, b, c, far = self.pieces
            both = swap(jnp.stack([b, c]), across, self.dp)
            self.pieces = [own, b, c, far, swap(b, second, self.dp), both]
        else:
            self.pieces.append(swap(self.pieces[4], across, self.dp))
        self.step += 1

    def ordered(self):
        own, b, c, far, d, both, far_d = self.pieces
        return [own, b, c, d, far, both[0], both[1], far_d]


class Reduction:
    def __init__(self, pending, name, grads, order, dp, tensor):
        self.pending, self.name = pending, name
        self.order, self.dp, self.tensor = order, dp, tensor
        self.came, self.parts = {}, {}
        for i in range(len(order) // 2):
            self.came["one", i] = swap(grads[2 * i], across, dp)
            pending.kept[name, "one", i] = grads[2 * i + 1]

    def add(self, step, i):
        came = self.pending.tie(self.came.pop((step, i)))
        return add(self.pending.kept.pop((self.name, step, i)), came)

    def across(self, i):
        total = self.add("one", i)
        self.pending.kept[self.name, "two", i] = total[:2]
        self.came["two", i] = swap(total[2:], first, self.dp)

    def first(self, i):
        total = self.add("two", i)
        self.pending.kept[self.name, "three", i] = total[0]
        self.came["three", i] = swap(total[1], second, self.dp)

    def second(self, i):
        total = self.add("three", i)
        for slot, part in zip(self.order[2 * i : 2 * i + 2], (total[0], total[1])):
            self.pending.kept[self.name, "part", slot] = part
        if i == 0:
            slot = self.order[0]
            self.parts[slot] = to_ahead(self.pending.kept.pop((self.name, "part", slot)), 1, self.tensor)

    def along(self):
        slot = self.order[-2]
        self.parts[slot] = to_ahead(self.pending.kept.pop((self.name, "part", slot)), slot, self.tensor)
        for slot in self.order[1:-2]:
            part = add(
                self.pending.kept.pop((self.name, "part", slot)),
                self.pending.tie(self.parts.pop(slot + 1)),
            )
            self.parts[slot] = to_ahead(part, 1, self.tensor)

    def result(self):
        parts = [self.pending.kept.pop((self.name, "part", 0))]
        parts += [self.parts[k] for k in sorted({1, self.tensor - 1})]
        return sum(p.astype(F32) for p in parts).astype(BF16)


def reduce_far(total, dp):
    mask = PIECES
    while mask < dp:
        total = add(total, swap(total, lambda i: mask, dp))
        mask *= 2
    return total


def norm_rows(rows, gain):
    rstd = lax.rsqrt(jnp.mean(rows * rows, axis=-1, keepdims=True) + EPS)
    return rows * rstd * gain


def project_t(left, right):
    return jnp.einsum("th,td->hd", left, right, preferred_element_type=F32)


def shards(dp, tensor, layer_input, segment, d_out, norm1_gain, w_query, w_key, w_value, w_beta,
           conv_weight, w_out, norm2_gain, w_gate, w_up, w_down):
    micro, _, tokens, width = layer_input.shape
    count = micro * tokens
    local_heads = w_query.shape[1] // HD
    heads = local_heads * tensor
    hidden = w_gate.shape[1]
    own = lax.axis_index("dp") % PIECES
    place = lax.axis_index("tensor")
    ids = piece_ids(own)
    gain1 = norm1_gain.astype(F32)[None]
    gain2 = norm2_gain.astype(F32)[None]
    mine = own[None].astype(jnp.int32)
    every = jnp.arange(PIECES, dtype=jnp.int32)

    pack = (w_query, w_key, w_value, w_beta.T, conv_weight)
    pack_f = (w_gate.T, w_up.T, w_down, w_out)
    piece = pack_mixer(mine, *pack)[0]
    others = [from_ahead(piece, k, tensor) for k in range(1, tensor)]
    rows = layer_input.reshape(count, width)
    _, rows, mine, every = sync(piece, rows, mine, every)
    normed1 = norm_rows(rows.astype(F32), gain1).astype(BF16)
    mixer_in = normed1.reshape(micro, tokens, width)
    ahead = [(i, i + 1) for i in range(tensor - 1)]
    behind = [(i + 1, i) for i in range(tensor - 1)]
    halo = lax.ppermute(mixer_in[:, tokens - HALO :], "tensor", ahead)
    mixer_own = pack_mixer(every, *pack)
    piece, piece2 = (a[0] for a in pack_ffn(mine, *pack_f))

    *others, halo, mixer_own, piece, piece2, every = sync(
        *others, halo, mixer_own, piece, piece2, every
    )
    mixer_others = jnp.stack(others)
    b, c = swap(mixer_others, first, dp), swap(mixer_others, second, dp)
    ffn_all = [lax.all_gather(p, "tensor") for p in (piece, piece2)]
    ffn_own = pack_ffn(every, *pack_f)
    mixer_others, b, c, *ffn_own = sync(mixer_others, b, c, *ffn_own)
    d = swap(b, second, dp)
    mixer_pieces = [mixer_others, b, c] + [swap(x, across, dp) for x in (mixer_others, b, c)]
    ffn_all[0], d, *mixer_pieces = sync(ffn_all[0], d, *mixer_pieces)
    mixer_pieces = mixer_pieces[:3] + [d] + mixer_pieces[3:] + [swap(d, across, dp)]

    def others_of(array):
        return jnp.stack(
            [lax.dynamic_index_in_dim(array, (place + k) % tensor, 0, False) for k in range(1, tensor)]
        )

    gates = Gather(others_of(ffn_all[0]), dp)


    x_ext = jnp.concatenate([halo, mixer_in], axis=1)

    seg = jnp.pad(segment[:, 0].astype(F32), ((0, 0), (HALO, 0)), constant_values=-1)
    seg = lax.dynamic_slice_in_dim(seg, place * tokens, HALO + tokens, 1)
    seg_row = jnp.broadcast_to(seg[:, None, HALO:], (micro, 8, tokens))
    seg = seg[..., None]

    part = local_heads * HD
    (mixer_w, beta, taps, beta_w, proj, qk, inv, scores, base, mix, keep, gain, state) = mixer_local(
        ids, mixer_in, halo, seg, seg_row, mixer_own, mixer_pieces, heads
    )
    tie = Pending().tie_all
    state, ffn_all[1], gates.pieces = tie(state, ffn_all[1], gates.pieces)
    recv = lax.ppermute(state, "tensor", ahead)
    gates.round()
    downs = Gather(others_of(ffn_all[1]), dp)
    recv = lax.ppermute(hop(recv, keep, gain, tensor, False), "tensor", ahead)
    recv, gates.pieces = tie(recv, gates.pieces)
    recv = lax.ppermute(hop(recv, keep, gain, tensor, False), "tensor", ahead)
    gates.round()
    downs.round()
    state, gates.pieces, downs.pieces = tie(recv, gates.pieces, downs.pieces)
    downs.round()
    mixed, update = mixer_output(qk, scores, base, mix, state, seg, tensor)
    mixed = mixed.reshape(count, heads * HD)

    out_grad = d_out.reshape(count, width)
    table = jnp.stack([ids[i] for i in (4, 6, 5, 7, 0, 2, 1, 3)])
    output, d_mid, d_mid_low, d_mixed, gain2_part, *grads = ffn(
        ids, table, mixed, rows, out_grad, gain2, ffn_own, gates.pieces + downs.pieces, hidden
    )
    order = reduce_order(tensor)
    pending = Pending()
    red = Reduction(pending, "f", grads, order, dp, tensor)

    d_mixed = d_mixed.reshape(micro, tokens, heads * HD)
    y0, back_gain, d_state = mixer_back_local(d_mixed, qk, inv, scores, beta, seg, tensor)
    recv = lax.ppermute(d_state, "tensor", behind)
    pending.tie(d_state)
    red.across(0)
    recv = lax.ppermute(hop(pending.tie(recv), keep, back_gain, tensor, True), "tensor", behind)
    red.across(1)
    xt, lt = flipped(table, *pending.tie(x_ext.reshape(-1, width), d_mid_low))
    pending.kept["xt"] = xt
    recv = lax.ppermute(hop(pending.tie(recv), keep, back_gain, tensor, True), "tensor", behind)
    red.first(0)
    d_qkv, d_beta, d_taps = mixer_back(
        d_mixed, y0, qk, inv, update, state, pending.tie(recv), proj, taps, beta, seg, seg_row, tensor
    )
    d_beta = pending.tie(d_beta)
    grads = grad_mixer(
        pending.kept.pop("xt"), d_qkv.reshape(-1, heads * 3 * HD), lt, mixed, tensor
    )
    mix = Reduction(pending, "m", grads, order, dp, tensor)
    red.second(0)
    red.first(1)
    mix.across(0)
    mix.across(1)
    d_qkv, d_beta, d_taps, gain2_part = pending.tie(d_qkv, d_beta, d_taps, gain2_part)
    d_b = d_beta.astype(BF16)
    front, d_normed1 = input_back(d_qkv, mixer_w, d_b, beta_w)
    front = lax.ppermute(front, "tensor", behind)
    d_normed1 = pending.tie(d_normed1)
    red.second(1)
    red.along()
    mix.first(0)
    mix.first(1)
    total = pending.tie(reduce_far(red.result(), dp))
    gather = Gather(total, dp)
    mix.second(0)
    mix.second(1)
    mix.along()
    d_normed1, front = pending.tie(d_normed1, front)
    input_grad, gain1_part = input_norm(d_normed1, front, rows, d_mid, gain1)
    gain1_part = pending.tie(gain1_part)

    span = width // tensor
    grad_b = project_t(d_b.reshape(count, HD), normed1)[::LANES].reshape(tensor, -1)
    d_taps = d_taps[:, :12].reshape(tensor, local_heads, 12, HD)
    d_taps = jnp.swapaxes(d_taps, 1, 2).reshape(tensor, -1)
    gains = jnp.concatenate([g[0].reshape(tensor, span) for g in (gain1_part, gain2_part)], axis=1)
    gains = lax.dynamic_slice_in_dim(jnp.concatenate([gains, gains]), place, tensor, 0)
    small = jnp.concatenate([grad_b, d_taps, gains], axis=1)
    small_in = swap(small, across, dp)

    gather.pieces, small_in, small = pending.tie_all(gather.pieces, small_in, small)
    gather.round()
    small = small + small_in
    total = reduce_far(mix.result(), dp)
    mixer_gather = Gather(total, dp)
    small_in = swap(small, lambda i: 2, dp)
    gather.pieces, small_in, small = pending.tie_all(gather.pieces, small_in, small)
    gather.round()
    small = small + small_in
    mixer_gather.pieces, small = pending.tie_all(mixer_gather.pieces, small)
    mixer_gather.round()
    small_in = swap(small, lambda i: 4, dp)
    gather.pieces, small_in, small = pending.tie_all(gather.pieces, small_in, small)
    small = small + small_in
    mask = PIECES
    while mask < dp:
        small = small + swap(small, lambda i: mask, dp)
        mask *= 2
    small_in = [to_ahead(small[k], k, tensor) for k in range(1, tensor)]
    gather.pieces, mixer_gather.pieces = pending.tie_all(gather.pieces, mixer_gather.pieces)
    mixer_gather.round()
    grad_gate, grad_up, grad_down = finish_ffn(ids, gather.ordered(), hidden)
    small = sum(small_in, small[0])
    grad_q, grad_k, grad_v, grad_out = finish_mixer(ids, mixer_gather.ordered(), part)
    cut = local_heads * width
    grad_beta = small[:cut].reshape(local_heads, width).T
    grad_conv = small[cut : cut + 12 * span].reshape(3, 4, span)
    cut += 12 * span
    grad_gain1 = small[cut : cut + span]
    grad_gain2 = small[cut + span :]
    return (
        output.reshape(micro, 1, tokens, width),
        input_grad.reshape(micro, 1, tokens, width),
        grad_gain1,
        grad_q,
        grad_k,
        grad_v,
        grad_beta,
        grad_conv,
        grad_out,
        grad_gain2,
        grad_gate.T,
        grad_up.T,
        grad_down,
    )


def solution(mesh):
    in_specs = (
        P(None, "dp", "tensor", None),
        P(None, "dp", None),
        P(None, "dp", "tensor", None),
        P(),
        P(None, "tensor"),
        P(None, "tensor"),
        P(None, "tensor"),
        P(None, "tensor"),
        P(None, None, "tensor"),
        P("tensor", None),
        P(),
        P(None, "tensor"),
        P(None, "tensor"),
        P("tensor", None),
    )
    out_specs = (
        P(None, "dp", "tensor", None),
        P(None, "dp", "tensor", None),
        P("tensor"),
        P(None, "tensor"),
        P(None, "tensor"),
        P(None, "tensor"),
        P(None, "tensor"),
        P(None, None, "tensor"),
        P("tensor", None),
        P("tensor"),
        P(None, "tensor"),
        P(None, "tensor"),
        P("tensor", None),
    )
    body = functools.partial(shards, mesh.shape["dp"], mesh.shape["tensor"])
    return jax.shard_map(body, mesh=mesh, in_specs=in_specs, out_specs=out_specs, check_vma=False)
```

```python
import functools

import jax
import jax.numpy as jnp
from jax import lax
from jax.experimental import pallas as pl
from jax.experimental.pallas import tpu as pltpu
from jax.sharding import PartitionSpec as P

HD = 128
HALO = 16
EXTRA = 16
LANES = 16
PIECES = 8
EPS = 1e-06
F32 = jnp.float32
BF16 = jnp.bfloat16
MIB = 1 << 20


def mm(a, b, ta=False, tb=False):
    dims = (((0 if ta else 1,), (1 if tb else 0,)), ((), ()))
    return lax.dot_general(a.astype(BF16), b.astype(BF16), dims, preferred_element_type=F32)


def interleave(makers):
    running = list(makers)
    while running:
        still = []
        for g in running:
            try:
                next(g)
                still.append(g)
            except StopIteration:
                pass
        running = still


def invert_unit(lows):
    size = lows[0].shape[0]
    row = lax.broadcasted_iota(jnp.int32, (size, size), 0)
    col = lax.broadcasted_iota(jnp.int32, (size, size), 1)
    eye = (row == col).astype(F32)
    invs = [eye - jnp.where((row >> 1) == (col >> 1), low, 0.0) for low in lows]
    step = 1
    while (2 << step) <= size:
        pair = ((row >> (step + 1)) == (col >> (step + 1))) & ((row >> step) != (col >> step))
        lefts = [mm(inv, jnp.where(pair, low, 0.0)) for inv, low in zip(invs, lows)]
        yield
        invs = [inv - mm(left, inv) for inv, left in zip(invs, lefts)]
        yield
        step += 1
    return invs


def short_conv(proj, taps, keeps):
    total = taps[0:1] * proj[HALO:]
    for i in range(1, 4):
        total = total + taps[i : i + 1] * (pltpu.roll(proj, i, 0)[HALO:] * keeps[i - 1])
    return total


def silu_unit(conv):
    sig = jax.nn.sigmoid(conv)
    act = conv * sig
    scale = lax.rsqrt(jnp.sum(act * act, axis=-1, keepdims=True) + EPS)
    return act * scale, scale, sig


def silu_unit_back(grad, conv, unit, scale, sig):
    d_act = scale * (grad - unit * jnp.sum(grad * unit, axis=-1, keepdims=True))
    return d_act * sig * (1.0 + conv * (1.0 - sig))


def flags(seg):
    own = seg[HALO:]
    equal = lambda a: jnp.where(own == a, 1.0, 0.0)
    keeps = [equal(pltpu.roll(jnp.broadcast_to(seg, (seg.shape[0], HD)), i, 0)[HALO:, 0:1]) for i in (1, 2, 3)]
    return keeps, equal(seg[HALO - 1 : HALO]), equal(seg[-1:])


def masks(seg, seg_row):
    n = seg_row.shape[1]
    row = lax.broadcasted_iota(jnp.int32, (n, n), 0)
    col = lax.broadcasted_iota(jnp.int32, (n, n), 1)
    same = seg[HALO:] == seg_row
    strict = jnp.where(same & (row > col), 1.0, 0.0)
    within = jnp.where(same & (row >= col), 1.0, 0.0)
    return strict, within


def pick(values, head):
    lane = lax.broadcasted_iota(jnp.int32, values.shape, 1)
    return jnp.sum(jnp.where(lane == head, values, 0.0), axis=-1, keepdims=True)


def piece_copies(ids_ref, own_ref, piece_refs, w_ref, sems):
    slots = [[pltpu.make_async_copy(own_ref, w_ref.at[0], sems.at[0, 0])]]
    for slot in range(1, w_ref.shape[0]):
        slots.append(
            [
                pltpu.make_async_copy(
                    piece.at[slot - 1], w_ref.at[slot, ids_ref[j]], sems.at[slot, j]
                )
                for j, piece in enumerate(piece_refs)
            ]
        )
    return slots


def local_kernel(ids_ref, x_ref, halo_ref, seg_ref, seg_row_ref, own_ref, *refs):
    pieces = refs[:PIECES]
    (w_ref, beta_ref, taps_ref, beta_w_ref, proj_ref, qk_ref, t_ref, p_ref, ub_ref, w_out_ref, m_ref,
     a_ref, s_ref, sems) = refs[PIECES:]
    slot = pl.program_id(0)
    per = taps_ref.shape[0]
    micro, tokens, width = x_ref.shape
    half = tokens // 2
    rows = width // PIECES
    copies = piece_copies(ids_ref, own_ref, pieces, w_ref, sems)

    @pl.when(slot == 0)
    def _():
        for group in copies:
            for copy in group:
                copy.start()
        beta_ref[...] = jnp.zeros_like(beta_ref)

    for k, group in enumerate(copies):

        @pl.when(slot == k)
        def _():
            for copy in group:
                copy.wait()

    def extra(piece, j):
        return w_ref[slot, piece, rows:, j * HD : (j + 1) * HD]

    beta_w = jnp.concatenate(
        [jnp.concatenate([extra(p, hh) for p in range(PIECES)], axis=1) for hh in range(per)], axis=0
    )
    beta_w_ref[0] = beta_w
    for hh in range(per):
        lines = [extra(per * (r % 4) + hh, per + r // 4)[0:1].astype(F32) for r in range(12)]
        taps_ref[hh] = jnp.concatenate(lines + [jnp.zeros((4, HD), F32)], axis=0)
    lane = lax.broadcasted_iota(jnp.int32, (tokens, HD), 1)

    weights = w_ref[slot, :, :rows].reshape(width, per * 3 * HD)
    shared = []
    for m in range(micro):
        x_ext = jnp.concatenate([halo_ref[m], x_ref[m]], axis=0)
        proj = jnp.dot(x_ext, weights, preferred_element_type=F32)
        seg = seg_ref[m]
        betas = jax.nn.sigmoid(mm(x_ref[m], beta_w, tb=True))
        shared.append((proj, betas, flags(seg), masks(seg, seg_row_ref[m, 0:1])))

    def instance(hh, m):
        proj, betas, (keeps, live, last), (strict, within) = shared[m]
        proj = proj[:, hh * 3 * HD : (hh + 1) * 3 * HD]
        taps = taps_ref[hh]
        proj_ref[hh, m] = proj
        convs = [
            short_conv(proj[:, j * HD : (j + 1) * HD], taps[4 * j : 4 * j + 4], keeps)
            for j in range(3)
        ]
        query = silu_unit(convs[0])[0]
        key = silu_unit(convs[1])[0]
        value = convs[2] * jax.nn.sigmoid(convs[2])
        beta = betas[:, hh * LANES : hh * LANES + 1]
        beta_ref[m] += jnp.where(lane == (slot * per + hh) * LANES, beta, 0.0)
        qk_ref[hh, m] = jnp.concatenate([query, key], axis=1).astype(BF16)
        yield
        low = beta * mm(key, key, tb=True) * strict
        scores = mm(query, key, tb=True) * within
        p_ref[hh, m] = scores.astype(BF16)
        yield
        top, bottom = yield from invert_unit([low[:half, :half], low[half:, half:]])
        cross = mm(bottom, low[half:, :half])
        yield
        cross = -mm(cross, top)
        yield
        inv = jnp.concatenate(
            [
                jnp.concatenate([top, jnp.zeros_like(top)], axis=1),
                jnp.concatenate([cross, bottom], axis=1),
            ],
            axis=0,
        ).astype(BF16)
        t_ref[hh, m] = inv
        both = mm(inv, jnp.concatenate([beta * value, (beta * live) * key], axis=1))
        yield
        late = (last * key).astype(BF16)
        sums = mm(both, late, ta=True)
        row = lax.broadcasted_iota(jnp.int32, (HD, HD), 0)
        col = lax.broadcasted_iota(jnp.int32, (HD, HD), 1)
        keep_state = jnp.where(row == col, live[tokens - 1 : tokens], 0.0)
        ub_ref[hh, m] = both[:, :HD]
        w_out_ref[hh, m] = both[:, HD:].astype(BF16)
        a_ref[hh, m] = sums[:HD]
        s_ref[hh, m] = sums[:HD].astype(BF16)
        m_ref[hh, m] = (keep_state - sums[HD:]).astype(BF16)

    interleave([instance(hh, m) for hh in range(per) for m in range(micro)])


def hop_kernel(back, state_ref, keep_ref, gain_ref, out_ref):
    for h in range(gain_ref.shape[0]):
        for m in range(gain_ref.shape[1]):
            moved = mm(state_ref[h, m], keep_ref[h, m], tb=back)
            out_ref[h, m] = (moved + gain_ref[h, m]).astype(BF16)


def output_kernel(qk_ref, p_ref, ub_ref, w_ref, state_ref, seg_ref, mixed_ref, u_ref):
    per, micro = ub_ref.shape[:2]

    def instance(hh, m):
        live = flags(seg_ref[m])[1]
        state = state_ref[hh, m]
        update = ub_ref[hh, m] - mm(w_ref[hh, m], state, tb=True)
        update = update.astype(BF16)
        far = live * mm(qk_ref[hh, m][:, :HD], state, tb=True)
        yield
        mixed = far + mm(p_ref[hh, m], update)
        u_ref[hh, m] = update
        yield
        mixed_ref[m, :, hh * HD : (hh + 1) * HD] = mixed.astype(BF16)

    interleave([instance(hh, m) for hh in range(per) for m in range(micro)])


def back_local_kernel(dmix_ref, qk_ref, t_ref, p_ref, beta_ref, seg_ref, y_ref, b_ref, s_ref):
    per, micro = qk_ref.shape[:2]
    slot = pl.program_id(0)

    def instance(hh, m):
        live = flags(seg_ref[m])[1]
        d_out = dmix_ref[m, :, hh * HD : (hh + 1) * HD]
        part = mm(p_ref[hh, m], d_out, ta=True)
        yield
        y0 = mm(t_ref[hh, m], part, ta=True)
        yield
        y_ref[hh, m] = y0
        qk = qk_ref[hh, m]
        beta = pick(beta_ref[m], (slot * per + hh) * LANES)
        gain = mm(live * d_out, qk[:, :HD], ta=True) - mm((beta * live) * y0, qk[:, HD:], ta=True)
        b_ref[hh, m] = gain
        s_ref[hh, m] = gain.astype(BF16)

    interleave([instance(hh, m) for hh in range(per) for m in range(micro)])


def back_kernel(dmix_ref, y_ref, qk_ref, t_ref, u_ref, state_ref, dstate_ref, proj_ref,
                taps_ref, beta_ref, seg_ref, seg_row_ref,
                dmain_ref, dbeta_ref, dtaps_ref):
    per, micro = qk_ref.shape[:2]
    tokens = qk_ref.shape[2]
    slot = pl.program_id(0)
    shared = [(flags(seg_ref[m]), masks(seg_ref[m], seg_row_ref[m, 0:1])) for m in range(micro)]
    lane = lax.broadcasted_iota(jnp.int32, (tokens, HD), 1)
    tap_totals = {}

    @pl.when(slot == 0)
    def _():
        dbeta_ref[...] = jnp.zeros_like(dbeta_ref)

    def instance(hh, m):
        (keeps, live, last), (strict, within) = shared[m]
        taps = taps_ref[hh]
        head = (slot * per + hh) * LANES
        proj = proj_ref[hh, m]
        beta = pick(beta_ref[m], head)
        q_low, k_low = qk_ref[hh, m][:, :HD], qk_ref[hh, m][:, HD:]
        state = state_ref[hh, m]
        dstate = dstate_ref[hh, m]
        update = u_ref[hh, m]
        d_out = dmix_ref[m, :, hh * HD : (hh + 1) * HD].astype(BF16)
        ahead = last * mm(k_low, dstate, tb=True)
        yield
        d_right = y_ref[hh, m] + mm(t_ref[hh, m], ahead, ta=True)
        d_right_low = d_right.astype(BF16)
        yield
        d_scores = (mm(d_out, update, tb=True) * within).astype(BF16)
        yield
        grad_sys = -mm(d_right_low, update, tb=True) * strict
        keys_keys = mm(k_low, k_low, tb=True)
        d_kk = (beta * grad_sys).astype(BF16)
        d_beta = jnp.sum(grad_sys * keys_keys, axis=-1, keepdims=True)
        yield
        carried = mm(k_low, state, tb=True)
        d_carried = ((-beta * live) * d_right).astype(BF16)
        d_query = live * mm(d_out, state) + mm(d_scores, k_low)
        yield
        d_key = (
            mm(d_scores, q_low, ta=True)
            + last * mm(update, dstate)
            + mm(d_carried, state)
            + mm(d_kk, k_low)
            + mm(d_kk, k_low, ta=True)
        )
        yield
        convs = [
            short_conv(proj[:, j * HD : (j + 1) * HD], taps[4 * j : 4 * j + 4], keeps)
            for j in range(3)
        ]
        query, q_scale, q_sig = silu_unit(convs[0])
        key, k_scale, k_sig = silu_unit(convs[1])
        v_sig = jax.nn.sigmoid(convs[2])
        value = convs[2] * v_sig
        d_beta = d_beta + jnp.sum(d_right * (value - live * carried), axis=-1, keepdims=True)
        dbeta_ref[m] += jnp.where(lane == head, d_beta * beta * (1.0 - beta), 0.0)
        d_value = beta * d_right
        d_convs = [
            silu_unit_back(d_query, convs[0], query, q_scale, q_sig),
            silu_unit_back(d_key, convs[1], key, k_scale, k_sig),
            d_value * v_sig * (1.0 + convs[2] * (1.0 - v_sig)),
        ]
        yield
        tap_sums = []
        for j in range(3):
            part = proj[:, j * HD : (j + 1) * HD]
            d_conv = d_convs[j]
            tap_sums.append(jnp.sum(d_conv * part[HALO:], axis=0, keepdims=True))
            zeros = jnp.zeros((HALO, HD), F32)
            d_proj = jnp.concatenate([zeros, taps[4 * j : 4 * j + 1] * d_conv], axis=0)
            for i in range(1, 4):
                kept = keeps[i - 1] * d_conv
                tap_sums.append(
                    jnp.sum(kept * pltpu.roll(part, i, 0)[HALO:], axis=0, keepdims=True)
                )
                spread = jnp.concatenate([zeros, taps[4 * j + i : 4 * j + i + 1] * kept], axis=0)
                d_proj = d_proj + pltpu.roll(spread, HALO + tokens - i, 0)
            at = (3 * hh + j) * HD
            dmain_ref[m, :, at : at + HD] = d_proj.astype(BF16)
            yield
        tap_totals[hh, m] = jnp.concatenate(tap_sums + [jnp.zeros((4, HD), F32)], axis=0)

    interleave([instance(hh, m) for hh in range(per) for m in range(micro)])
    for hh in range(per):
        dtaps_ref[hh] = sum(tap_totals[hh, m] for m in range(micro))


def flip(v):
    return v.astype(F32).T.astype(BF16)


def pack_mixer_kernel(table_ref, q_ref, k_ref, v_ref, beta_ref, conv_ref, out_ref):
    piece = table_ref[pl.program_id(0)]
    rows, n = q_ref.shape
    per = n // HD
    parts = []
    for hh in range(per):
        parts += [r[:, hh * HD : (hh + 1) * HD] for r in (q_ref, k_ref, v_ref)]
    out_ref[0, :rows] = jnp.concatenate(parts, axis=1)
    conv = conv_ref[...].astype(F32)
    lines = [beta_ref[hh : hh + 1].astype(F32) for hh in range(per)]
    for j in range(conv.shape[0]):
        line = jnp.zeros((1, HD), F32)
        for p in range(PIECES):
            own = conv[j, p // per : p // per + 1, p % per * HD : (p % per + 1) * HD]
            line = line + jnp.where(piece == p, own, 0.0)
        lines.append(line)
    lines.append(jnp.zeros((1, 3 * n - HD * len(lines)), F32))
    line = jnp.concatenate(lines, axis=1)
    row = lax.broadcasted_iota(jnp.int32, (EXTRA, 3 * n), 0)
    out_ref[0, rows:] = jnp.where(row == 0, line, 0.0).astype(BF16)


def pack_ffn_kernel(table_ref, gate_ref, up_ref, down_ref, out_w_ref, gu_ref, do_ref):
    hidden, rows = gate_ref.shape
    main = hidden // HD * HD
    gu_ref[0, :, :main] = flip(gate_ref[:main])
    gu_ref[0, :, main : 2 * main] = flip(up_ref[:main])
    gu_ref[0, :, 2 * main :] = flip(jnp.concatenate([gate_ref[main:], up_ref[main:]], axis=0))
    wide = main + HD
    down = jnp.concatenate([down_ref[...].astype(F32), jnp.zeros((wide - hidden, rows), F32)], axis=0)
    do_ref[0, :, :wide] = down.T.astype(BF16)
    do_ref[0, :, wide:] = flip(out_w_ref[...])


def flip_pieces(table_ref, src_ref, dst_ref):
    rows = src_ref.shape[1] // PIECES
    for pos in range(PIECES):
        start = pl.multiple_of(table_ref[pos] * rows, rows)
        dst_ref[pos * rows : (pos + 1) * rows] = flip(src_ref[:, pl.ds(start, rows)])


def ordered(pieces):
    own, b, c, far, d, both, far_d = pieces
    return [own, b, c, d, far, both.at[0], both.at[1], far_d]


def ffn_kernel(hidden, ids_ref, table_ref, mixed_ref, rows_ref, dout_ref, gain_ref, *refs):
    owns, groups, refs = refs[:2], [ordered(refs[2:9]), ordered(refs[9:16])], refs[16:]
    out_ref, dmid_ref, dlow_ref, dmixed_ref, gpart_ref = refs[:5]
    (w_ref, wo_ref, x_ref, xt_ref, dt_ref, mid_ref, res_ref, dn_ref, grad_ref, sems, o_sems,
     g_sems) = refs[-12:]
    grad_refs = refs[5:-12]
    step = pl.program_id(0)
    slots = wo_ref.shape[0]
    width = rows_ref.shape[1]
    rows = width // PIECES
    main = hidden // HD * HD
    wide = main + HD
    cut = 2 * hidden + wide
    part = mixed_ref.shape[1]
    ring = w_ref.shape[0]
    order = reduce_order(slots)

    def brought(slot, group, at, target, start, size, sem):
        to = lambda ref: ref.at[:, pl.ds(start, size)]
        if slot == 0:
            return [pltpu.make_async_copy(owns[group].at[:, :, pl.ds(at, size)], target.at[:, :, pl.ds(start, size)], sem.at[0])]
        return [
            pltpu.make_async_copy(piece.at[slot - 1, :, pl.ds(at, size)], to(target.at[ids_ref[j]]), sem.at[j])
            for j, piece in enumerate(groups[group])
        ]

    outs = [brought(k, 1, wide, wo_ref.at[k], 0, part, o_sems.at[k]) for k in range(slots)]
    mains = [
        brought(k, 0, 0, w_ref.at[i % ring], 0, 2 * hidden, sems.at[0, i % ring])
        + brought(k, 1, 0, w_ref.at[i % ring], 2 * hidden, wide, sems.at[1, i % ring])
        for i, k in enumerate(order)
    ]

    def leaving(i):
        return [
            pltpu.make_async_copy(
                grad_ref.at[i % 2, h], grad_refs[i // 2 * 2 + h].at[:, i % 2], g_sems.at[i % 2, h]
            )
            for h in range(2)
        ]

    @pl.when(step == 0)
    def _():
        for group in outs + mains[:ring]:
            for copy in group:
                copy.start()
        mid_ref[...] = rows_ref[...].astype(F32)
        dn_ref[...] = jnp.zeros_like(dn_ref)
        flip_pieces(table_ref, dout_ref, dt_ref)

    for i in range(slots):

        @pl.when(step == i)
        def _():
            for copy in outs[i]:
                copy.wait()

        @pl.when(step == slots + i)
        def _():
            for copy in mains[i]:
                copy.wait()
            if i >= 2:
                for copy in leaving(i - 2):
                    copy.wait()

    @pl.when(step < slots)
    def _():
        mid_ref[...] += mm(mixed_ref[...], wo_ref[step].reshape(width, part), tb=True)

    def norm():
        mid = mid_ref[...]
        rstd = lax.rsqrt(jnp.mean(mid * mid, axis=-1, keepdims=True) + EPS)
        return mid * rstd, rstd

    @pl.when(step == slots - 1)
    def _():
        unit, _ = norm()
        x_ref[...] = (unit * gain_ref[...]).astype(BF16)
        flip_pieces(table_ref, x_ref, xt_ref)
        res_ref[...] = mid_ref[...]

    @pl.when(step >= slots)
    def _():
        at = lax.rem(step - slots, ring)
        w_gu = w_ref[at, :, :, : 2 * hidden].reshape(width, 2 * hidden)
        w_dn = w_ref[at, :, :, 2 * hidden :].reshape(width, wide)
        both = mm(x_ref[...], w_gu)
        rest = both[:, 2 * main :]
        gate = jnp.concatenate([both[:, :main], rest], axis=1)
        up = jnp.concatenate([both[:, main : 2 * main], pltpu.roll(rest, HD // 2, 1)], axis=1)
        sig = jax.nn.sigmoid(gate)
        act = gate * sig
        hid = (act * up).astype(BF16)
        d_hid = mm(dout_ref[...], w_dn)
        d_gate = (d_hid * up * (sig * (1.0 + gate * (1.0 - sig)))).astype(BF16)
        d_up = (d_hid * act).astype(BF16)
        last = d_gate[:, main:].astype(F32) + pltpu.roll(d_up[:, main:].astype(F32), HD // 2, 1)
        d_gu = jnp.concatenate([d_gate[:, :main], d_up[:, :main], last.astype(BF16)], axis=1)
        res_ref[...] += mm(hid, w_dn, tb=True)
        dn_ref[...] += mm(d_gu, w_gu, tb=True)
        to = lax.rem(step - slots, 2)
        shape = (PIECES // 2, rows)
        for h in range(2):
            span = slice(h * width // 2, (h + 1) * width // 2)
            grad_ref[to, h, :, :, : 2 * hidden] = (
                mm(xt_ref[span], d_gu).astype(BF16).reshape(shape + (2 * hidden,))
            )
            grad_ref[to, h, :, :, 2 * hidden :] = (
                mm(dt_ref[span], hid).astype(BF16).reshape(shape + (wide,))
            )

    for i in range(slots):

        @pl.when(step == slots + i)
        def _():
            for copy in leaving(i):
                copy.start()
            if i + ring < slots:
                for copy in mains[i + ring]:
                    copy.start()

    @pl.when(step == 2 * slots - 1)
    def _():
        out_ref[...] = res_ref[...].astype(BF16)
        unit, rstd = norm()
        grad = dn_ref[...]
        gpart_ref[...] = jnp.broadcast_to(jnp.sum(grad * unit, axis=0, keepdims=True), gpart_ref.shape)
        scaled = grad * gain_ref[...]
        d_mid = dout_ref[...].astype(F32) + rstd * (
            scaled - unit * jnp.mean(scaled * unit, axis=-1, keepdims=True)
        )
        dmid_ref[...] = d_mid
        low = d_mid.astype(BF16)
        dlow_ref[...] = low
        for k in range(slots):
            dmixed_ref[:, k * part : (k + 1) * part] = mm(low, wo_ref[k].reshape(width, part))
        for i in range(max(slots - 2, 0), slots):
            for copy in leaving(i):
                copy.wait()


def grad_mixer_kernel(xt_ref, dqkv_ref, lt_ref, mixed_ref, *refs):
    grad_ref, g_sems = refs[-2:]
    grad_refs = refs[:-2]
    step = pl.program_id(0)
    width = xt_ref.shape[0]
    rows = width // PIECES
    n = dqkv_ref.shape[1]
    slots = pl.num_programs(0)

    def leaving(i):
        return [
            pltpu.make_async_copy(
                grad_ref.at[i % 2, h], grad_refs[i // 2 * 2 + h].at[:, i % 2], g_sems.at[i % 2, h]
            )
            for h in range(2)
        ]

    for i in range(2, slots):

        @pl.when(step == i)
        def _():
            for copy in leaving(i - 2):
                copy.wait()

    to = lax.rem(step, 2)
    for h in range(2):
        span = slice(h * width // 2, (h + 1) * width // 2)
        shape = (PIECES // 2, rows)
        grad_ref[to, h, :, :, :n] = mm(xt_ref[span], dqkv_ref[...]).astype(BF16).reshape(shape + (n,))
        out = mm(lt_ref[span], mixed_ref[...]).astype(BF16)
        grad_ref[to, h, :, :, n:] = out.reshape(shape + (out.shape[1],))

    for i in range(slots):

        @pl.when(step == i)
        def _():
            for copy in leaving(i):
                copy.start()
            if i == slots - 1:
                for j in range(max(slots - 2, 0), slots):
                    for copy in leaving(j):
                        copy.wait()


def bring(ids_ref, pieces, w_ref, sems):
    @pl.when(pl.program_id(0) == 0)
    def _():
        copies = [
            pltpu.make_async_copy(piece, w_ref.at[ids_ref[j]], sems.at[j])
            for j, piece in enumerate(pieces)
        ]
        for copy in copies:
            copy.start()
        for copy in copies:
            copy.wait()


def finish_ffn_kernel(hidden, ids_ref, *refs):
    gate_ref, up_ref, down_ref, w_ref, sems = refs[PIECES:]
    bring(ids_ref, refs[:PIECES], w_ref, sems)
    step = pl.program_id(0)
    main = hidden // HD * HD
    wide = main + HD
    take = lambda at, n: w_ref[step, :, at : at + n].astype(F32).T
    gate_ref[:main] = take(0, main)
    up_ref[:main] = take(main, main)
    rest = take(2 * main, HD)
    gate_ref[main:] = rest[: HD // 2]
    up_ref[main:] = rest[HD // 2 :]
    down_ref[...] = take(2 * hidden, wide)[:hidden]


def finish_mixer_kernel(ids_ref, *refs):
    outs, out_w_ref, w_ref, sems = refs[PIECES:-3], refs[-3], refs[-2], refs[-1]
    bring(ids_ref, refs[:PIECES], w_ref, sems)
    step = pl.program_id(0)
    n = outs[0].shape[1]
    for hh in range(n // HD):
        for j, out in enumerate(outs):
            at = (3 * hh + j) * HD
            out[:, hh * HD : (hh + 1) * HD] = w_ref[step, :, at : at + HD].astype(F32)
    out_w_ref[...] = w_ref[step, :, 3 * n :].astype(F32).T


def input_kernel(dqkv_ref, w_ref, db_ref, beta_w_ref, front_ref, out_ref):
    step = pl.program_id(0)
    width, n = out_ref.shape[2], dqkv_ref.shape[2]
    weights = w_ref[0, :, : width // PIECES].reshape(width, n)
    for m in range(out_ref.shape[0]):
        grad = mm(dqkv_ref[m], weights, tb=True)
        more = mm(db_ref[m], beta_w_ref[0])

        @pl.when(step == 0)
        def _():
            front_ref[m] = grad[:HALO]
            out_ref[m] = grad[HALO:] + more

        @pl.when(step > 0)
        def _():
            front_ref[m] += grad[:HALO]
            out_ref[m] += grad[HALO:] + more


def norm_kernel(grad_ref, front_ref, rows_ref, dmid_ref, gain_ref, out_ref, gpart_ref):
    tokens = grad_ref.shape[1]
    cut = tokens - HALO
    total = jnp.zeros((1, grad_ref.shape[2]), F32)
    for m in range(grad_ref.shape[0]):
        grad = jnp.concatenate([grad_ref[m, :cut], grad_ref[m, cut:] + front_ref[m]], axis=0)
        rows = rows_ref[m * tokens : (m + 1) * tokens].astype(F32)
        rstd = lax.rsqrt(jnp.mean(rows * rows, axis=-1, keepdims=True) + EPS)
        unit = rows * rstd
        total = total + jnp.sum(grad * unit, axis=0, keepdims=True)
        scaled = grad * gain_ref[...]
        out_ref[m * tokens : (m + 1) * tokens] = (
            dmid_ref[m * tokens : (m + 1) * tokens]
            + rstd * (scaled - unit * jnp.mean(scaled * unit, axis=-1, keepdims=True))
        ).astype(BF16)
    gpart_ref[...] = jnp.broadcast_to(total, gpart_ref.shape)


def params(mib=60):
    return pltpu.CompilerParams(
        dimension_semantics=("arbitrary",), vmem_limit_bytes=mib * MIB
    )


def cost(flops, nbytes):
    return pl.CostEstimate(flops=int(flops), bytes_accessed=int(nbytes), transcendentals=0)


ANYWHERE = pl.BlockSpec(memory_space=pl.ANY)


def whole(shape):
    return pl.BlockSpec(tuple(shape), lambda *_: (0,) * len(shape), pipeline_mode=pl.Buffered(1))


def reduce_order(slots):
    return list(range(slots - 2, 0, -1)) + [slots - 1, 0]


def lead(n, shape):
    return pl.BlockSpec((n,) + tuple(shape[1:]), lambda h, *_: (h,) + (0,) * (len(shape) - 1))


def rolled(n, shape, shift, steps):
    return pl.BlockSpec(
        (n,) + tuple(shape[1:]), lambda h, *_: ((h + shift) % steps,) + (0,) * (len(shape) - 1)
    )


def sds(shape, dtype):
    return jax.ShapeDtypeStruct(tuple(shape), dtype)


def call(kernel, grid, in_specs, out_specs, out_shape, estimate, name, scratch=(), prefetch=0, mib=60):
    return pl.pallas_call(
        kernel,
        grid_spec=pltpu.PrefetchScalarGridSpec(
            num_scalar_prefetch=prefetch,
            grid=(grid,),
            in_specs=in_specs,
            out_specs=out_specs,
            scratch_shapes=list(scratch),
        ),
        out_shape=out_shape,
        compiler_params=params(mib),
        cost_estimate=cost(*estimate),
        name=name,
    )


def pack_mixer(table, w_query, w_key, w_value, beta_t, conv):
    width, n = w_query.shape
    rows = width // PIECES
    spec = pl.BlockSpec((rows, n), lambda i, t: (t[i], 0))
    count = table.shape[0]
    return call(
        pack_mixer_kernel, count,
        [spec] * 3 + [pl.BlockSpec((beta_t.shape[0], rows), lambda i, t: (0, t[i])), whole(conv.shape)],
        pl.BlockSpec((1, rows + EXTRA, 3 * n), lambda i, t: (i, 0, 0)),
        sds((count, rows + EXTRA, 3 * n), BF16), (0, 12 * count * rows * n), "pack_mixer", prefetch=1,
    )(table, w_query, w_key, w_value, beta_t, conv)


def pack_ffn(table, gate_t, up_t, w_down, w_out):
    hidden, width = gate_t.shape
    rows = width // PIECES
    n = hidden // HD * HD + HD + w_out.shape[0]
    count = table.shape[0]
    return call(
        pack_ffn_kernel, count,
        [pl.BlockSpec((w.shape[0], rows), lambda i, t: (0, t[i])) for w in (gate_t, up_t, w_down, w_out)],
        [pl.BlockSpec((1, rows, m), lambda i, t: (i, 0, 0)) for m in (2 * hidden, n)],
        [sds((count, rows, m), BF16) for m in (2 * hidden, n)], (0, 0), "pack_ffn", prefetch=1,
    )(table, gate_t, up_t, w_down, w_out)


def mixer_local(ids, x, halo, seg, seg_row, own, pieces, heads):
    micro, tokens, width = x.shape
    slots = pieces[0].shape[0] + 1
    per = heads // slots
    hm = (heads, micro)
    rows, n = own.shape[1:]
    outs = [
        sds((slots, PIECES, rows, n), BF16),
        sds((micro, tokens, HD), F32),
        sds((heads, 16, HD), F32),
        sds((slots, per * LANES, width), BF16),
        sds(hm + (HALO + tokens, 3 * HD), F32),
        sds(hm + (tokens, 2 * HD), BF16),
        sds(hm + (tokens, tokens), BF16),
        sds(hm + (tokens, tokens), BF16),
        sds(hm + (tokens, HD), F32),
        sds(hm + (tokens, HD), BF16),
        sds(hm + (HD, HD), BF16),
        sds(hm + (HD, HD), F32),
        sds(hm + (HD, HD), BF16),
    ]
    return call(
        local_kernel, slots,
        [whole(x.shape), whole(halo.shape), whole(seg.shape), whole(seg_row.shape)]
        + [ANYWHERE] * (1 + PIECES),
        [whole(o.shape) for o in outs[:2]] + [lead(per, outs[2].shape), lead(1, outs[3].shape)]
        + [lead(per, o.shape) for o in outs[4:]],
        outs, (heads * micro * 1e9, heads * micro * 2e6), "mixer_local",
        [pltpu.SemaphoreType.DMA((slots, PIECES))], prefetch=1,
    )(ids, x, halo, seg, seg_row, own, *pieces)


def hop(state, keep, gain, slots, back):
    per = gain.shape[0] // slots
    shift = slots - 1 if back else 1
    return call(
        functools.partial(hop_kernel, back), slots,
        [rolled(per, state.shape, shift, slots), lead(per, keep.shape), lead(per, gain.shape)],
        lead(per, gain.shape), sds(gain.shape, BF16),
        (gain.size * 512, gain.size * 12), "hop", mib=12,
    )(state, keep, gain)


def mixer_output(qk, scores, base, mix, state, seg, slots):
    heads, micro, tokens = qk.shape[:3]
    per = heads // slots
    return call(
        output_kernel, slots,
        [lead(per, a.shape) for a in (qk, scores, base, mix)]
        + [rolled(per, state.shape, 1, slots), whole(seg.shape)],
        [pl.BlockSpec((micro, tokens, per * HD), lambda h: (0, 0, h)), lead(per, base.shape)],
        [sds((micro, tokens, heads * HD), BF16), sds(base.shape, BF16)],
        (heads * micro * 5e7, heads * micro * 5e5), "mixer_output",
    )(qk, scores, base, mix, state, seg)


def mixer_back_local(d_mixed, qk, inv, scores, beta, seg, slots):
    heads, micro, tokens = qk.shape[:3]
    per = heads // slots
    outs = [sds((heads, micro, tokens, HD), F32), sds((heads, micro, HD, HD), F32)]
    outs.append(sds((heads, micro, HD, HD), BF16))
    return call(
        back_local_kernel, slots,
        [pl.BlockSpec((micro, tokens, per * HD), lambda h: (0, 0, h))]
        + [lead(per, a.shape) for a in (qk, inv, scores)]
        + [whole(beta.shape), whole(seg.shape)],
        [lead(per, o.shape) for o in outs], outs,
        (heads * micro * 5e7, heads * micro * 5e5), "mixer_back_local",
    )(d_mixed, qk, inv, scores, beta, seg)


def mixer_back(d_mixed, y0, qk, inv, update, state, d_state, proj, taps, beta, seg, seg_row, slots):
    heads, micro, tokens = qk.shape[:3]
    per = heads // slots
    columns = lambda rows, n: pl.BlockSpec((micro, rows, per * n), lambda h: (0, 0, h))
    return call(
        back_kernel, slots,
        [columns(tokens, HD)]
        + [lead(per, a.shape) for a in (y0, qk, inv, update)]
        + [rolled(per, state.shape, 1, slots), rolled(per, d_state.shape, slots - 1, slots)]
        + [lead(per, proj.shape), lead(per, taps.shape)]
        + [whole(a.shape) for a in (beta, seg, seg_row)],
        [columns(HALO + tokens, 3 * HD), whole(beta.shape), lead(per, taps.shape)],
        [
            sds((micro, HALO + tokens, heads * 3 * HD), BF16),
            sds(beta.shape, F32),
            sds(taps.shape, F32),
        ],
        (heads * micro * 5e8, heads * micro * 2e6), "mixer_back",
    )(d_mixed, y0, qk, inv, update, state, d_state, proj, taps, beta, seg, seg_row)


def grads_out(slots, rows, n):
    shape = (PIECES // 2, rows, n)
    return (
        [sds((PIECES // 2, 2, rows, n), BF16)] * slots,
        [pltpu.VMEM((2, 2) + shape, BF16)],
        pltpu.SemaphoreType.DMA((2, 2)),
    )


def ffn(ids, table, mixed, rows, d_out, gain, own, pieces, hidden):
    count, width = rows.shape
    slots = pieces[0].shape[0] + 1
    assert len(pieces) == 14
    wide = hidden // HD * HD + HD
    part = mixed.shape[1] // slots
    piece = width // PIECES
    full = whole((count, width))
    grads, room, g_sems = grads_out(slots, piece, 2 * hidden + wide)
    outs = [
        sds((count, width), BF16), sds((count, width), F32), sds((count, width), BF16),
        sds((count, mixed.shape[1]), F32), sds((8, width), F32),
    ]
    ring = 2
    return call(
        functools.partial(ffn_kernel, hidden), 2 * slots,
        [pl.BlockSpec((count, part), lambda s, *_: (0, jnp.minimum(s, slots - 1))),
         full, full, whole(gain.shape)] + [ANYWHERE] * 16,
        [full, full, full, whole((count, mixed.shape[1])), whole((8, width))] + [ANYWHERE] * len(grads),
        outs + grads, (26 * count * width * hidden * slots, 6e7), "ffn",
        [
            pltpu.VMEM((ring, PIECES, piece, 2 * hidden + wide), BF16),
            pltpu.VMEM((slots, PIECES, piece, part), BF16),
            pltpu.VMEM((count, width), BF16),
            pltpu.VMEM((width, count), BF16),
            pltpu.VMEM((width, count), BF16),
            pltpu.VMEM((count, width), F32),
            pltpu.VMEM((count, width), F32),
            pltpu.VMEM((count, width), F32),
        ]
        + room
        + [
            pltpu.SemaphoreType.DMA((2, ring, PIECES)),
            pltpu.SemaphoreType.DMA((slots, PIECES)),
            g_sems,
        ],
        prefetch=2,
    )(ids, table, mixed, rows, d_out, gain, *own, *pieces)


def grad_mixer(xt, d_qkv, lt, mixed, slots):
    width = xt.shape[0]
    n, part = d_qkv.shape[1] // slots, mixed.shape[1] // slots
    grads, room, g_sems = grads_out(slots, width // PIECES, n + part)
    order = reduce_order(slots)

    def at(s):
        return sum(jnp.where(s == i, k, 0) for i, k in enumerate(order))

    columns = lambda a, size: pl.BlockSpec((a.shape[0], size), lambda s: (0, at(s)))
    return call(
        grad_mixer_kernel, slots,
        [whole(xt.shape), columns(d_qkv, n), whole(lt.shape), columns(mixed, part)],
        [ANYWHERE] * len(grads), grads,
        (2 * width * mixed.shape[0] * (n + part) * slots, 2 * width * (n + part) * slots), "grad_mixer",
        room + [g_sems],
    )(xt, d_qkv, lt, mixed)


def finish_ffn(ids, pieces, hidden):
    rows, n = pieces[0].shape
    width = rows * PIECES
    return call(
        functools.partial(finish_ffn_kernel, hidden), PIECES, [ANYWHERE] * PIECES,
        [pl.BlockSpec((hidden, rows), lambda i, t: (0, i))] * 3,
        [sds((hidden, width), F32)] * 3,
        (0, 6 * n * width), "finish_ffn",
        [pltpu.VMEM((PIECES, rows, n), BF16), pltpu.SemaphoreType.DMA((PIECES,))], prefetch=1,
    )(ids, *pieces)


def flip_kernel(table_ref, x_ref, y_ref, xt_ref, yt_ref):
    flip_pieces(table_ref, x_ref, xt_ref)
    flip_pieces(table_ref, y_ref, yt_ref)


def flipped(table, x, y):
    outs = [sds(a.shape[::-1], BF16) for a in (x, y)]
    return call(
        flip_kernel, 1, [whole(x.shape), whole(y.shape)], [whole(o.shape) for o in outs], outs,
        (0, 8 * x.size), "flip", prefetch=1,
    )(table, x, y)


def finish_mixer(ids, pieces, n):
    rows, total = pieces[0].shape
    width = rows * PIECES
    part = total - 3 * n
    return call(
        finish_mixer_kernel, PIECES, [ANYWHERE] * PIECES,
        [pl.BlockSpec((rows, n), lambda i, t: (i, 0))] * 3 + [pl.BlockSpec((part, rows), lambda i, t: (0, i))],
        [sds((width, n), F32)] * 3 + [sds((part, width), F32)],
        (0, 6 * total * width), "finish_mixer",
        [pltpu.VMEM((PIECES, rows, total), BF16), pltpu.SemaphoreType.DMA((PIECES,))], prefetch=1,
    )(ids, *pieces)


def input_back(d_qkv, w, d_b, beta_w):
    micro, ext, _ = d_qkv.shape
    slots, _, _, n = w.shape
    width = beta_w.shape[2]
    outs = [sds((micro, HALO, width), F32), sds((micro, ext - HALO, width), F32)]
    lanes = beta_w.shape[1]
    return call(
        input_kernel, slots,
        [pl.BlockSpec((micro, ext, n), lambda s: (0, 0, s)), lead(1, w.shape),
         whole(d_b.shape[:2] + (HD,)), lead(1, (slots, HD, width))],
        [whole(o.shape) for o in outs], outs,
        (2 * micro * ext * width * n * slots, 2 * slots * width * n), "input_back",
    )(d_qkv, w, d_b, jnp.stack([jnp.pad(beta_w[k], ((k * lanes, HD - (k + 1) * lanes), (0, 0))) for k in range(slots)]))


def input_norm(grad, front, rows, d_mid, gain):
    outs = [sds(rows.shape, BF16), sds((8, rows.shape[1]), F32)]
    return call(
        norm_kernel, 1, [whole(a.shape) for a in (grad, front, rows, d_mid, gain)],
        [whole(o.shape) for o in outs], outs, (0, 12 * rows.size), "input_norm",
    )(grad, front, rows, d_mid, gain)


def swap(x, mask_of, size):
    return lax.ppermute(x, "dp", [(i, i ^ mask_of(i)) for i in range(size)])


def first(i):
    return 4 if i & 1 else 2


def second(i):
    return 2 if i & 1 else 4


def across(i):
    return 1


def from_ahead(x, k, size):
    return lax.ppermute(x, "tensor", [(i, (i - k) % size) for i in range(size)])


def to_ahead(x, k, size):
    return lax.ppermute(x, "tensor", [(i, (i + k) % size) for i in range(size)])


def plane_gather(own, dp):
    b = swap(own, first, dp)
    c = swap(own, second, dp)
    d = swap(b, second, dp)
    near = [own, b, c, d]
    return near + [swap(piece, across, dp) for piece in near]


def piece_ids(own):
    core = own & 1
    f = jnp.where(core == 1, 4, 2)
    s = jnp.where(core == 1, 2, 4)
    return jnp.stack([own, own ^ f, own ^ s, own ^ 6, own ^ 1, own ^ 1 ^ s, own ^ 1 ^ f, own ^ 7])


def sync(*xs):
    return lax.optimization_barrier(xs)


def add(a, b):
    return (a.astype(F32) + b.astype(F32)).astype(BF16)


class Pending:
    def __init__(self):
        self.kept = {}

    def tie(self, *xs):
        keys = list(self.kept)
        values = sync(*xs, *(self.kept[k] for k in keys))
        self.kept = dict(zip(keys, values[len(xs) :]))
        return values[0] if len(xs) == 1 else values[: len(xs)]

    def tie_all(self, *trees):
        leaves, shape = jax.tree.flatten(trees)
        return jax.tree.unflatten(shape, self.tie(*leaves))


class Gather:
    def __init__(self, own, dp):
        self.dp, self.step = dp, 0
        self.pieces = [own, swap(own, first, dp), swap(own, second, dp), swap(own, across, dp)]

    def round(self):
        if self.step == 0:
            own, b, c, far = self.pieces
            both = swap(jnp.stack([b, c]), across, self.dp)
            self.pieces = [own, b, c, far, swap(b, second, self.dp), both]
        else:
            self.pieces.append(swap(self.pieces[4], across, self.dp))
        self.step += 1

    def ordered(self):
        own, b, c, far, d, both, far_d = self.pieces
        return [own, b, c, d, far, both[0], both[1], far_d]


class Reduction:
    def __init__(self, pending, name, grads, order, dp, tensor):
        self.pending, self.name = pending, name
        self.order, self.dp, self.tensor = order, dp, tensor
        self.came, self.parts = {}, {}
        for i in range(len(order) // 2):
            self.came["one", i] = swap(grads[2 * i], across, dp)
            pending.kept[name, "one", i] = grads[2 * i + 1]

    def add(self, step, i):
        came = self.pending.tie(self.came.pop((step, i)))
        return add(self.pending.kept.pop((self.name, step, i)), came)

    def across(self, i):
        total = self.add("one", i)
        self.pending.kept[self.name, "two", i] = total[:2]
        self.came["two", i] = swap(total[2:], first, self.dp)

    def first(self, i):
        total = self.add("two", i)
        self.pending.kept[self.name, "three", i] = total[0]
        self.came["three", i] = swap(total[1], second, self.dp)

    def second(self, i):
        total = self.add("three", i)
        for slot, part in zip(self.order[2 * i : 2 * i + 2], (total[0], total[1])):
            self.pending.kept[self.name, "part", slot] = part
        if i == 0:
            slot = self.order[0]
            self.parts[slot] = to_ahead(self.pending.kept.pop((self.name, "part", slot)), 1, self.tensor)

    def along(self):
        slot = self.order[-2]
        self.parts[slot] = to_ahead(self.pending.kept.pop((self.name, "part", slot)), slot, self.tensor)
        for slot in self.order[1:-2]:
            part = add(
                self.pending.kept.pop((self.name, "part", slot)),
                self.pending.tie(self.parts.pop(slot + 1)),
            )
            self.parts[slot] = to_ahead(part, 1, self.tensor)

    def result(self):
        parts = [self.pending.kept.pop((self.name, "part", 0))]
        parts += [self.parts[k] for k in sorted({1, self.tensor - 1})]
        return sum(p.astype(F32) for p in parts).astype(BF16)


def reduce_far(total, dp):
    mask = PIECES
    while mask < dp:
        total = add(total, swap(total, lambda i: mask, dp))
        mask *= 2
    return total


def norm_rows(rows, gain):
    rstd = lax.rsqrt(jnp.mean(rows * rows, axis=-1, keepdims=True) + EPS)
    return rows * rstd * gain


def project_t(left, right):
    return jnp.einsum("th,td->hd", left, right, preferred_element_type=F32)


def shards(dp, tensor, layer_input, segment, d_out, norm1_gain, w_query, w_key, w_value, w_beta,
           conv_weight, w_out, norm2_gain, w_gate, w_up, w_down):
    micro, _, tokens, width = layer_input.shape
    count = micro * tokens
    local_heads = w_query.shape[1] // HD
    heads = local_heads * tensor
    hidden = w_gate.shape[1]
    own = lax.axis_index("dp") % PIECES
    place = lax.axis_index("tensor")
    ids = piece_ids(own)
    gain1 = norm1_gain.astype(F32)[None]
    gain2 = norm2_gain.astype(F32)[None]
    mine = own[None].astype(jnp.int32)
    every = jnp.arange(PIECES, dtype=jnp.int32)

    pack = (w_query, w_key, w_value, w_beta.T, conv_weight)
    pack_f = (w_gate.T, w_up.T, w_down, w_out)
    piece = pack_mixer(mine, *pack)[0]
    others = [from_ahead(piece, k, tensor) for k in range(1, tensor)]
    rows = layer_input.reshape(count, width)
    _, rows, mine, every = sync(piece, rows, mine, every)
    normed1 = norm_rows(rows.astype(F32), gain1).astype(BF16)
    mixer_in = normed1.reshape(micro, tokens, width)
    ahead = [(i, i + 1) for i in range(tensor - 1)]
    behind = [(i + 1, i) for i in range(tensor - 1)]
    halo = lax.ppermute(mixer_in[:, tokens - HALO :], "tensor", ahead)
    mixer_own = pack_mixer(every, *pack)
    piece, piece2 = (a[0] for a in pack_ffn(mine, *pack_f))

    *others, halo, mixer_own, piece, piece2, every = sync(
        *others, halo, mixer_own, piece, piece2, every
    )
    mixer_others = jnp.stack(others)
    b, c = swap(mixer_others, first, dp), swap(mixer_others, second, dp)
    ffn_all = [lax.all_gather(p, "tensor") for p in (piece, piece2)]
    ffn_own = pack_ffn(every, *pack_f)
    mixer_others, b, c, *ffn_own = sync(mixer_others, b, c, *ffn_own)
    d = swap(b, second, dp)
    mixer_pieces = [mixer_others, b, c] + [swap(x, across, dp) for x in (mixer_others, b, c)]
    ffn_all[0], d, *mixer_pieces = sync(ffn_all[0], d, *mixer_pieces)
    mixer_pieces = mixer_pieces[:3] + [d] + mixer_pieces[3:] + [swap(d, across, dp)]

    def others_of(array):
        return jnp.stack(
            [lax.dynamic_index_in_dim(array, (place + k) % tensor, 0, False) for k in range(1, tensor)]
        )

    gates = Gather(others_of(ffn_all[0]), dp)


    x_ext = jnp.concatenate([halo, mixer_in], axis=1)

    seg = jnp.pad(segment[:, 0].astype(F32), ((0, 0), (HALO, 0)), constant_values=-1)
    seg = lax.dynamic_slice_in_dim(seg, place * tokens, HALO + tokens, 1)
    seg_row = jnp.broadcast_to(seg[:, None, HALO:], (micro, 8, tokens))
    seg = seg[..., None]

    part = local_heads * HD
    (mixer_w, beta, taps, beta_w, proj, qk, inv, scores, base, mix, keep, gain, state) = mixer_local(
        ids, mixer_in, halo, seg, seg_row, mixer_own, mixer_pieces, heads
    )
    tie = Pending().tie_all
    state, ffn_all[1], gates.pieces = tie(state, ffn_all[1], gates.pieces)
    recv = lax.ppermute(state, "tensor", ahead)
    gates.round()
    downs = Gather(others_of(ffn_all[1]), dp)
    recv = lax.ppermute(hop(recv, keep, gain, tensor, False), "tensor", ahead)
    recv, gates.pieces = tie(recv, gates.pieces)
    recv = lax.ppermute(hop(recv, keep, gain, tensor, False), "tensor", ahead)
    gates.round()
    downs.round()
    state, gates.pieces, downs.pieces = tie(recv, gates.pieces, downs.pieces)
    downs.round()
    mixed, update = mixer_output(qk, scores, base, mix, state, seg, tensor)
    mixed = mixed.reshape(count, heads * HD)

    out_grad = d_out.reshape(count, width)
    table = jnp.stack([ids[i] for i in (4, 6, 5, 7, 0, 2, 1, 3)])
    output, d_mid, d_mid_low, d_mixed, gain2_part, *grads = ffn(
        ids, table, mixed, rows, out_grad, gain2, ffn_own, gates.pieces + downs.pieces, hidden
    )
    order = reduce_order(tensor)
    pending = Pending()
    red = Reduction(pending, "f", grads, order, dp, tensor)

    d_mixed = d_mixed.reshape(micro, tokens, heads * HD)
    y0, back_gain, d_state = mixer_back_local(d_mixed, qk, inv, scores, beta, seg, tensor)
    recv = lax.ppermute(d_state, "tensor", behind)
    pending.tie(d_state)
    red.across(0)
    recv = lax.ppermute(hop(pending.tie(recv), keep, back_gain, tensor, True), "tensor", behind)
    red.across(1)
    xt, lt = flipped(table, *pending.tie(x_ext.reshape(-1, width), d_mid_low))
    pending.kept["xt"] = xt
    recv = lax.ppermute(hop(pending.tie(recv), keep, back_gain, tensor, True), "tensor", behind)
    red.first(0)
    d_qkv, d_beta, d_taps = mixer_back(
        d_mixed, y0, qk, inv, update, state, pending.tie(recv), proj, taps, beta, seg, seg_row, tensor
    )
    d_beta = pending.tie(d_beta)
    grads = grad_mixer(
        pending.kept.pop("xt"), d_qkv.reshape(-1, heads * 3 * HD), lt, mixed, tensor
    )
    mix = Reduction(pending, "m", grads, order, dp, tensor)
    red.second(0)
    red.first(1)
    mix.across(0)
    mix.across(1)
    d_qkv, d_beta, d_taps, gain2_part = pending.tie(d_qkv, d_beta, d_taps, gain2_part)
    d_b = d_beta.astype(BF16)
    front, d_normed1 = input_back(d_qkv, mixer_w, d_b, beta_w)
    front = lax.ppermute(front, "tensor", behind)
    d_normed1 = pending.tie(d_normed1)
    mix.first(0)
    red.second(1)
    red.along()
    mix.first(1)
    total = pending.tie(reduce_far(red.result(), dp))
    gather = Gather(total, dp)
    mix.second(0)
    mix.second(1)
    mix.along()
    d_normed1, front = pending.tie(d_normed1, front)
    input_grad, gain1_part = input_norm(d_normed1, front, rows, d_mid, gain1)
    gain1_part = pending.tie(gain1_part)

    span = width // tensor
    grad_b = project_t(d_b.reshape(count, HD), normed1)[::LANES].reshape(tensor, -1)
    d_taps = d_taps[:, :12].reshape(tensor, local_heads, 12, HD)
    d_taps = jnp.swapaxes(d_taps, 1, 2).reshape(tensor, -1)
    gains = jnp.concatenate([g[0].reshape(tensor, span) for g in (gain1_part, gain2_part)], axis=1)
    gains = lax.dynamic_slice_in_dim(jnp.concatenate([gains, gains]), place, tensor, 0)
    small = jnp.concatenate([grad_b, d_taps, gains], axis=1)
    small_in = swap(small, across, dp)

    gather.pieces, small_in, small = pending.tie_all(gather.pieces, small_in, small)
    gather.round()
    small = small + small_in
    total = reduce_far(mix.result(), dp)
    mixer_gather = Gather(total, dp)
    small_in = swap(small, lambda i: 2, dp)
    gather.pieces, small_in, small = pending.tie_all(gather.pieces, small_in, small)
    gather.round()
    small = small + small_in
    mixer_gather.pieces, small = pending.tie_all(mixer_gather.pieces, small)
    mixer_gather.round()
    small_in = swap(small, lambda i: 4, dp)
    gather.pieces, small_in, small = pending.tie_all(gather.pieces, small_in, small)
    small = small + small_in
    mask = PIECES
    while mask < dp:
        small = small + swap(small, lambda i: mask, dp)
        mask *= 2
    small_in = [to_ahead(small[k], k, tensor) for k in range(1, tensor)]
    grad_gate, grad_up, grad_down = finish_ffn(ids, gather.ordered(), hidden)
    grad_gate, mixer_gather.pieces = pending.tie_all(grad_gate, mixer_gather.pieces)
    mixer_gather.round()
    small = sum(small_in, small[0])
    grad_q, grad_k, grad_v, grad_out = finish_mixer(ids, mixer_gather.ordered(), part)
    cut = local_heads * width
    grad_beta = small[:cut].reshape(local_heads, width).T
    grad_conv = small[cut : cut + 12 * span].reshape(3, 4, span)
    cut += 12 * span
    grad_gain1 = small[cut : cut + span]
    grad_gain2 = small[cut + span :]
    return (
        output.reshape(micro, 1, tokens, width),
        input_grad.reshape(micro, 1, tokens, width),
        grad_gain1,
        grad_q,
        grad_k,
        grad_v,
        grad_beta,
        grad_conv,
        grad_out,
        grad_gain2,
        grad_gate.T,
        grad_up.T,
        grad_down,
    )


def solution(mesh):
    in_specs = (
        P(None, "dp", "tensor", None),
        P(None, "dp", None),
        P(None, "dp", "tensor", None),
        P(),
        P(None, "tensor"),
        P(None, "tensor"),
        P(None, "tensor"),
        P(None, "tensor"),
        P(None, None, "tensor"),
        P("tensor", None),
        P(),
        P(None, "tensor"),
        P(None, "tensor"),
        P("tensor", None),
    )
    out_specs = (
        P(None, "dp", "tensor", None),
        P(None, "dp", "tensor", None),
        P("tensor"),
        P(None, "tensor"),
        P(None, "tensor"),
        P(None, "tensor"),
        P(None, "tensor"),
        P(None, None, "tensor"),
        P("tensor", None),
        P("tensor"),
        P(None, "tensor"),
        P(None, "tensor"),
        P("tensor", None),
    )
    body = functools.partial(shards, mesh.shape["dp"], mesh.shape["tensor"])
    return jax.shard_map(body, mesh=mesh, in_specs=in_specs, out_specs=out_specs, check_vma=False)
```
